32 devices in a mesh: img: 4 (over x, core), mlp: 8 (over z, y).
Axes of the slice: x: 2, y: 2, z: 4, core: 2. Of those that a mesh axis runs over, the one named last changes fastest.
Arguments:
- tokens: bfloat16 [64, 14, 14, 384], P(('img', 'mlp')), may hold values from -6 to 6
- ln1_gain: bfloat16 [384], replicated, may hold values from 0.5 to 1.5
- ln1_bias: bfloat16 [384], replicated, may hold values from -1.75 to 1.75
- f_weight: bfloat16 [384, 772], replicated, may hold values from -0.3125 to 0.3125
- f_bias: bfloat16 [772], replicated, may hold values from -1.75 to 1.75
- dw_small: bfloat16 [9, 384], replicated, may hold values from -2 to 2
- dw_middle: bfloat16 [25, 384], replicated, may hold values from -1.25 to 1.25
- dw_large: bfloat16 [49, 384], replicated, may hold values from -0.875 to 0.875
- h_weight: bfloat16 [384, 384], replicated, may hold values from -0.3125 to 0.3125
- h_bias: bfloat16 [384], replicated, may hold values from -1.75 to 1.75
- proj_weight: bfloat16 [384, 384], replicated, may hold values from -0.3125 to 0.3125
- proj_bias: bfloat16 [384], replicated, may hold values from -1.75 to 1.75
- ln2_gain: bfloat16 [384], replicated, may hold values from 0.5 to 1.5
- ln2_bias: bfloat16 [384], replicated, may hold values from -1.75 to 1.75
- fc1_weight: bfloat16 [384, 1536], P(None, 'mlp'), may hold values from -0.3125 to 0.3125
- fc1_bias: bfloat16 [1536], P('mlp'), may hold values from -1.75 to 1.75
- fc2_weight: bfloat16 [1536, 384], P('mlp'), may hold values from -0.15625 to 0.15625
- fc2_bias: bfloat16 [384], replicated, may hold values from -1.75 to 1.75
- out_grad: bfloat16 [64, 14, 14, 384], P(('img', 'mlp')), may hold values from -6 to 6
Outputs:
- block_out: float32 [64, 14, 14, 384], P(('img', 'mlp'))
- tokens_grad: float32 [64, 14, 14, 384], P(('img', 'mlp'))
- ln1_gain_grad: float32 [384], replicated
- ln1_bias_grad: float32 [384], replicated
- f_weight_grad: float32 [384, 772], replicated
- f_bias_grad: float32 [772], replicated
- dw_small_grad: float32 [9, 384], replicated
- dw_middle_grad: float32 [25, 384], replicated
- dw_large_grad: float32 [49, 384], replicated
- h_weight_grad: float32 [384, 384], replicated
- h_bias_grad: float32 [384], replicated
- proj_weight_grad: float32 [384, 384], replicated
- proj_bias_grad: float32 [384], replicated
- ln2_gain_grad: float32 [384], replicated
- ln2_bias_grad: float32 [384], replicated
- fc1_weight_grad: float32 [384, 1536], P(None, 'mlp')
- fc1_bias_grad: float32 [1536], P('mlp')
- fc2_weight_grad: float32 [1536, 384], P('mlp')
- fc2_bias_grad: float32 [384], replicated
The draws below stay inside these ranges and needn't reach their ends.
All inputs are finite; a program needn't handle non-finite values.
Results may differ from the reference program's by a relative error of at most 0.017.
Values may be sent and summed in bfloat16 or wider, within the bound.
No kernel may reach another device: no remote copies, remote signals or barrier semaphores. Data moves between devices by JAX's collectives and lax.ppermute only.
A program may use at most 128 MiB of HBM per device.

```python
import math
import jax
import jax.numpy as jnp
from jax import lax

D = 384
FF = 1536
SIDE = 14
IMAGES = 64


def block_levels(stream_key, shape, pieces, least, largest):
    level, own = 1.0, jax.random.fold_in(stream_key, 6)
    for position, parts in pieces:
        steps = jnp.exp(jax.random.uniform(jax.random.fold_in(own, position), (parts,), jnp.float32, least / len(pieces), largest / len(pieces)))
        level = level * jnp.repeat(steps, shape[position] // parts).reshape([-1 if axis == position else 1 for axis in range(len(shape))])
    return level


def normal_values(key, shape, spread, reach, pieces=(), kind=jnp.bfloat16):
    values = jax.random.normal(key, shape, jnp.float32) * spread
    if len(pieces) > 0:
        values = block_levels(key, shape, pieces, -0.22, 0.18) * values
    return jnp.clip(values, min=-reach, max=reach).astype(kind)


def setup_inputs(seed: int = 0) -> dict:
    streams_of = jax.random.split(jax.random.key(seed), 20)
    return {
        "tokens": normal_values(streams_of[0], (IMAGES, SIDE, SIDE, D), 1.0, 6.0, ((0, 32),)),
        "ln1_gain": jnp.clip(1.0 + 0.1 * jax.random.normal(streams_of[1], (D,), jnp.float32), 0.5, 1.5).astype(jnp.bfloat16),
        "ln1_bias": normal_values(streams_of[2], (D,), 0.3, 1.75),
        "f_weight": normal_values(streams_of[3], (D, 2 * D + 4), D ** -0.5, 0.3125),
        "f_bias": normal_values(streams_of[4], (2 * D + 4,), 0.3, 1.75),
        "dw_small": normal_values(streams_of[5], (9, D), 9 ** -0.5, 2.0),
        "dw_middle": normal_values(streams_of[6], (25, D), 25 ** -0.5, 1.25),
        "dw_large": normal_values(streams_of[7], (49, D), 49 ** -0.5, 0.875),
        "h_weight": normal_values(streams_of[8], (D, D), D ** -0.5, 0.3125),
        "h_bias": normal_values(streams_of[9], (D,), 0.3, 1.75),
        "proj_weight": normal_values(streams_of[10], (D, D), D ** -0.5, 0.3125),
        "proj_bias": normal_values(streams_of[11], (D,), 0.3, 1.75),
        "ln2_gain": jnp.clip(1.0 + 0.1 * jax.random.normal(streams_of[12], (D,), jnp.float32), 0.5, 1.5).astype(jnp.bfloat16),
        "ln2_bias": normal_values(streams_of[13], (D,), 0.3, 1.75),
        "fc1_weight": normal_values(streams_of[14], (D, FF), D ** -0.5, 0.3125, ((1, 8),)),
        "fc1_bias": normal_values(streams_of[15], (FF,), 0.3, 1.75, ((0, 8),)),
        "fc2_weight": normal_values(streams_of[16], (FF, D), FF ** -0.5, 0.15625, ((0, 8),)),
        "fc2_bias": normal_values(streams_of[17], (D,), 0.3, 1.75),
        "out_grad": normal_values(streams_of[18], (IMAGES, SIDE, SIDE, D), 1.0, 6.0, ((0, 32),)),
    }


highest = lax.Precision.HIGHEST
epsilon = 1e-05

@jax.custom_vjp
def low(v):
    return lax.optimization_barrier(v.astype(jnp.bfloat16)).astype(jnp.float32)

@jax.custom_vjp
def low_back(v):
    return v

def low_keep(v):
    return (low(v), None)

def low_pass(kept, grad):
    return (grad,)

def back_keep(v):
    return (v, None)

def back_low(kept, grad):
    return (low(grad),)
low.defvjp(low_keep, low_pass)
low_back.defvjp(back_keep, back_low)

def layer_norm(values, ln_gain, ln_bias):
    average = lax.optimization_barrier(jnp.mean(values, axis=-1, keepdims=True))
    centred = values - average
    variance = lax.optimization_barrier(jnp.mean(centred * centred, axis=-1, keepdims=True))
    return centred * lax.rsqrt(variance + epsilon) * ln_gain + ln_bias

def exact_gelu(values):
    return jax.nn.gelu(values, approximate=False)

def depthwise(values, kernel):
    extent = math.isqrt(kernel.shape[0])
    filters = kernel.reshape(extent, extent, 1, kernel.shape[1])
    return lax.conv_general_dilated(values, filters, (1, 1), 'SAME', dimension_numbers=('NHWC', 'HWIO', 'NHWC'), feature_group_count=values.shape[-1], precision=highest)

def dense(values, weight):
    return jnp.einsum('bijc,cd->bijd', values, weight, precision=highest)

def mixer_block(inputs, ln1_gain, ln1_bias, f_weight, f_bias, dw_small, dw_middle, dw_large, h_weight, h_bias, proj_weight, proj_bias, ln2_gain, ln2_bias, fc1_weight, fc1_bias, fc2_weight, fc2_bias):
    width = inputs.shape[-1]
    normed = low(layer_norm(inputs, ln1_gain, ln1_bias))
    focal = low_back(dense(normed, f_weight) + f_bias)
    query = focal[..., :width]
    context = focal[..., width:2 * width]
    gates = focal[..., 2 * width:]
    level_one = exact_gelu(depthwise(context, dw_small))
    level_two = exact_gelu(depthwise(level_one, dw_middle))
    level_three = exact_gelu(depthwise(level_two, dw_large))
    global_ctx = exact_gelu(lax.optimization_barrier(jnp.mean(level_three, axis=(1, 2), keepdims=True)))
    aggregated = level_one * gates[..., 0:1] + level_two * gates[..., 1:2] + level_three * gates[..., 2:3] + global_ctx * gates[..., 3:4]
    modulator = low_back(dense(low(aggregated), h_weight) + h_bias)
    mixed = low(query * modulator)
    branch = low_back(dense(mixed, proj_weight) + proj_bias)
    middle = inputs + branch
    normed_two = low(layer_norm(middle, ln2_gain, ln2_bias))
    before = low_back(dense(normed_two, fc1_weight) + fc1_bias)
    hidden = low(exact_gelu(before))
    mlp_out = low_back(dense(hidden, fc2_weight) + fc2_bias)
    return middle + mlp_out

def reference(tokens, ln1_gain, ln1_bias, f_weight, f_bias, dw_small, dw_middle, dw_large, h_weight, h_bias, proj_weight, proj_bias, ln2_gain, ln2_bias, fc1_weight, fc1_bias, fc2_weight, fc2_bias, out_grad):
    weights = tuple((item.astype(jnp.float32) for item in (ln1_gain, ln1_bias, f_weight, f_bias, dw_small, dw_middle, dw_large, h_weight, h_bias, proj_weight, proj_bias, ln2_gain, ln2_bias, fc1_weight, fc1_bias, fc2_weight, fc2_bias)))
    group_size = math.gcd(IMAGES, 16)
    group_count = IMAGES // group_size
    grouped_inputs = tokens.astype(jnp.float32).reshape(group_count, group_size, SIDE, SIDE, D)
    grouped_cots = out_grad.astype(jnp.float32).reshape(group_count, group_size, SIDE, SIDE, D)

    def one_group(totals, inputs_pair):
        group_in, group_cot = inputs_pair
        outputs, pullback = jax.vjp(mixer_block, group_in, *weights)
        gradients = pullback(group_cot)
        summed = tuple((total + grad_item for total, grad_item in zip(totals, gradients[1:])))
        return (summed, (outputs, gradients[0]))
    zero_totals = tuple((jnp.zeros_like(item) for item in weights))
    totals, (outputs, input_grads) = lax.scan(one_group, zero_totals, (grouped_inputs, grouped_cots))
    block_out = outputs.reshape(IMAGES, SIDE, SIDE, D)
    tokens_grad = input_grads.reshape(IMAGES, SIDE, SIDE, D)
    return (block_out, tokens_grad, totals[0], totals[1], totals[2], totals[3], totals[4], totals[5], totals[6], totals[7], totals[8], totals[9], totals[10], totals[11], totals[12], totals[13], totals[14], totals[15], totals[16])
```

```python
import functools
import math

import jax
import jax.numpy as jnp
from jax import lax
from jax.experimental import pallas as pl
from jax.experimental.pallas import tpu as pltpu
from jax.experimental.layout import Layout, with_layout_constraint
from jax.sharding import Mesh
from jax.sharding import PartitionSpec as P

epsilon = 1e-05
lanes = 128
sublanes = 8
edge = 3
extents = (3, 5, 7)
starts = (0, 9, 34)
taps = 83
LN1_GAIN, LN1_BIAS, QUERY_BIAS, CONTEXT_BIAS, GATE_BIAS = 83, 84, 85, 86, 87
H_BIAS, PROJ_BIAS, LN2_GAIN, LN2_BIAS, FC2_BIAS = 88, 89, 90, 91, 92
f32 = jnp.float32
bf16 = jnp.bfloat16


def flip(values, axis="core", size=2, bit=1):
    return lax.ppermute(values, axis, [(place, place ^ bit) for place in range(size)])


def exchange(values, axes):
    return lax.all_to_all(values, axes, split_axis=0, concat_axis=0, tiled=True)


def after(values, *others):
    return lax.optimization_barrier((values,) + others)[0]


def nn(left, right):
    return jnp.dot(left, right, preferred_element_type=f32)


def nt(left, right):
    return lax.dot_general(left, right, (((1,), (1,)), ((), ())), preferred_element_type=f32)


def tn(left, right):
    return lax.dot_general(left, right, (((0,), (0,)), ((), ())), preferred_element_type=f32)


def gelu_pair(values):
    below = 0.5 * (1.0 + lax.erf(values * math.sqrt(0.5)))
    density = jnp.exp(values * values * -0.5) * (1.0 / math.sqrt(2.0 * math.pi))
    return values * below, below + values * density


class Shape:
    def __init__(self, images, side, width):
        self.images, self.side, self.width = images, side, width
        self.tiles = width // lanes
        self.slots = images * self.tiles
        self.patches = side * side
        self.segment = -(-self.patches // 8) * 8
        self.rows = images * self.segment
        self.line = side * sublanes
        self.centre = edge * self.line
        self.grid = (side + 2 * edge) * self.line
        self.inner = side * self.line
        self.packed = self.patches * self.slots
        self.block = next(size for size in (80, 40, 16, 8) if self.rows % size == 0)

    def places(self):
        return [
            (image, tile, tile * self.images + image)
            for image in range(self.images)
            for tile in range(self.tiles)
        ]


def columns(tile):
    return slice(tile * lanes, (tile + 1) * lanes)


def unpack(shape, packed, rows):
    for image, tile, slot in shape.places():
        first = image * shape.segment
        rows[first : first + shape.patches, columns(tile)] = packed[
            pl.ds(slot, shape.patches, stride=shape.slots), :
        ]
    for image in range(shape.images):
        first = image * shape.segment
        spare = shape.segment - shape.patches
        if spare:
            rows[first + shape.patches : first + shape.segment, 0 : shape.width] = jnp.zeros(
                (spare, shape.width), f32
            )


def pack(shape, rows, packed):
    for image, tile, slot in shape.places():
        first = image * shape.segment
        packed[pl.ds(slot, shape.patches, stride=shape.slots), :] = rows[
            first : first + shape.patches, columns(tile)
        ]


def blocks(shape, body, init=None):
    def step(index, carry):
        first = pl.multiple_of(index * shape.block, shape.block)
        return body(pl.ds(first, shape.block), carry)

    return lax.fori_loop(0, shape.rows // shape.block, step, init)


def normalise(values):
    average = jnp.mean(values, axis=-1, keepdims=True)
    centred = values - average
    variance = jnp.mean(centred * centred, axis=-1, keepdims=True)
    scale = lax.rsqrt(variance + epsilon)
    return centred * scale, scale


def norm_back(values, grad, gain):
    unit, scale = normalise(values)
    inner = grad * gain
    first = jnp.mean(inner, axis=-1, keepdims=True)
    second = jnp.mean(inner * unit, axis=-1, keepdims=True)
    return scale * (inner - first - unit * second), grad * unit


def fold(values):
    return jnp.sum(values.reshape(values.shape[0] // 8, 8, values.shape[1]), axis=0)


def row_sum(values):
    return jnp.sum(values, axis=0, keepdims=True)


def spread_taps(shape, small, tap_ref):
    tap_ref[...] = jnp.zeros_like(tap_ref)
    for _, tile, slot in shape.places():
        tap_ref[pl.ds(slot, taps, stride=sublanes), :] = small[0:taps, columns(tile)]


def line_at(shape, ref, line):
    first = pl.multiple_of(line * shape.line, shape.line)
    values = ref[pl.ds(first, shape.line), :]
    return [values[w * sublanes : (w + 1) * sublanes] for w in range(shape.side)]


def correlate(shape, source, tap_ref, level, line, turned):
    extent = extents[level]
    reach = extent // 2
    totals = [None] * shape.side
    for down in range(extent):
        values = line_at(shape, source, line + down + edge - reach)
        for along in range(extent):
            entry = down * extent + along
            if turned:
                entry = extent * extent - 1 - entry
            tap = tap_ref[pl.ds((starts[level] + entry) * sublanes, sublanes), :]
            for w in range(shape.side):
                other = w + along - reach
                if 0 <= other < shape.side:
                    term = values[other] * tap
                    totals[w] = term if totals[w] is None else totals[w] + term
    return jnp.concatenate(totals, axis=0)


def tap_grads(shape, source, grad, level, out):
    extent = extents[level]
    reach = extent // 2
    for down in range(extent):

        def step(line, totals, down=down):
            values = line_at(shape, source, line + down + edge - reach)
            grads = line_at(shape, grad, line + edge)
            result = []
            for along in range(extent):
                total = totals[along]
                for w in range(shape.side):
                    other = w + along - reach
                    if 0 <= other < shape.side:
                        total = total + values[other] * grads[w]
                result.append(total)
            return tuple(result)

        zero = jnp.zeros((sublanes, lanes), f32)
        totals = lax.fori_loop(0, shape.side, step, (zero,) * extent)
        for along in range(extent):
            out[pl.ds((starts[level] + down * extent + along) * sublanes, sublanes), :] = totals[
                along
            ]


def clear_edges(shape, ref):
    zeros = jnp.zeros((shape.centre, lanes), f32)
    ref[0 : shape.centre, :] = zeros
    ref[shape.centre + shape.inner : shape.grid, :] = zeros


def gate_values(shape, normed, f_turned, small, gates):
    weight = f_turned[2 * shape.width : 2 * shape.width + 4, :].astype(f32)
    wide = jnp.concatenate(
        [jnp.broadcast_to(weight[g : g + 1], (lanes, shape.width)) for g in range(4)]
    ).astype(bf16)
    bias = small[GATE_BIAS : GATE_BIAS + 1, :]
    wide_bias = jnp.concatenate(
        [jnp.broadcast_to(bias[:, g : g + 1], (1, lanes)) for g in range(4)], axis=1
    )
    gates[...] = nt(normed[...], wide) + wide_bias


def level_rows(shape, level, image, slot):
    return level[pl.ds(shape.centre + slot, shape.segment, stride=sublanes), :]


def run_levels(shape, moves, chain, tap_ref):
    total = jnp.zeros((sublanes, lanes), f32)
    for level, source, target, slope in chain:
        clear_edges(shape, target)

        def line_step(line, total, level=level, source=source, target=target, slope=slope):
            before = correlate(shape, source, tap_ref, level, line, False)
            value, rise = gelu_pair(before)
            here = pl.multiple_of((line + edge) * shape.line, shape.line)
            target[pl.ds(here, shape.line), :] = value
            slope[pl.ds(pl.multiple_of(line * shape.line, shape.line), shape.line), :] = rise
            if level == 2:
                total = total + fold(value)
            return total

        total = lax.fori_loop(0, shape.side, line_step, total)
        moves.leave(target, slope)
    return total


def entry_kernel(
    shape,
    moves,
    tokens,
    f_turned,
    out_grad,
    dw_small,
    dw_middle,
    dw_large,
    ln1_gain,
    ln1_bias,
    f_bias,
    h_bias,
    proj_bias,
    ln2_gain,
    ln2_bias,
    fc2_bias,
    small,
    cot,
    inputs,
    normed,
    query,
    gates,
    context,
    one,
    slope_one,
    tap_ref,
    packed,
    wide,
):
    width = shape.width
    for source, first in zip((dw_small, dw_middle, dw_large), starts):
        small[first : first + source.shape[0], :] = source[...].astype(f32)
    shared = f_bias[...].astype(f32).reshape(1, 2 * width + 4)
    vectors = {
        QUERY_BIAS: shared[:, 0:width],
        CONTEXT_BIAS: shared[:, width : 2 * width],
        GATE_BIAS: jnp.concatenate(
            [shared[:, 2 * width :], jnp.zeros((1, width - 4), f32)], axis=1
        ),
    }
    for row, source in (
        (LN1_GAIN, ln1_gain),
        (LN1_BIAS, ln1_bias),
        (H_BIAS, h_bias),
        (PROJ_BIAS, proj_bias),
        (LN2_GAIN, ln2_gain),
        (LN2_BIAS, ln2_bias),
        (FC2_BIAS, fc2_bias),
    ):
        vectors[row] = source[...].astype(f32).reshape(1, width)
    for row, value in vectors.items():
        small[row : row + 1, :] = value
    last = FC2_BIAS + 1
    small[last:, :] = jnp.zeros((small.shape[0] - last, width), f32)
    moves.leave(small)
    moves.arrive(tokens)
    packed[...] = tokens[...].astype(f32)
    unpack(shape, packed, inputs)
    moves.leave(inputs)
    spread_taps(shape, small, tap_ref)
    gain = small[LN1_GAIN : LN1_GAIN + 1, :]
    bias = small[LN1_BIAS : LN1_BIAS + 1, :]

    def first_norm(rows, carry):
        unit, _ = normalise(inputs[rows, :])
        normed[rows, :] = (unit * gain + bias).astype(bf16)
        return carry

    blocks(shape, first_norm, 0)
    moves.leave(normed)
    moves.arrive(out_grad)
    packed[...] = out_grad[...].astype(f32)
    unpack(shape, packed, wide)
    cot[...] = wide[...].astype(bf16)
    moves.leave(cot)
    moves.arrive(f_turned)
    wide[...] = (
        nt(normed[...], f_turned[width : 2 * width, :]) + small[CONTEXT_BIAS : CONTEXT_BIAS + 1, :]
    )
    context[...] = jnp.zeros_like(context)
    for image, tile, slot in shape.places():
        first = image * shape.segment
        context[pl.ds(shape.centre + slot, shape.patches, stride=sublanes), :] = wide[
            first : first + shape.patches, columns(tile)
        ]
    moves.leave(context)
    query[...] = nt(normed[...], f_turned[0:width, :]) + small[QUERY_BIAS : QUERY_BIAS + 1, :]
    moves.leave(query)
    gate_values(shape, normed, f_turned, small, gates)
    moves.leave(gates)
    run_levels(shape, moves, ((0, context, one, slope_one),), tap_ref)


def modulation_kernel(
    shape,
    moves,
    one,
    small,
    gates,
    h_weight,
    query,
    inputs,
    proj_weight,
    far_one,
    far_gates,
    far_query,
    modulator,
    aggregated,
    mixed,
    middle,
    normed_two,
    two,
    three,
    slope_two,
    slope_three,
    pooled,
    wide,
    tap_ref,
):
    chain = ((1, one, two, slope_two), (2, two, three, slope_three))
    moves.arrive(small)
    spread_taps(shape, small, tap_ref)
    moves.copy(one, far_one)
    moves.copy(gates, far_gates)
    moves.copy(query, far_query)
    total = run_levels(shape, moves, chain, tap_ref)
    value, rise = gelu_pair(total * (1.0 / shape.patches))
    pooled[0:sublanes, :] = value
    pooled[sublanes : 2 * sublanes, :] = rise * (1.0 / shape.patches)
    moves.leave(pooled)
    moves.arrive(h_weight, proj_weight)
    for image, tile, slot in shape.places():
        rows = pl.ds(image * shape.segment, shape.segment)
        wide[rows, columns(tile)] = (
            level_rows(shape, one, image, slot) * gates[rows, columns(0)]
            + level_rows(shape, two, image, slot) * gates[rows, columns(1)]
            + level_rows(shape, three, image, slot) * gates[rows, columns(2)]
            + value[slot : slot + 1] * gates[rows, columns(3)]
        )
    aggregated[...] = wide[...].astype(bf16)
    moves.leave(aggregated)
    modulator[...] = nn(aggregated[...], h_weight[...]) + small[H_BIAS : H_BIAS + 1, :]

    moves.leave(modulator)

    def mix(rows, carry):
        mixed[rows, :] = (query[rows, :] * modulator[rows, :]).astype(bf16)
        return carry

    blocks(shape, mix, 0)
    moves.leave(mixed)
    middle[...] = (
        inputs[...] + nn(mixed[...], proj_weight[...]) + small[PROJ_BIAS : PROJ_BIAS + 1, :]
    )
    moves.leave(middle)
    gain = small[LN2_GAIN : LN2_GAIN + 1, :]
    bias = small[LN2_BIAS : LN2_BIAS + 1, :]

    def second_norm(rows, carry):
        unit, _ = normalise(middle[rows, :])
        normed_two[rows, :] = (unit * gain + bias).astype(bf16)
        return carry

    blocks(shape, second_norm, 0)


class Moves:
    def __init__(self):
        self.incoming, self.outgoing = {}, {}
        self.started, self.free = [], []

    def copy(self, source, target):
        move = pltpu.make_async_copy(source, target, self.free.pop())
        move.start()
        self.started.append(move)

    def arrive(self, *buffers):
        for buffer in buffers:
            move = self.incoming.pop(id(buffer), None)
            if move is not None:
                move.wait()

    def leave(self, *buffers):
        for buffer in buffers:
            move = self.outgoing.pop(id(buffer), None)
            if move is not None:
                move.start()
                self.started.append(move)

    def finish(self):
        for move in list(self.incoming.values()):
            move.wait()
        for move in list(self.outgoing.values()):
            move.start()
            self.started.append(move)
        for move in self.started:
            move.wait()


def with_moves(kernel, far_in, far_out, extra):
    def run(*refs):
        refs = list(refs)
        ins, refs = refs[: len(far_in)], refs[len(far_in) :]
        outs, refs = refs[: len(far_out)], refs[len(far_out) :]
        semaphores = refs.pop()
        count = sum(far_in) + sum(far_out)
        buffers, scratch = refs[len(refs) - count :], refs[: len(refs) - count]
        moves = Moves()
        moves.free = [semaphores.at[count + spare] for spare in range(extra)]
        index = 0
        for group, flags, table in (
            (ins, far_in, moves.incoming),
            (outs, far_out, moves.outgoing),
        ):
            for place, far in enumerate(flags):
                if far:
                    buffer, outer = buffers[index], group[place]
                    pair = (outer, buffer) if group is ins else (buffer, outer)
                    move = pltpu.make_async_copy(*pair, semaphores.at[index])
                    if group is ins:
                        move.start()
                    table[id(buffer)] = move
                    group[place] = buffer
                    index += 1
        kernel(moves, *ins, *outs, *scratch)
        moves.finish()

    return run


class Units:
    def __init__(self, shards, unit):
        self.shards, self.unit = shards, unit
        self.piece_rows = 2 * unit + 16
        self.total = shards * unit
        self.head_rows, self.late_rows = 40, 16
        self.pieces = 2 * shards
        self.share = self.head_rows + self.late_rows
        self.head_total = 2 * self.pieces * self.head_rows
        self.late_total = 2 * self.pieces * self.late_rows


def sum_kernel(parts, source, out):
    size = out.shape[0]
    block = 16 if size % 16 == 0 else size

    def step(index, carry):
        rows = pl.ds(pl.multiple_of(index * block, block), block)
        total = source[0, rows, :].astype(f32)
        for part in range(1, parts):
            total = total + source[part, rows, :].astype(f32)
        out[rows, :] = total.astype(bf16)
        return carry

    lax.fori_loop(0, size // block, step, 0)


def pair_kernel(first, second, out):
    for part in range(out.shape[0]):
        total = first[part].astype(f32) + second[part].astype(f32)
        out[part] = total.astype(bf16)


def rows_kernel(shape, moves, first, second, arrived, first_out, second_out):
    def step(index, carry):
        rows = pl.ds(pl.multiple_of(index * 16, 16), 16)
        more = pl.ds(pl.multiple_of(index * 16 + shape.rows, 16), 16)
        first_out[rows, :] = (first[rows, :].astype(f32) + arrived[rows, :].astype(f32)).astype(bf16)
        second_out[rows, :] = (second[rows, :].astype(f32) + arrived[more, :].astype(f32)).astype(
            bf16
        )
        return carry

    lax.fori_loop(0, shape.rows // 16, step, 0)


def share_kernel(parts, out):
    total = parts[0].astype(f32)
    for part in range(1, parts.shape[0]):
        total = total + parts[part].astype(f32)
    share = total.astype(bf16)
    for copy in range(out.shape[0]):
        out[copy] = share


def piece_kernel(units, copies, spots, first, second, far_bias, out, own, bias, semaphores):
    unit = units.unit
    width = first.shape[1]
    rows = pl.ds(pl.multiple_of(spots[0] * unit, 16), unit)
    moves = [
        pltpu.make_async_copy(source.at[rows, :], own.at[index], semaphores.at[index])
        for index, source in enumerate((first, second))
    ]
    moves.insert(0, pltpu.make_async_copy(far_bias, bias, semaphores.at[2]))
    for move in moves:
        move.start()
    moves.pop(0).wait()
    shard = spots[1]
    values = bias[...].astype(f32).reshape(1, bias.shape[0])
    values = jnp.concatenate([values, jnp.zeros((1, width - bias.shape[0]), f32)], axis=1)
    values = pltpu.roll(jnp.broadcast_to(values, (8, width)), spots[2], 1)
    lane = lax.broadcasted_iota(jnp.int32, (8, width), 1) - shard * unit
    row = lax.broadcasted_iota(jnp.int32, (8, width), 0)
    values = jnp.where((lane >= 0) & (lane < unit) & (row == 0), values, 0.0)
    line = jnp.concatenate([values, jnp.zeros((8, width), f32)]).astype(bf16)
    for move in moves:
        move.wait()
    for copy in range(copies):
        base = copy * units.piece_rows
        out[base : base + unit, :] = own[0]
        out[base + unit : base + 2 * unit, :] = own[1]
        out[base + 2 * unit : base + units.piece_rows, :] = line


def feed_kernel(shape, units, resumed, moves, weights, *refs):
    refs = list(refs)

    def take(count):
        taken = refs[:count]
        del refs[:count]
        return taken

    groups = 1 if resumed is None else 2
    closing = resumed is not False
    normed, cots = take(groups), take(groups)
    if resumed:
        old_grads, old_bias, *near = take(6)
    if resumed:
        out, d_out, both = take(3)
        outs = [out, both.at[shape.rows : 2 * shape.rows, :]]
        d_outs = [d_out, both.at[0 : shape.rows, :]]
        d_near, out_near = take(2)
    else:
        outs, d_outs = take(groups), take(groups)
    grads = take(1)[0]
    if not closing:
        bias_grad = take(1)[0]
    first_weight, second_weight, total_grads, total_bias = take(4)
    unit, width = units.unit, shape.width
    bias = None
    for shard in range(units.shards):
        base, here = shard * units.piece_rows, shard * unit
        first_weight[here : here + unit, :] = weights[base : base + unit, :]
        second_weight[here : here + unit, :] = weights[base + unit : base + 2 * unit, :]
        term = weights[base + 2 * unit : base + units.piece_rows, :].astype(f32)
        bias = term if bias is None else bias + term
    bias = bias[0:1]
    if resumed:
        moves.arrive(*near)
        for target, own, arrived in ((d_near, near[0], near[1]), (out_near, near[2], near[3])):
            target[...] = own[...].astype(f32) + arrived[...].astype(f32)
            moves.leave(target)
    for group in range(groups):
        moves.arrive(normed[group], cots[group])
        rows, cot = normed[group], cots[group]
        value, rise = gelu_pair(nt(rows[...], first_weight[...]) + bias)
        hidden = value.astype(bf16)
        outs[group][...] = nn(hidden, second_weight[...]).astype(bf16)
        d_before = (nt(cot[...], second_weight[...]) * rise).astype(bf16)
        d_outs[group][...] = nn(d_before, first_weight[...]).astype(bf16)
        moves.leave(outs[group], d_outs[group])
        first, second = tn(d_before, rows[...]), tn(hidden, cot[...])
        line = fold(d_before.astype(f32))
        if group == 0 and not resumed:
            total_grads[0 : units.total, :] = first
            total_grads[units.total :, :] = second
            total_bias[...] = line
        elif group == 0:
            total_grads[0 : units.total, :] = old_grads[0 : units.total, :] + first
            total_grads[units.total :, :] = old_grads[units.total :, :] + second
            total_bias[...] = old_bias[...] + line
        else:
            total_grads[0 : units.total, :] += first
            total_grads[units.total :, :] += second
            total_bias[...] += line
    if not closing:
        grads[...] = total_grads[...]
        bias_grad[...] = total_bias[...]
        return
    row = jnp.concatenate([row_sum(total_bias[...]), jnp.zeros((15, width), f32)])
    for shard in range(units.shards):
        base, here = shard * units.piece_rows, shard * unit
        more = units.total + here
        grads[base : base + units.piece_rows, :] = jnp.concatenate(
            [total_grads[here : here + unit, :], total_grads[more : more + unit, :], row]
        ).astype(bf16)


def heads_kernel(
    shape,
    units,
    moves,
    core,
    small,
    cot,
    middle,
    d_near,
    d_far,
    proj_weight,
    query,
    modulator,
    h_weight,
    normed,
    aggregated,
    mixed,
    *refs,
):
    later, refs = refs[:8], refs[8:]
    d_middle, d_query, d_aggregated, own_rest, other_rest, *refs = refs
    fetched, refs = refs[:8], refs[8:]
    heads_body(
        shape,
        units,
        moves,
        core,
        small,
        cot,
        middle,
        d_near,
        d_far,
        proj_weight,
        query,
        modulator,
        h_weight,
        normed,
        aggregated,
        mixed,
        list(zip(later, fetched)),
        d_middle,
        d_query,
        d_aggregated,
        own_rest,
        other_rest,
        *refs,
    )


def heads_body(
    shape,
    units,
    moves,
    core,
    small,
    cot,
    middle,
    d_near,
    d_far,
    proj_weight,
    query,
    modulator,
    h_weight,
    normed,
    aggregated,
    mixed,
    later,
    d_middle,
    d_query,
    d_aggregated,
    own_rest,
    other_rest,
    d_mixed,
    d_modulator,
    head,
    d_branch,
):
    width = shape.width
    zero = jnp.zeros((8, width), f32)
    moves.arrive(small, cot, middle, d_near)
    for source, target in later:
        moves.copy(source, target)
    gain = small[LN2_GAIN : LN2_GAIN + 1, :]

    def second_norm(rows, carry):
        grads = d_near[rows, :] + d_far[rows, :].astype(f32)
        cots = cot[rows, :].astype(f32)
        d_input, d_gain = norm_back(middle[rows, :], grads, gain)
        d_total = cots + d_input
        d_middle[rows, :] = d_total
        rounded = d_total.astype(bf16)
        d_branch[rows, :] = rounded
        added = (d_gain, grads, rounded.astype(f32), cots)
        return tuple(total + fold(item) for total, item in zip(carry, added))

    d_gain, d_bias, proj_bias, out_bias = blocks(shape, second_norm, (zero,) * 4)
    moves.leave(d_middle)
    moves.arrive(proj_weight)
    d_mixed[...] = nt(d_branch[...], proj_weight[...])
    moves.arrive(query, modulator)

    def split(rows, carry):
        values = d_mixed[rows, :]
        for_query = (values * modulator[rows, :]).astype(bf16)
        for_modulator = (values * query[rows, :]).astype(bf16)
        d_query[rows, :] = for_query
        d_modulator[rows, :] = for_modulator
        return carry[0] + fold(for_query.astype(f32)), carry[1] + fold(for_modulator.astype(f32))

    query_bias, h_bias = blocks(shape, split, (zero, zero))
    moves.leave(d_query)
    moves.arrive(h_weight)
    d_aggregated[...] = nt(d_modulator[...], h_weight[...])
    moves.leave(d_aggregated)
    moves.arrive(normed, aggregated, mixed)
    head[0:width, :] = tn(d_query[...], normed[...])
    head[width : 2 * width, :] = tn(aggregated[...], d_modulator[...])
    head[2 * width : 3 * width, :] = tn(mixed[...], d_branch[...])
    sums = (h_bias, proj_bias, d_gain, d_bias, out_bias, query_bias)
    head[3 * width :, :] = jnp.concatenate(
        [row_sum(item) for item in sums]
        + [jnp.zeros((units.head_total - 3 * width - 6, width), f32)]
    )
    for half, target in enumerate((own_rest, other_rest)):
        absolute = jnp.bitwise_xor(core[0], half)
        for piece in range(units.pieces):
            first = (absolute * units.pieces + piece) * units.head_rows
            target[piece] = head[pl.ds(pl.multiple_of(first, 8), units.head_rows), :].astype(bf16)


def levels_back_kernel(
    shape,
    moves,
    small,
    gates,
    d_aggregated,
    pooled,
    slope_three,
    slope_two,
    slope_one,
    one,
    two,
    three,
    d_one,
    d_two,
    d_three,
    rounded,
    d_gates,
    tap_ref,
    d_levels,
    products,
    d_context,
):
    width = shape.width
    inner = shape.inner
    moves.arrive(small)
    spread_taps(shape, small, tap_ref)
    for ref in (d_one, d_two, d_three):
        clear_edges(shape, ref)
    moves.arrive(gates, d_aggregated, pooled)
    pool_grad = [None] * sublanes
    for image in range(shape.images):
        rows = pl.ds(image * shape.segment, shape.segment)
        for tile in range(shape.tiles):
            slot = tile * shape.images + image
            values = d_aggregated[rows, columns(tile)]
            for level in range(3):
                d_levels[pl.ds(level * inner + slot, shape.patches, stride=sublanes), :] = (
                    values[: shape.patches] * gates[rows, columns(level)][: shape.patches]
                )
            pool_grad[slot] = jnp.sum(values * gates[rows, columns(3)], axis=0, keepdims=True)
    blank = jnp.zeros((1, lanes), f32)
    pool_grad = jnp.concatenate([blank if item is None else item for item in pool_grad])
    pool_grad = pool_grad * pooled[sublanes : 2 * sublanes, :]
    wide_pool = jnp.concatenate([pool_grad] * shape.side)

    def third(line, carry):
        here = pl.multiple_of(line * shape.line, shape.line)
        value = (d_levels[pl.ds(2 * inner + here, shape.line), :] + wide_pool) * slope_three[
            pl.ds(here, shape.line), :
        ]
        d_three[pl.ds(here + shape.centre, shape.line), :] = value
        return carry

    moves.arrive(slope_three)
    lax.fori_loop(0, shape.side, third, 0)
    moves.leave(d_three)
    moves.arrive(slope_two, slope_one)
    for level, source, target, slope in ((2, d_three, d_two, slope_two), (1, d_two, d_one, slope_one)):

        def back(line, carry, level=level, source=source, target=target, slope=slope):
            here = pl.multiple_of(line * shape.line, shape.line)
            value = correlate(shape, source, tap_ref, level, line, True)
            value = (value + d_levels[pl.ds((level - 1) * inner + here, shape.line), :]) * slope[
                pl.ds(here, shape.line), :
            ]
            target[pl.ds(here + shape.centre, shape.line), :] = value
            return carry

        lax.fori_loop(0, shape.side, back, 0)
        moves.leave(target)

    def back_context(line, carry):
        here = pl.multiple_of(line * shape.line, shape.line)
        d_levels[pl.ds(here, shape.line), :] = correlate(shape, d_one, tap_ref, 0, line, True)
        return carry

    lax.fori_loop(0, shape.side, back_context, 0)
    for image, tile, slot in shape.places():
        first = image * shape.segment
        d_context[first : first + shape.patches, columns(tile)] = d_levels[
            pl.ds(slot, shape.patches, stride=sublanes), :
        ]
        if tile == 0 and shape.segment > shape.patches:
            d_context[first + shape.patches : first + shape.segment, :] = jnp.zeros(
                (shape.segment - shape.patches, width), f32
            )
    rounded[...] = d_context[...].astype(bf16)
    moves.leave(rounded)
    moves.arrive(one, two, three)
    for image in range(shape.images):
        rows = pl.ds(image * shape.segment, shape.segment)
        totals = [None] * 4
        for tile in range(shape.tiles):
            slot = tile * shape.images + image
            values = d_aggregated[rows, columns(tile)]
            for level, ref in enumerate((one, two, three)):
                term = values * level_rows(shape, ref, image, slot)
                totals[level] = term if tile == 0 else totals[level] + term
            term = values * pooled[slot : slot + 1, :]
            totals[3] = term if tile == 0 else totals[3] + term
        for gate in range(4):
            products[rows, columns(gate)] = totals[gate]
    chooser = (
        lax.broadcasted_iota(jnp.int32, (4 * lanes, lanes), 0) // lanes
        == lax.broadcasted_iota(jnp.int32, (4 * lanes, lanes), 1)
    ).astype(f32).astype(bf16)
    d_gates[...] = nn(products[...].astype(bf16), chooser).astype(bf16)


def exit_kernel(
    shape,
    units,
    moves,
    core,
    two,
    d_three,
    one,
    d_two,
    context,
    d_one,
    rounded,
    d_gates,
    small,
    normed,
    f_turned,
    d_query,
    tokens,
    d_inputs,
    own_late,
    other_late,
    packed,
    tap_grad,
    inputs,
    d_context,
    gathered,
    gate_rows,
):
    width = shape.width
    moves.arrive(two, d_three)
    tap_grads(shape, two, d_three, 2, tap_grad)
    moves.arrive(one, d_two)
    tap_grads(shape, one, d_two, 1, tap_grad)
    moves.arrive(context, d_one)
    tap_grads(shape, context, d_one, 0, tap_grad)
    moves.arrive(rounded, d_gates, small, normed, f_turned, d_query, tokens)
    gathered[0:width, :] = tn(rounded[...], normed[...])
    gathered[width : width + 8, :] = tn(d_gates[...], normed[...])[0:8]
    for tile in range(shape.tiles):
        total = None
        for image in range(shape.images):
            slot = tile * shape.images + image
            term = tap_grad[pl.ds(slot, taps, stride=sublanes), :]
            total = term if total is None else total + term
        gathered[width + 8 : width + 8 + taps, columns(tile)] = total
    gate_rows[...] = jnp.concatenate(
        [
            f_turned[2 * width : 2 * width + 4, :].astype(f32),
            jnp.zeros((lanes - 4, width), f32),
        ]
    ).astype(bf16)
    d_normed = d_context
    gate_bias = row_sum(fold(d_gates[...].astype(f32)))
    context_bias = row_sum(fold(rounded[...].astype(f32)))
    d_normed[...] = (
        nn(d_query[...], f_turned[0:width, :])
        + nn(rounded[...], f_turned[width : 2 * width, :])
        + nn(d_gates[...], gate_rows[...])
    )
    packed[...] = tokens[...].astype(f32)
    unpack(shape, packed, inputs)
    gain = small[LN1_GAIN : LN1_GAIN + 1, :]
    zero = jnp.zeros((8, width), f32)

    def finish(rows, carry):
        values = d_normed[rows, :]
        d_input, d_gain = norm_back(inputs[rows, :], values, gain)
        d_inputs[rows, :] = d_input
        return carry[0] + fold(d_gain), carry[1] + fold(values)

    d_gain, d_bias = blocks(shape, finish, (zero, zero))
    moves.leave(d_inputs)
    last = width + 8 + taps
    rest = units.late_total - last - 4
    gathered[last:, :] = jnp.concatenate(
        [
            row_sum(d_gain),
            row_sum(d_bias),
            context_bias,
            jnp.concatenate([gate_bias, jnp.zeros((1, width - lanes), f32)], axis=1),
            jnp.zeros((rest, width), f32),
        ]
    )
    for half, target in enumerate((own_late, other_late)):
        absolute = jnp.bitwise_xor(core[0], half)
        for place in range(2):
            for spot in range(units.shards):
                first = ((place * 2 + absolute) * units.shards + spot) * units.late_rows
                target[place * units.shards + spot] = gathered[
                    pl.ds(pl.multiple_of(first, 16), units.late_rows), :
                ].astype(bf16)


def finish_kernel(
    shape,
    moves,
    d_middle,
    d_inputs,
    small,
    middle,
    out_near,
    out_far,
    tokens_grad,
    block_out,
    rows_ref,
):
    moves.arrive(d_middle, d_inputs)

    def add_grads(rows, carry):
        rows_ref[rows, :] = d_middle[rows, :] + d_inputs[rows, :]
        return carry

    blocks(shape, add_grads, 0)
    pack(shape, rows_ref, tokens_grad)
    moves.leave(tokens_grad)
    moves.arrive(small, middle, out_near, out_far)

    def add_outs(rows, carry):
        total = middle[rows, :] + small[FC2_BIAS : FC2_BIAS + 1, :]
        rows_ref[rows, :] = total + out_near[rows, :] + out_far[rows, :].astype(f32)
        return carry

    blocks(shape, add_outs, 0)
    pack(shape, rows_ref, block_out)


def unpack_kernel(
    shape,
    units,
    spots,
    piece,
    piece_x,
    piece_core,
    piece_both,
    late_own,
    late_core,
    own,
    own_b,
    own_x,
    own_both,
    core_own,
    core_b,
    core_x,
    core_both,
    ln1_gain,
    ln1_bias,
    f_grad,
    f_bias,
    small_grad,
    middle_grad,
    large_grad,
    h_grad,
    h_bias,
    proj_grad,
    proj_bias,
    ln2_gain,
    ln2_bias,
    first_grad,
    first_bias,
    second_grad,
    second_bias,
    held,
    held_late,
    head,
    late,
):
    width = shape.width
    unit = units.unit
    size = own.shape[0]
    parts = (own, own_b, own_x, own_both, core_own, core_b, core_x, core_both)
    for index, part in enumerate(parts):
        held[index * size : (index + 1) * size, :] = part[...].astype(f32)
    late_size = late_own.shape[0]
    held_late[0:late_size, :] = late_own[...].astype(f32)
    held_late[late_size : 2 * late_size, :] = late_core[...].astype(f32)
    core, shift = spots[0], spots[2]
    far = units.shards // 2
    for half in range(2):
        late_base = jnp.bitwise_xor(core, half) * late_size
        for place in range(2):
            for close in range(2):
                slot = jnp.bitwise_xor(core, half) * 4 + jnp.bitwise_xor(spots[3], place) * 2
                base = (slot + jnp.bitwise_xor(spots[4], close)) * size
                for away in range(far):
                    here = base + jnp.bitwise_xor(spots[5], away) * units.head_rows
                    to = ((half * 2 + place) * far + away) * 2 + close
                    head[to * units.head_rows : (to + 1) * units.head_rows, :] = held[
                        pl.ds(pl.multiple_of(here, 8), units.head_rows), :
                    ]
                    here = late_base + ((place * far + away) * 2 + close) * units.late_rows
                    to = ((place * 2 + half) * far + away) * 2 + close
                    late[to * units.late_rows : (to + 1) * units.late_rows, :] = held_late[
                        pl.ds(pl.multiple_of(here, 8), units.late_rows), :
                    ]
    total = None
    lane = lax.broadcasted_iota(jnp.int32, (8, width), 1)
    for index, source in enumerate((piece, piece_core, piece_x, piece_both)):
        quarter = jnp.bitwise_xor(spots[1], index)
        to = pl.ds(pl.multiple_of(quarter * unit, 8), unit)
        first_grad[to, :] = source[0:unit, :].astype(f32)
        second_grad[to, :] = source[unit : 2 * unit, :].astype(f32)
        row = source[2 * unit : units.piece_rows, :].astype(f32)[0:8]
        moved = shift + quarter * unit
        moved = jnp.where(moved >= width, moved - width, moved)
        row = pltpu.roll(row, moved, 1)
        row = jnp.where((lane >= quarter * unit) & (lane < (quarter + 1) * unit), row, 0.0)
        total = row if total is None else total + row
    first_bias[...] = total[0:1, 0 : first_bias.shape[0]].reshape(first_bias.shape)
    f_grad[0:width, :] = head[0:width, :]
    f_grad[width : 2 * width + 4, :] = late[0 : width + 4, :]
    h_grad[...] = head[width : 2 * width, :]
    proj_grad[...] = head[2 * width : 3 * width, :]
    first = width + 8
    small_grad[...] = late[first : first + 9, :]
    middle_grad[...] = late[first + 9 : first + 34, :]
    large_grad[...] = late[first + 34 : first + taps, :]
    first = first + taps
    for out, source, row in (
        (h_bias, head, 3 * width),
        (proj_bias, head, 3 * width + 1),
        (ln2_gain, head, 3 * width + 2),
        (ln2_bias, head, 3 * width + 3),
        (second_bias, head, 3 * width + 4),
        (ln1_gain, late, first),
        (ln1_bias, late, first + 1),
    ):
        out[...] = source[row : row + 1, :].reshape(width)
    f_bias[0:width] = head[3 * width + 5 : 3 * width + 6, :].reshape(width)
    f_bias[width : 2 * width] = late[first + 2 : first + 3, :].reshape(width)
    f_bias[2 * width : 2 * width + 4] = late[first + 3 : first + 4, 0:4].reshape(4)


def call(kernel, name, outs, scratch, micros, room, *operands):
    spec = pl.BlockSpec(memory_space=pltpu.VMEM)
    outer = pl.BlockSpec(memory_space=pltpu.HBM)
    far_in = [isinstance(item, Far) for item in operands]
    far_out = [isinstance(item, Far) for item in outs]
    anywhere = [isinstance(item, Anywhere) for item in operands]
    raw = [isinstance(item, Raw) for item in operands]
    operands = [item.value if far else item for item, far in zip(operands, far_in)]
    operands = [
        pltpu.with_memory_space_constraint(item, pltpu.HBM) if far and not free else item
        for item, far, free in zip(operands, far_in, anywhere)
    ]
    raw_out = [isinstance(item, Raw) for item in outs]
    outs = [
        pltpu.HBM(item.value.shape, item.value.dtype) if far else item
        for item, far in zip(outs, far_out)
    ]
    specs = []
    for item, far, free in zip(operands, far_in, anywhere):
        if free:
            specs.append(pl.BlockSpec(memory_space=pl.ANY))
        elif item.dtype == jnp.int32:
            specs.append(pl.BlockSpec(memory_space=pltpu.SMEM))
        else:
            specs.append(outer if far else spec)
    out_specs = [outer if far else spec for far in far_out]
    if name not in plain:
        far_in = [far and not own for far, own in zip(far_in, raw)]
        far_out = [far and not own for far, own in zip(far_out, raw_out)]
        pairs = list(zip(operands, far_in)) + list(zip(outs, far_out))
        buffers = [pltpu.VMEM(item.shape, item.dtype) for item, far in pairs if far]
        extra = sum(raw) + sum(raw_out)
        semaphores = pltpu.SemaphoreType.DMA((max(len(buffers) + extra, 1),))
        scratch = list(scratch) + buffers + [semaphores]
        kernel = with_moves(kernel, far_in, far_out, extra)
    moved = sum(item.size * item.dtype.itemsize for item in operands)
    return pl.pallas_call(
        kernel,
        name=name,
        out_shape=outs,
        in_specs=specs,
        out_specs=out_specs,
        scratch_shapes=scratch,
        compiler_params=pltpu.CompilerParams(vmem_limit_bytes=room * 1024 * 1024),
        cost_estimate=pl.CostEstimate(
            flops=int(micros * 1.1e9), bytes_accessed=moved, transcendentals=0
        ),
    )(*operands)


plain = ("piece", "sum", "pair", "share", "unpack")


class Far:
    def __init__(self, value):
        self.value = value


class Anywhere(Far):
    pass


class Raw(Far):
    pass


def far_array(*dims, kind=jnp.float32):
    return Far(array(*dims, kind=kind))


def array(*dims, kind=jnp.float32):
    return jax.ShapeDtypeStruct(dims, kind)


def to_packed(values, shape):
    moved = with_layout_constraint(values.transpose(1, 2, 0, 3), Layout((0, 1, 2, 3)))
    moved = moved.reshape(shape.patches, shape.images, shape.tiles, lanes)
    moved = with_layout_constraint(moved, Layout((0, 2, 1, 3)))
    return moved.transpose(0, 2, 1, 3).reshape(shape.packed, lanes)


def from_packed(values, shape):
    moved = values.reshape(shape.patches, shape.tiles, shape.images, lanes).transpose(0, 2, 1, 3)
    moved = moved.reshape(shape.side, shape.side, shape.images, shape.width)
    return moved.transpose(2, 0, 1, 3)


everyone = ("x", "core", "a", "b")


def gather_plainly(units, first, bias, second):
    first = lax.all_gather(first, ("a", "b"), axis=0, tiled=True)
    second = lax.all_gather(second, ("a", "b"), axis=0, tiled=True)
    bias = lax.all_gather(bias, ("a", "b"), axis=0, tiled=True)
    width = first.shape[1]
    rows = jnp.pad(bias.reshape(4, 1, 1, width), ((0, 0), (0, units.shards - 1), (0, 15), (0, 0)))
    shape = (4, units.shards, units.unit, width)
    both = jnp.concatenate([first.reshape(shape), second.reshape(shape), rows], axis=2)
    both = both.reshape(4, units.shards * units.piece_rows, width)
    return [both[index] for index in range(4)]


def total_of(values, parts):
    rows = values.shape[0] // parts
    kernel = functools.partial(sum_kernel, parts)
    values = values.reshape(parts, rows, values.shape[1])
    return call(kernel, "sum", [array(rows, values.shape[2], kind=bf16)], [], 1, 4, values)[0]


def reduce_plainly(shape, units, feed, rest, late):
    width = shape.width
    unit = units.unit
    both = jnp.stack(feed).reshape(4, units.shards, units.piece_rows, width)
    first = both[:, :, :unit].reshape(4 * units.total, width)
    second = both[:, :, unit : 2 * unit].reshape(4 * units.total, width)
    bias = both[:, 0, 2 * unit].reshape(4 * units.total, 1)

    def shared(values):
        part = lax.psum_scatter(values, ("a", "b"), scatter_dimension=0, tiled=True)
        return lax.psum(part, ("x", "core")).astype(f32)

    late = jnp.stack(late).reshape(2, 2, units.shards, units.late_rows, width)
    late = late.transpose(1, 0, 2, 3, 4).reshape(units.late_total, width)
    late = lax.psum(late, everyone).astype(f32)
    head = jnp.concatenate(rest).reshape(units.head_total, width)
    head = lax.psum(head, everyone).astype(f32)
    last = width + 8
    vectors = head[3 * width : 3 * width + 8]
    more = late[last + taps : last + taps + 4]
    return (
        more[0],
        more[1],
        jnp.concatenate([head[:width], late[: width + 4]]),
        jnp.concatenate([vectors[5], more[2], more[3, :4]]),
        late[last : last + 9],
        late[last + 9 : last + 34],
        late[last + 34 : last + taps],
        head[width : 2 * width],
        vectors[0],
        head[2 * width : 3 * width],
        vectors[1],
        vectors[2],
        vectors[3],
        shared(first),
        shared(bias)[:, 0],
        shared(second),
        vectors[4],
    )


def shards(
    sizes,
    tokens,
    ln1_gain,
    ln1_bias,
    f_weight,
    f_bias,
    dw_small,
    dw_middle,
    dw_large,
    h_weight,
    h_bias,
    proj_weight,
    proj_bias,
    ln2_gain,
    ln2_bias,
    fc1_weight,
    fc1_bias,
    fc2_weight,
    fc2_bias,
    out_grad,
):
    images, side, _, width = tokens.shape
    shape = Shape(images, side, width)
    rows, grid, inner = shape.rows, shape.grid, shape.inner
    hidden = fc1_weight.shape[1] * sizes["a"] * sizes["b"]
    quick = sizes["x"] == 2 and sizes["a"] * sizes["b"] == 8
    units = Units(8, hidden // 32)
    f_turned = f_weight.T
    first, second = fc1_weight.T, fc2_weight
    scratch = pltpu.VMEM
    core = jnp.zeros((1,), jnp.int32)
    if quick:
        core = lax.axis_index("core").astype(jnp.int32).reshape(1)
        quarter = lax.axis_index("x") * 2 + core[0]
        shard = lax.axis_index("a") * 2 + lax.axis_index("b")
        turn = lax.rem(shard - quarter + units.shards, units.shards) * units.unit
        spots = jnp.stack([quarter, shard, turn]).astype(jnp.int32)
        (pieces,) = call(
            functools.partial(piece_kernel, units, units.shards),
            "piece",
            [array(units.shards * units.piece_rows, width, kind=bf16)],
            [
                scratch((2, units.unit, width), bf16),
                scratch(fc1_bias.shape, bf16),
                pltpu.SemaphoreType.DMA((3,)),
            ],
            1,
            6,
            spots,
            Far(first),
            Far(second),
            Far(fc1_bias),
        )
        weights = exchange(pieces, ("a", "b"))
    tokens_packed = to_packed(tokens, shape)

    def rows_array(kind=bf16):
        return far_array(rows, width, kind=kind)

    small, cot, inputs, normed, query, gates, context, one, slope_one = call(
        functools.partial(entry_kernel, shape),
        "entry",
        [
            far_array(96, width),
            rows_array(),
            array(rows, width),
            rows_array(),
            array(rows, width),
            array(rows, 4 * lanes),
            far_array(grid, lanes),
            array(grid, lanes),
            far_array(inner, lanes),
        ],
        [
            scratch((taps * sublanes, lanes), f32),
            scratch((shape.packed, lanes), f32),
            scratch((rows, width), f32),
        ],
        5,
        16,
        Far(tokens_packed),
        Far(f_turned),
        Far(to_packed(out_grad, shape)),
        dw_small,
        dw_middle,
        dw_large,
        ln1_gain,
        ln1_bias,
        f_bias,
        h_bias,
        proj_bias,
        ln2_gain,
        ln2_bias,
        fc2_bias,
    )
    if quick:
        cot_far = flip(cot, "x")
        cot_core = flip(cot)
    one, gates, query, *results = call(
        functools.partial(modulation_kernel, shape),
        "modulation",
        [
            Raw(array(grid, lanes)),
            Raw(array(rows, 4 * lanes)),
            Raw(array(rows, width)),
            rows_array(f32),
            rows_array(),
            rows_array(),
            rows_array(f32),
            rows_array(),
            far_array(grid, lanes),
            far_array(grid, lanes),
            far_array(inner, lanes),
            far_array(inner, lanes),
            far_array(2 * sublanes, lanes),
        ],
        [scratch((rows, width), f32), scratch((taps * sublanes, lanes), f32)],
        8,
        20,
        one,
        Far(small),
        gates,
        Far(h_weight),
        query,
        inputs,
        Far(proj_weight),
    )
    modulator, aggregated, mixed, middle, normed_two, *results = results
    two, three, slope_two, slope_three, pooled = results

    def feed(resumed, outs, *operands):
        return call(
            functools.partial(feed_kernel, shape, units, resumed),
            "feed",
            outs,
            [
                scratch((units.total, width), bf16),
                scratch((units.total, width), bf16),
                scratch((2 * units.total, width), f32),
                scratch((8, width), f32),
            ],
            6,
            24,
            *operands,
        )

    near_rows = array(rows, width, kind=bf16)
    feed_total = array(units.shards * units.piece_rows, width, kind=bf16)
    if quick:
        cot_both = flip(after(cot_far, middle))
        normed_far = flip(normed_two, "x")
        normed_core = flip(normed_two)
        out_own, out_core, d_own, d_core, *carry = feed(
            False,
            [near_rows] * 4 + [array(2 * units.total, width), array(8, width)],
            weights,
            Far(normed_two),
            normed_core,
            Far(cot),
            cot_core,
        )
        out_core, d_core = flip(out_core), flip(d_core)
        normed_far = after(normed_far, d_own)
        normed_both = flip(normed_far)
        out_far, d_far, both, d_near, out_near, feed_grads = feed(
            True,
            [near_rows] * 2
            + [array(2 * rows, width, kind=bf16), rows_array(f32), rows_array(f32), feed_total],
            weights,
            normed_far,
            normed_both,
            cot_far,
            cot_both,
            *carry,
            d_own,
            d_core,
            out_own,
            out_core,
        )
        arrived = flip(both)
        d_far, out_far = call(
            functools.partial(rows_kernel, shape),
            "rows",
            [near_rows, rows_array()],
            [],
            1,
            8,
            d_far,
            out_far,
            arrived,
        )
        feed_grads = after(feed_grads, d_far)
        d_far = flip(d_far, "x")
        feed_parts = exchange(feed_grads, ("a", "b"))
    else:
        out_far = d_far = jnp.zeros((rows, width), bf16)
        out_near, d_near, feed_grads = jnp.zeros((rows, width), f32), 0.0, []
        for weights in gather_plainly(units, first, fc1_bias, second):
            out, d_out, grads = feed(
                None, [near_rows, near_rows, feed_total], weights, normed_two, cot
            )
            out_near, d_near = out_near + out.astype(f32), d_near + d_out.astype(f32)
            feed_grads.append(grads)
    rest = array(units.pieces, units.head_rows, width, kind=bf16)
    later = [gates, pooled, slope_three, slope_two, slope_one, one, two, three]
    d_middle, d_query, d_aggregated, own_rest, other_rest, *fetched = call(
        functools.partial(heads_kernel, shape, units),
        "heads",
        [rows_array(f32), rows_array(), array(rows, width), rest, rest]
        + [array(*item.shape) for item in later],
        [
            scratch((rows, width), f32),
            scratch((rows, width), bf16),
            scratch((units.head_total, width), f32),
            scratch((rows, width), bf16),
        ],
        5,
        16,
        core,
        Far(small),
        Far(cot),
        Far(middle),
        Far(d_near),
        d_far,
        Far(proj_weight),
        Far(query),
        Far(modulator),
        Far(h_weight),
        Far(normed),
        Far(aggregated),
        Far(mixed),
        *[Raw(item) for item in later],
    )
    if quick:
        out_far = flip(after(out_far, d_middle), "x")
        rest_arrived = flip(other_rest)
    d_one, d_two, d_three, rounded, d_gates = call(
        functools.partial(levels_back_kernel, shape),
        "levels_back",
        [
            far_array(grid, lanes),
            far_array(grid, lanes),
            far_array(grid, lanes),
            rows_array(),
            far_array(rows, lanes, kind=bf16),
        ],
        [
            scratch((taps * sublanes, lanes), f32),
            scratch((3 * inner, lanes), f32),
            scratch((rows, 4 * lanes), f32),
            scratch((rows, width), f32),
        ],
        8,
        24,
        Far(small),
        fetched[0],
        d_aggregated,
        *fetched[1:],
    )
    if quick:
        (rest_half,) = call(pair_kernel, "pair", [rest], [], 1, 4, own_rest, rest_arrived)
        feed_parts = after(feed_parts, d_one)
        piece = total_of(feed_parts, units.shards)
        rest_half = after(rest_half, piece)
        d_one = after(d_one, rest_half, out_far)
        shares = rest_half.shape
        rest_parts = exchange(rest_half.reshape(-1, width), ("x", "a", "b")).reshape(shares)
    late = array(units.pieces, units.late_rows, width, kind=bf16)
    d_inputs, own_late, other_late = call(
        functools.partial(exit_kernel, shape, units),
        "exit",
        [rows_array(f32), late, late],
        [
            scratch((shape.packed, lanes), f32),
            scratch((taps * sublanes, lanes), f32),
            scratch((rows, width), f32),
            scratch((rows, width), f32),
            scratch((units.late_total, width), f32),
            scratch((lanes, width), bf16),
        ],
        9,
        24,
        core,
        Far(two),
        Far(d_three),
        Far(one),
        Far(d_two),
        Far(context),
        Far(d_one),
        Far(rounded),
        Far(d_gates),
        Far(small),
        Far(normed),
        Far(f_turned),
        Far(d_query),
        Far(tokens_packed),
    )
    if quick:
        late_arrived = flip(other_late)
        piece_x = flip(piece, "x")
        piece_core, piece_both = flip(piece), flip(piece_x)
        rest_parts = after(rest_parts, own_late)
        head_sum = total_of(rest_parts.reshape(-1, width), units.pieces)
        (late_half,) = call(pair_kernel, "pair", [late], [], 1, 4, own_late, late_arrived)
        late_half = after(late_half, head_sum)
        shares = late_half.shape
        late_parts = exchange(late_half.reshape(-1, width), ("x", "a", "b")).reshape(shares)
        d_inputs = after(d_inputs, late_half)
    tokens_grad, block_out = call(
        functools.partial(finish_kernel, shape),
        "finish",
        [far_array(shape.packed, lanes), far_array(shape.packed, lanes)],
        [scratch((rows, width), f32)],
        3,
        16,
        Far(d_middle),
        Far(d_inputs),
        Far(small),
        Far(middle),
        Far(out_near),
        Anywhere(out_far),
    )
    if quick:
        steps = [flip(head_sum, "a", sizes["a"], bit) for bit in range(1, sizes["a"])]
        own = jnp.concatenate([head_sum] + steps)
        held_b, held_x = flip(own, "b"), flip(own, "x")
        held_both = flip(held_b, "x")
        held = [own, held_b, held_x, held_both]
        late_parts = after(late_parts, tokens_grad)
        (share,) = call(
            share_kernel,
            "share",
            [array(units.pieces, units.late_rows, width, kind=bf16)],
            [],
            1,
            6,
            late_parts,
        )
        share = after(share, piece_core, piece_both, held_both)
        late_own = exchange(share.reshape(-1, width), ("x", "a", "b"))
        held = [late_own, flip(late_own)] + held + [flip(item) for item in held]
        turn = lax.rem(units.shards - shard, units.shards) * units.unit
        spots = [core[0], quarter, turn] + [lax.axis_index(axis) for axis in ("x", "b", "a")]
        spots = jnp.stack(spots).astype(jnp.int32)
        total = 4 * units.unit
        others = call(
            functools.partial(unpack_kernel, shape, units),
            "unpack",
            [
                array(width),
                array(width),
                array(2 * width + 4, width),
                array(2 * width + 4),
                array(9, width),
                array(25, width),
                array(49, width),
                array(width, width),
                array(width),
                array(width, width),
                array(width),
                array(width),
                array(width),
                array(total, width),
                array(total),
                array(total, width),
                array(width),
            ],
            [
                scratch((units.head_total, width), f32),
                scratch((units.late_total, width), f32),
                scratch((units.head_total, width), f32),
                scratch((units.late_total, width), f32),
            ],
            2,
            16,
            spots,
            piece,
            piece_x,
            piece_core,
            piece_both,
            *held,
        )
    else:
        others = reduce_plainly(
            shape, units, feed_grads, (own_rest, other_rest), (own_late, other_late)
        )
    others = list(others)
    others[2] = others[2].T
    others[13] = others[13].T
    return from_packed(block_out, shape), from_packed(tokens_grad, shape), *others


def solution(mesh):
    img, mlp = mesh.shape["img"], mesh.shape["mlp"]
    sizes = {"x": img // 2, "core": 2, "a": mlp // 2, "b": 2}
    finer = Mesh(mesh.devices.reshape(*sizes.values()), everyone)
    images = P(everyone, None, None, None)
    hidden = ("a", "b")
    return jax.shard_map(
        functools.partial(shards, sizes),
        mesh=finer,
        in_specs=(images,)
        + (P(),) * 13
        + (P(None, hidden), P(hidden), P(hidden, None), P(), images),
        out_specs=(images, images)
        + (P(),) * 13
        + (P(None, hidden), P(hidden), P(hidden, None), P()),
        check_vma=False,
    )
```

```python
import functools
import math

import jax
import jax.numpy as jnp
from jax import lax
from jax.experimental import pallas as pl
from jax.experimental.pallas import tpu as pltpu
from jax.experimental.layout import Layout, with_layout_constraint
from jax.sharding import Mesh
from jax.sharding import PartitionSpec as P

epsilon = 1e-05
lanes = 128
sublanes = 8
edge = 3
extents = (3, 5, 7)
starts = (0, 9, 34)
taps = 83
LN1_GAIN, LN1_BIAS, QUERY_BIAS, CONTEXT_BIAS, GATE_BIAS = 83, 84, 85, 86, 87
H_BIAS, PROJ_BIAS, LN2_GAIN, LN2_BIAS, FC2_BIAS = 88, 89, 90, 91, 92
f32 = jnp.float32
bf16 = jnp.bfloat16


def flip(values, axis="core", size=2, bit=1):
    return lax.ppermute(values, axis, [(place, place ^ bit) for place in range(size)])


def exchange(values, axes):
    return lax.all_to_all(values, axes, split_axis=0, concat_axis=0, tiled=True)


def after(values, *others):
    return lax.optimization_barrier((values,) + others)[0]


def nn(left, right):
    return jnp.dot(left, right, preferred_element_type=f32)


def nt(left, right):
    return lax.dot_general(left, right, (((1,), (1,)), ((), ())), preferred_element_type=f32)


def tn(left, right):
    return lax.dot_general(left, right, (((0,), (0,)), ((), ())), preferred_element_type=f32)


def gelu_pair(values):
    below = 0.5 * (1.0 + lax.erf(values * math.sqrt(0.5)))
    density = jnp.exp(values * values * -0.5) * (1.0 / math.sqrt(2.0 * math.pi))
    return values * below, below + values * density


class Shape:
    def __init__(self, images, side, width):
        self.images, self.side, self.width = images, side, width
        self.tiles = width // lanes
        self.slots = images * self.tiles
        self.patches = side * side
        self.segment = -(-self.patches // 8) * 8
        self.rows = images * self.segment
        self.line = side * sublanes
        self.centre = edge * self.line
        self.grid = (side + 2 * edge) * self.line
        self.inner = side * self.line
        self.packed = self.patches * self.slots
        self.block = next(size for size in (80, 40, 16, 8) if self.rows % size == 0)

    def places(self):
        return [
            (image, tile, tile * self.images + image)
            for image in range(self.images)
            for tile in range(self.tiles)
        ]


def columns(tile):
    return slice(tile * lanes, (tile + 1) * lanes)


def unpack(shape, packed, rows):
    for image, tile, slot in shape.places():
        first = image * shape.segment
        rows[first : first + shape.patches, columns(tile)] = packed[
            pl.ds(slot, shape.patches, stride=shape.slots), :
        ]
    for image in range(shape.images):
        first = image * shape.segment
        spare = shape.segment - shape.patches
        if spare:
            rows[first + shape.patches : first + shape.segment, 0 : shape.width] = jnp.zeros(
                (spare, shape.width), f32
            )


def pack(shape, rows, packed):
    for image, tile, slot in shape.places():
        first = image * shape.segment
        packed[pl.ds(slot, shape.patches, stride=shape.slots), :] = rows[
            first : first + shape.patches, columns(tile)
        ]


def blocks(shape, body, init=None):
    def step(index, carry):
        first = pl.multiple_of(index * shape.block, shape.block)
        return body(pl.ds(first, shape.block), carry)

    return lax.fori_loop(0, shape.rows // shape.block, step, init)


def normalise(values):
    average = jnp.mean(values, axis=-1, keepdims=True)
    centred = values - average
    variance = jnp.mean(centred * centred, axis=-1, keepdims=True)
    scale = lax.rsqrt(variance + epsilon)
    return centred * scale, scale


def norm_back(values, grad, gain):
    unit, scale = normalise(values)
    inner = grad * gain
    first = jnp.mean(inner, axis=-1, keepdims=True)
    second = jnp.mean(inner * unit, axis=-1, keepdims=True)
    return scale * (inner - first - unit * second), grad * unit


def fold(values):
    return jnp.sum(values.reshape(values.shape[0] // 8, 8, values.shape[1]), axis=0)


def row_sum(values):
    return jnp.sum(values, axis=0, keepdims=True)


def spread_taps(shape, small, tap_ref):
    tap_ref[...] = jnp.zeros_like(tap_ref)
    for _, tile, slot in shape.places():
        tap_ref[pl.ds(slot, taps, stride=sublanes), :] = small[0:taps, columns(tile)]


def line_at(shape, ref, line):
    first = pl.multiple_of(line * shape.line, shape.line)
    values = ref[pl.ds(first, shape.line), :]
    return [values[w * sublanes : (w + 1) * sublanes] for w in range(shape.side)]


def correlate(shape, source, tap_ref, level, line, turned):
    extent = extents[level]
    reach = extent // 2
    totals = [None] * shape.side
    for down in range(extent):
        values = line_at(shape, source, line + down + edge - reach)
        for along in range(extent):
            entry = down * extent + along
            if turned:
                entry = extent * extent - 1 - entry
            tap = tap_ref[pl.ds((starts[level] + entry) * sublanes, sublanes), :]
            for w in range(shape.side):
                other = w + along - reach
                if 0 <= other < shape.side:
                    term = values[other] * tap
                    totals[w] = term if totals[w] is None else totals[w] + term
    return jnp.concatenate(totals, axis=0)


def tap_grads(shape, source, grad, level, out):
    extent = extents[level]
    reach = extent // 2
    for down in range(extent):

        def step(line, totals, down=down):
            values = line_at(shape, source, line + down + edge - reach)
            grads = line_at(shape, grad, line + edge)
            result = []
            for along in range(extent):
                total = totals[along]
                for w in range(shape.side):
                    other = w + along - reach
                    if 0 <= other < shape.side:
                        total = total + values[other] * grads[w]
                result.append(total)
            return tuple(result)

        zero = jnp.zeros((sublanes, lanes), f32)
        first, last = max(0, reach - down), min(shape.side, shape.side + reach - down)
        totals = lax.fori_loop(first, last, step, (zero,) * extent)
        for along in range(extent):
            out[pl.ds((starts[level] + down * extent + along) * sublanes, sublanes), :] = totals[
                along
            ]


def clear_edges(shape, ref):
    zeros = jnp.zeros((shape.centre, lanes), f32)
    ref[0 : shape.centre, :] = zeros
    ref[shape.centre + shape.inner : shape.grid, :] = zeros


def gate_values(shape, normed, f_turned, small, gates):
    weight = f_turned[2 * shape.width : 2 * shape.width + 4, :].astype(f32)
    wide = jnp.concatenate(
        [jnp.broadcast_to(weight[g : g + 1], (lanes, shape.width)) for g in range(4)]
    ).astype(bf16)
    bias = small[GATE_BIAS : GATE_BIAS + 1, :]
    wide_bias = jnp.concatenate(
        [jnp.broadcast_to(bias[:, g : g + 1], (1, lanes)) for g in range(4)], axis=1
    )
    gates[...] = nt(normed[...], wide) + wide_bias


def level_rows(shape, level, image, slot):
    return level[pl.ds(shape.centre + slot, shape.segment, stride=sublanes), :]


def run_levels(shape, moves, chain, tap_ref):
    total = jnp.zeros((sublanes, lanes), f32)
    for level, source, target, slope in chain:
        clear_edges(shape, target)

        def line_step(line, total, level=level, source=source, target=target, slope=slope):
            before = correlate(shape, source, tap_ref, level, line, False)
            value, rise = gelu_pair(before)
            here = pl.multiple_of((line + edge) * shape.line, shape.line)
            target[pl.ds(here, shape.line), :] = value
            slope[pl.ds(pl.multiple_of(line * shape.line, shape.line), shape.line), :] = rise
            if level == 2:
                total = total + fold(value)
            return total

        total = lax.fori_loop(0, shape.side, line_step, total)
        moves.leave(target, slope)
    return total


def entry_kernel(
    shape,
    moves,
    tokens,
    f_turned,
    out_grad,
    dw_small,
    dw_middle,
    dw_large,
    ln1_gain,
    ln1_bias,
    f_bias,
    h_bias,
    proj_bias,
    ln2_gain,
    ln2_bias,
    fc2_bias,
    small,
    cot,
    inputs,
    normed,
    query,
    gates,
    context,
    one,
    slope_one,
    tap_ref,
    packed,
    wide,
):
    width = shape.width
    for source, first in zip((dw_small, dw_middle, dw_large), starts):
        small[first : first + source.shape[0], :] = source[...].astype(f32)
    shared = f_bias[...].astype(f32).reshape(1, 2 * width + 4)
    vectors = {
        QUERY_BIAS: shared[:, 0:width],
        CONTEXT_BIAS: shared[:, width : 2 * width],
        GATE_BIAS: jnp.concatenate(
            [shared[:, 2 * width :], jnp.zeros((1, width - 4), f32)], axis=1
        ),
    }
    for row, source in (
        (LN1_GAIN, ln1_gain),
        (LN1_BIAS, ln1_bias),
        (H_BIAS, h_bias),
        (PROJ_BIAS, proj_bias),
        (LN2_GAIN, ln2_gain),
        (LN2_BIAS, ln2_bias),
        (FC2_BIAS, fc2_bias),
    ):
        vectors[row] = source[...].astype(f32).reshape(1, width)
    for row, value in vectors.items():
        small[row : row + 1, :] = value
    last = FC2_BIAS + 1
    small[last:, :] = jnp.zeros((small.shape[0] - last, width), f32)
    moves.leave(small)
    moves.arrive(tokens)
    packed[...] = tokens[...].astype(f32)
    unpack(shape, packed, inputs)
    moves.leave(inputs)
    spread_taps(shape, small, tap_ref)
    gain = small[LN1_GAIN : LN1_GAIN + 1, :]
    bias = small[LN1_BIAS : LN1_BIAS + 1, :]

    def first_norm(rows, carry):
        unit, _ = normalise(inputs[rows, :])
        normed[rows, :] = (unit * gain + bias).astype(bf16)
        return carry

    blocks(shape, first_norm, 0)
    moves.leave(normed)
    moves.arrive(out_grad)
    packed[...] = out_grad[...].astype(f32)
    unpack(shape, packed, wide)
    cot[...] = wide[...].astype(bf16)
    moves.leave(cot)
    moves.arrive(f_turned)
    wide[...] = (
        nt(normed[...], f_turned[width : 2 * width, :]) + small[CONTEXT_BIAS : CONTEXT_BIAS + 1, :]
    )
    context[...] = jnp.zeros_like(context)
    for image, tile, slot in shape.places():
        first = image * shape.segment
        context[pl.ds(shape.centre + slot, shape.patches, stride=sublanes), :] = wide[
            first : first + shape.patches, columns(tile)
        ]
    moves.leave(context)
    query[...] = nt(normed[...], f_turned[0:width, :]) + small[QUERY_BIAS : QUERY_BIAS + 1, :]
    moves.leave(query)
    gate_values(shape, normed, f_turned, small, gates)
    moves.leave(gates)
    run_levels(shape, moves, ((0, context, one, slope_one),), tap_ref)


def modulation_kernel(
    shape,
    moves,
    one,
    small,
    gates,
    h_weight,
    query,
    inputs,
    proj_weight,
    slope_one,
    far_one,
    far_gates,
    far_query,
    far_slope,
    modulator,
    aggregated,
    mixed,
    middle,
    normed_two,
    two,
    three,
    slope_two,
    slope_three,
    pooled,
    wide,
    tap_ref,
):
    chain = ((1, one, two, slope_two), (2, two, three, slope_three))
    moves.arrive(small)
    spread_taps(shape, small, tap_ref)
    moves.copy(one, far_one)
    moves.copy(gates, far_gates)
    moves.copy(query, far_query)
    moves.copy(slope_one, far_slope)
    total = run_levels(shape, moves, chain, tap_ref)
    value, rise = gelu_pair(total * (1.0 / shape.patches))
    pooled[0:sublanes, :] = value
    pooled[sublanes : 2 * sublanes, :] = rise * (1.0 / shape.patches)
    moves.leave(pooled)
    moves.arrive(h_weight, proj_weight)
    for image, tile, slot in shape.places():
        rows = pl.ds(image * shape.segment, shape.segment)
        wide[rows, columns(tile)] = (
            level_rows(shape, one, image, slot) * gates[rows, columns(0)]
            + level_rows(shape, two, image, slot) * gates[rows, columns(1)]
            + level_rows(shape, three, image, slot) * gates[rows, columns(2)]
            + value[slot : slot + 1] * gates[rows, columns(3)]
        )
    aggregated[...] = wide[...].astype(bf16)
    moves.leave(aggregated)
    modulator[...] = nn(aggregated[...], h_weight[...]) + small[H_BIAS : H_BIAS + 1, :]

    moves.leave(modulator)

    def mix(rows, carry):
        mixed[rows, :] = (query[rows, :] * modulator[rows, :]).astype(bf16)
        return carry

    blocks(shape, mix, 0)
    moves.leave(mixed)
    middle[...] = (
        inputs[...] + nn(mixed[...], proj_weight[...]) + small[PROJ_BIAS : PROJ_BIAS + 1, :]
    )
    moves.leave(middle)
    gain = small[LN2_GAIN : LN2_GAIN + 1, :]
    bias = small[LN2_BIAS : LN2_BIAS + 1, :]

    def second_norm(rows, carry):
        unit, _ = normalise(middle[rows, :])
        normed_two[rows, :] = (unit * gain + bias).astype(bf16)
        return carry

    blocks(shape, second_norm, 0)


class Moves:
    def __init__(self):
        self.incoming, self.outgoing = {}, {}
        self.started, self.free = [], []

    def copy(self, source, target):
        move = pltpu.make_async_copy(source, target, self.free.pop())
        move.start()
        self.started.append(move)

    def arrive(self, *buffers):
        for buffer in buffers:
            move = self.incoming.pop(id(buffer), None)
            if move is not None:
                move.wait()

    def leave(self, *buffers):
        for buffer in buffers:
            move = self.outgoing.pop(id(buffer), None)
            if move is not None:
                move.start()
                self.started.append(move)

    def finish(self):
        for move in list(self.incoming.values()):
            move.wait()
        for move in list(self.outgoing.values()):
            move.start()
            self.started.append(move)
        for move in self.started:
            move.wait()


def with_moves(kernel, far_in, far_out, extra):
    def run(*refs):
        refs = list(refs)
        ins, refs = refs[: len(far_in)], refs[len(far_in) :]
        outs, refs = refs[: len(far_out)], refs[len(far_out) :]
        semaphores = refs.pop()
        count = sum(far_in) + sum(far_out)
        buffers, scratch = refs[len(refs) - count :], refs[: len(refs) - count]
        moves = Moves()
        moves.free = [semaphores.at[count + spare] for spare in range(extra)]
        index = 0
        for group, flags, table in (
            (ins, far_in, moves.incoming),
            (outs, far_out, moves.outgoing),
        ):
            for place, far in enumerate(flags):
                if far:
                    buffer, outer = buffers[index], group[place]
                    pair = (outer, buffer) if group is ins else (buffer, outer)
                    move = pltpu.make_async_copy(*pair, semaphores.at[index])
                    if group is ins:
                        move.start()
                    table[id(buffer)] = move
                    group[place] = buffer
                    index += 1
        kernel(moves, *ins, *outs, *scratch)
        moves.finish()

    return run


class Units:
    def __init__(self, shards, unit):
        self.shards, self.unit = shards, unit
        self.piece_rows = 2 * unit + 16
        self.feed_rows = 2 * unit
        self.total = shards * unit
        self.head_rows, self.late_rows = 40, 16
        self.pieces = 2 * shards
        self.share = self.head_rows + self.late_rows
        self.head_total = 2 * self.pieces * self.head_rows
        self.late_total = 2 * self.pieces * self.late_rows


def sum_kernel(parts, source, out):
    size = out.shape[0]
    block = 16 if size % 16 == 0 else size

    def step(index, carry):
        rows = pl.ds(pl.multiple_of(index * block, block), block)
        total = source[0, rows, :].astype(f32)
        for part in range(1, parts):
            total = total + source[part, rows, :].astype(f32)
        out[rows, :] = total.astype(bf16)
        return carry

    lax.fori_loop(0, size // block, step, 0)


def pair_kernel(first, second, out):
    for part in range(out.shape[0]):
        total = first[part].astype(f32) + second[part].astype(f32)
        out[part] = total.astype(bf16)


def rows_kernel(shape, moves, first, second, arrived, first_out, second_out):
    def step(index, carry):
        rows = pl.ds(pl.multiple_of(index * 16, 16), 16)
        more = pl.ds(pl.multiple_of(index * 16 + shape.rows, 16), 16)
        first_out[rows, :] = (first[rows, :].astype(f32) + arrived[rows, :].astype(f32)).astype(bf16)
        second_out[rows, :] = (second[rows, :].astype(f32) + arrived[more, :].astype(f32)).astype(
            bf16
        )
        return carry

    lax.fori_loop(0, shape.rows // 16, step, 0)


def share_kernel(head_parts, late_parts, out):
    sums = []
    for parts in (head_parts, late_parts):
        total = parts[0].astype(f32)
        for part in range(1, parts.shape[0]):
            total = total + parts[part].astype(f32)
        sums.append(total)
    share = jnp.concatenate(sums).astype(bf16)
    for copy in range(out.shape[0]):
        out[copy] = share


def piece_kernel(units, copies, spots, first, second, far_bias, out, own, bias, semaphores):
    unit = units.unit
    width = first.shape[1]
    rows = pl.ds(pl.multiple_of(spots[0] * unit, 16), unit)
    moves = [
        pltpu.make_async_copy(source.at[rows, :], own.at[index], semaphores.at[index])
        for index, source in enumerate((first, second))
    ]
    moves.insert(0, pltpu.make_async_copy(far_bias, bias, semaphores.at[2]))
    for move in moves:
        move.start()
    moves.pop(0).wait()
    shard = spots[1]
    values = bias[...].astype(f32).reshape(1, bias.shape[0])
    values = jnp.concatenate([values, jnp.zeros((1, width - bias.shape[0]), f32)], axis=1)
    values = pltpu.roll(jnp.broadcast_to(values, (8, width)), spots[2], 1)
    lane = lax.broadcasted_iota(jnp.int32, (8, width), 1) - shard * unit
    row = lax.broadcasted_iota(jnp.int32, (8, width), 0)
    values = jnp.where((lane >= 0) & (lane < unit) & (row == 0), values, 0.0)
    line = jnp.concatenate([values, jnp.zeros((8, width), f32)]).astype(bf16)
    for move in moves:
        move.wait()
    for copy in range(copies):
        base = copy * units.piece_rows
        out[base : base + unit, :] = own[0]
        out[base + unit : base + 2 * unit, :] = own[1]
        out[base + 2 * unit : base + units.piece_rows, :] = line


def feed_kernel(shape, units, resumed, moves, weights, *refs):
    refs = list(refs)

    def take(count):
        taken = refs[:count]
        del refs[:count]
        return taken

    groups = 1 if resumed is None else 2
    closing = resumed is not False
    normed, cots = take(groups), take(groups)
    if resumed:
        old_grads, old_bias, *near = take(6)
    if resumed:
        out, d_out, both = take(3)
        outs = [out, both.at[shape.rows : 2 * shape.rows, :]]
        d_outs = [d_out, both.at[0 : shape.rows, :]]
        d_near, out_near = take(2)
    else:
        outs, d_outs = take(groups), take(groups)
    grads, bias_grad = take(2)
    first_weight, second_weight, total_grads, total_bias = take(4)
    unit, width = units.unit, shape.width
    bias = None
    for shard in range(units.shards):
        base, here = shard * units.piece_rows, shard * unit
        first_weight[here : here + unit, :] = weights[base : base + unit, :]
        second_weight[here : here + unit, :] = weights[base + unit : base + 2 * unit, :]
        term = weights[base + 2 * unit : base + units.piece_rows, :].astype(f32)
        bias = term if bias is None else bias + term
    bias = bias[0:1]
    if resumed:
        moves.arrive(*near)
        for target, own, arrived in ((d_near, near[0], near[1]), (out_near, near[2], near[3])):
            target[...] = own[...].astype(f32) + arrived[...].astype(f32)
            moves.leave(target)
    for group in range(groups):
        moves.arrive(normed[group], cots[group])
        rows, cot = normed[group], cots[group]
        value, rise = gelu_pair(nt(rows[...], first_weight[...]) + bias)
        hidden = value.astype(bf16)
        outs[group][...] = nn(hidden, second_weight[...]).astype(bf16)
        d_before = (nt(cot[...], second_weight[...]) * rise).astype(bf16)
        d_outs[group][...] = nn(d_before, first_weight[...]).astype(bf16)
        moves.leave(outs[group], d_outs[group])
        first, second = tn(d_before, rows[...]), tn(hidden, cot[...])
        line = fold(d_before.astype(f32))
        if group == 0 and not resumed:
            total_grads[0 : units.total, :] = first
            total_grads[units.total :, :] = second
            total_bias[...] = line
        elif group == 0:
            total_grads[0 : units.total, :] = old_grads[0 : units.total, :] + first
            total_grads[units.total :, :] = old_grads[units.total :, :] + second
            total_bias[...] = old_bias[...] + line
        else:
            total_grads[0 : units.total, :] += first
            total_grads[units.total :, :] += second
            total_bias[...] += line
    if not closing:
        grads[...] = total_grads[...]
        bias_grad[...] = total_bias[...]
        return
    bias_grad[...] = total_bias[...]
    for shard in range(units.shards):
        base, here = shard * units.feed_rows, shard * unit
        more = units.total + here
        grads[base : base + units.feed_rows, :] = jnp.concatenate(
            [total_grads[here : here + unit, :], total_grads[more : more + unit, :]]
        ).astype(bf16)


def heads_kernel(
    shape,
    units,
    moves,
    core,
    small,
    cot,
    middle,
    d_near,
    d_far,
    bias_grads,
    proj_weight,
    query,
    modulator,
    h_weight,
    normed,
    aggregated,
    mixed,
    *refs,
):
    later, refs = refs[:9], refs[9:]
    d_middle, d_query, d_aggregated, own_rest, other_rest, *refs = refs
    fetched, refs = refs[:9], refs[9:]
    heads_body(
        shape,
        units,
        moves,
        core,
        small,
        cot,
        middle,
        d_near,
        d_far,
        bias_grads,
        proj_weight,
        query,
        modulator,
        h_weight,
        normed,
        aggregated,
        mixed,
        list(zip(later, fetched)),
        d_middle,
        d_query,
        d_aggregated,
        own_rest,
        other_rest,
        *refs,
    )


def heads_body(
    shape,
    units,
    moves,
    core,
    small,
    cot,
    middle,
    d_near,
    d_far,
    bias_grads,
    proj_weight,
    query,
    modulator,
    h_weight,
    normed,
    aggregated,
    mixed,
    later,
    d_middle,
    d_query,
    d_aggregated,
    own_rest,
    other_rest,
    d_mixed,
    d_modulator,
    head,
    d_branch,
):
    width = shape.width
    zero = jnp.zeros((8, width), f32)
    moves.arrive(small, cot, middle, d_near)
    for source, target in later:
        moves.copy(source, target)
    gain = small[LN2_GAIN : LN2_GAIN + 1, :]

    def second_norm(rows, carry):
        grads = d_near[rows, :] + d_far[rows, :].astype(f32)
        cots = cot[rows, :].astype(f32)
        d_input, d_gain = norm_back(middle[rows, :], grads, gain)
        d_total = cots + d_input
        d_middle[rows, :] = d_total
        rounded = d_total.astype(bf16)
        d_branch[rows, :] = rounded
        added = (d_gain, grads, rounded.astype(f32), cots)
        return tuple(total + fold(item) for total, item in zip(carry, added))

    d_gain, d_bias, proj_bias, out_bias = blocks(shape, second_norm, (zero,) * 4)
    moves.leave(d_middle)
    moves.arrive(proj_weight)
    d_mixed[...] = nt(d_branch[...], proj_weight[...])
    moves.arrive(query, modulator)

    def split(rows, carry):
        values = d_mixed[rows, :]
        for_query = (values * modulator[rows, :]).astype(bf16)
        for_modulator = (values * query[rows, :]).astype(bf16)
        d_query[rows, :] = for_query
        d_modulator[rows, :] = for_modulator
        return carry[0] + fold(for_query.astype(f32)), carry[1] + fold(for_modulator.astype(f32))

    query_bias, h_bias = blocks(shape, split, (zero, zero))
    moves.leave(d_query)
    moves.arrive(h_weight)
    d_aggregated[...] = nt(d_modulator[...], h_weight[...])
    moves.leave(d_aggregated)
    moves.arrive(normed, aggregated, mixed)
    head[0:width, :] = tn(d_query[...], normed[...])
    head[width : 2 * width, :] = tn(aggregated[...], d_modulator[...])
    head[2 * width : 3 * width, :] = tn(mixed[...], d_branch[...])
    sums = (h_bias, proj_bias, d_gain, d_bias, out_bias, query_bias)
    head[3 * width :, :] = jnp.concatenate(
        [row_sum(item) for item in sums]
        + [jnp.zeros((2, width), f32)]
        + [row_sum(bias_grads[8 * index : 8 * index + 8, :]) for index in range(4)]
        + [jnp.zeros((units.head_total - 3 * width - 12, width), f32)]
    )
    for half, target in enumerate((own_rest, other_rest)):
        absolute = jnp.bitwise_xor(core[0], half)
        for piece in range(units.pieces):
            first = (absolute * units.pieces + piece) * units.head_rows
            target[piece] = head[pl.ds(pl.multiple_of(first, 8), units.head_rows), :].astype(bf16)


def levels_back_kernel(
    shape,
    moves,
    small,
    gates,
    d_aggregated,
    pooled,
    slope_three,
    slope_two,
    slope_one,
    one,
    two,
    three,
    d_one,
    d_two,
    d_three,
    rounded,
    d_gates,
    tap_ref,
    d_levels,
    products,
    d_context,
):
    width = shape.width
    inner = shape.inner
    moves.arrive(small)
    spread_taps(shape, small, tap_ref)
    for ref in (d_one, d_two, d_three):
        clear_edges(shape, ref)
    moves.arrive(gates, d_aggregated, pooled)
    pool_grad = [None] * sublanes
    for image in range(shape.images):
        rows = pl.ds(image * shape.segment, shape.segment)
        for tile in range(shape.tiles):
            slot = tile * shape.images + image
            values = d_aggregated[rows, columns(tile)]
            for level in range(3):
                d_levels[pl.ds(level * inner + slot, shape.patches, stride=sublanes), :] = (
                    values[: shape.patches] * gates[rows, columns(level)][: shape.patches]
                )
            pool_grad[slot] = jnp.sum(values * gates[rows, columns(3)], axis=0, keepdims=True)
    blank = jnp.zeros((1, lanes), f32)
    pool_grad = jnp.concatenate([blank if item is None else item for item in pool_grad])
    pool_grad = pool_grad * pooled[sublanes : 2 * sublanes, :]
    wide_pool = jnp.concatenate([pool_grad] * shape.side)

    def third(line, carry):
        here = pl.multiple_of(line * shape.line, shape.line)
        value = (d_levels[pl.ds(2 * inner + here, shape.line), :] + wide_pool) * slope_three[
            pl.ds(here, shape.line), :
        ]
        d_three[pl.ds(here + shape.centre, shape.line), :] = value
        return carry

    moves.arrive(slope_three)
    lax.fori_loop(0, shape.side, third, 0)
    moves.leave(d_three)
    moves.arrive(slope_two, slope_one)
    for level, source, target, slope in ((2, d_three, d_two, slope_two), (1, d_two, d_one, slope_one)):

        def back(line, carry, level=level, source=source, target=target, slope=slope):
            here = pl.multiple_of(line * shape.line, shape.line)
            value = correlate(shape, source, tap_ref, level, line, True)
            value = (value + d_levels[pl.ds((level - 1) * inner + here, shape.line), :]) * slope[
                pl.ds(here, shape.line), :
            ]
            target[pl.ds(here + shape.centre, shape.line), :] = value
            return carry

        lax.fori_loop(0, shape.side, back, 0)
        moves.leave(target)

    def back_context(line, carry):
        here = pl.multiple_of(line * shape.line, shape.line)
        d_levels[pl.ds(here, shape.line), :] = correlate(shape, d_one, tap_ref, 0, line, True)
        return carry

    lax.fori_loop(0, shape.side, back_context, 0)
    for image, tile, slot in shape.places():
        first = image * shape.segment
        d_context[first : first + shape.patches, columns(tile)] = d_levels[
            pl.ds(slot, shape.patches, stride=sublanes), :
        ]
        if tile == 0 and shape.segment > shape.patches:
            d_context[first + shape.patches : first + shape.segment, :] = jnp.zeros(
                (shape.segment - shape.patches, width), f32
            )
    rounded[...] = d_context[...].astype(bf16)
    moves.leave(rounded)
    moves.arrive(one, two, three)
    for image in range(shape.images):
        rows = pl.ds(image * shape.segment, shape.segment)
        totals = [None] * 4
        for tile in range(shape.tiles):
            slot = tile * shape.images + image
            values = d_aggregated[rows, columns(tile)]
            for level, ref in enumerate((one, two, three)):
                term = values * level_rows(shape, ref, image, slot)
                totals[level] = term if tile == 0 else totals[level] + term
            term = values * pooled[slot : slot + 1, :]
            totals[3] = term if tile == 0 else totals[3] + term
        for gate in range(4):
            products[rows, columns(gate)] = totals[gate]
    chooser = (
        lax.broadcasted_iota(jnp.int32, (4 * lanes, lanes), 0) // lanes
        == lax.broadcasted_iota(jnp.int32, (4 * lanes, lanes), 1)
    ).astype(f32).astype(bf16)
    d_gates[...] = nn(products[...].astype(bf16), chooser).astype(bf16)


def exit_kernel(
    shape,
    units,
    moves,
    core,
    two,
    d_three,
    one,
    d_two,
    context,
    d_one,
    rounded,
    d_gates,
    small,
    normed,
    f_turned,
    d_query,
    tokens,
    d_inputs,
    own_late,
    other_late,
    packed,
    tap_grad,
    inputs,
    d_context,
    gathered,
    gate_rows,
):
    width = shape.width
    moves.arrive(two, d_three)
    tap_grads(shape, two, d_three, 2, tap_grad)
    moves.arrive(one, d_two)
    tap_grads(shape, one, d_two, 1, tap_grad)
    moves.arrive(context, d_one)
    tap_grads(shape, context, d_one, 0, tap_grad)
    moves.arrive(rounded, d_gates, small, normed, f_turned, d_query, tokens)
    gathered[0:width, :] = tn(rounded[...], normed[...])
    gathered[width : width + 8, :] = tn(d_gates[...], normed[...])[0:8]
    for tile in range(shape.tiles):
        total = None
        for image in range(shape.images):
            slot = tile * shape.images + image
            term = tap_grad[pl.ds(slot, taps, stride=sublanes), :]
            total = term if total is None else total + term
        gathered[width + 8 : width + 8 + taps, columns(tile)] = total
    gate_rows[...] = jnp.concatenate(
        [
            f_turned[2 * width : 2 * width + 4, :].astype(f32),
            jnp.zeros((lanes - 4, width), f32),
        ]
    ).astype(bf16)
    d_normed = d_context
    gate_bias = row_sum(fold(d_gates[...].astype(f32)))
    context_bias = row_sum(fold(rounded[...].astype(f32)))
    d_normed[...] = (
        nn(d_query[...], f_turned[0:width, :])
        + nn(rounded[...], f_turned[width : 2 * width, :])
        + nn(d_gates[...], gate_rows[...])
    )
    packed[...] = tokens[...].astype(f32)
    unpack(shape, packed, inputs)
    gain = small[LN1_GAIN : LN1_GAIN + 1, :]
    zero = jnp.zeros((8, width), f32)

    def finish(rows, carry):
        values = d_normed[rows, :]
        d_input, d_gain = norm_back(inputs[rows, :], values, gain)
        d_inputs[rows, :] = d_input
        return carry[0] + fold(d_gain), carry[1] + fold(values)

    d_gain, d_bias = blocks(shape, finish, (zero, zero))
    moves.leave(d_inputs)
    last = width + 8 + taps
    rest = units.late_total - last - 4
    gathered[last:, :] = jnp.concatenate(
        [
            row_sum(d_gain),
            row_sum(d_bias),
            context_bias,
            jnp.concatenate([gate_bias, jnp.zeros((1, width - lanes), f32)], axis=1),
            jnp.zeros((rest, width), f32),
        ]
    )
    for half, target in enumerate((own_late, other_late)):
        absolute = jnp.bitwise_xor(core[0], half)
        for place in range(2):
            for spot in range(units.shards):
                first = ((place * 2 + absolute) * units.shards + spot) * units.late_rows
                target[place * units.shards + spot] = gathered[
                    pl.ds(pl.multiple_of(first, 16), units.late_rows), :
                ].astype(bf16)


def finish_kernel(
    shape,
    moves,
    d_middle,
    d_inputs,
    small,
    middle,
    out_near,
    out_far,
    tokens_grad,
    block_out,
    rows_ref,
):
    moves.arrive(d_middle, d_inputs)

    def add_grads(rows, carry):
        rows_ref[rows, :] = d_middle[rows, :] + d_inputs[rows, :]
        return carry

    blocks(shape, add_grads, 0)
    pack(shape, rows_ref, tokens_grad)
    moves.leave(tokens_grad)
    moves.arrive(small, middle, out_near, out_far)

    def add_outs(rows, carry):
        total = middle[rows, :] + small[FC2_BIAS : FC2_BIAS + 1, :]
        rows_ref[rows, :] = total + out_near[rows, :] + out_far[rows, :].astype(f32)
        return carry

    blocks(shape, add_outs, 0)
    pack(shape, rows_ref, block_out)


def unpack_kernel(
    shape,
    units,
    spots,
    piece,
    piece_x,
    piece_core,
    piece_both,
    own,
    own_b,
    own_x,
    own_both,
    core_own,
    core_b,
    core_x,
    core_both,
    ln1_gain,
    ln1_bias,
    f_grad,
    f_bias,
    small_grad,
    middle_grad,
    large_grad,
    h_grad,
    h_bias,
    proj_grad,
    proj_bias,
    ln2_gain,
    ln2_bias,
    first_grad,
    first_bias,
    second_grad,
    second_bias,
    held,
    head,
    late,
):
    width = shape.width
    unit = units.unit
    size = own.shape[0]
    parts = (own, own_b, own_x, own_both, core_own, core_b, core_x, core_both)
    for index, part in enumerate(parts):
        held[index * size : (index + 1) * size, :] = part[...].astype(f32)
    core, shift = spots[0], spots[2]
    far = units.shards // 2
    for half in range(2):
        for place in range(2):
            for close in range(2):
                slot = jnp.bitwise_xor(core, half) * 4 + jnp.bitwise_xor(spots[3], place) * 2
                base = (slot + jnp.bitwise_xor(spots[4], close)) * size
                for away in range(far):
                    here = base + away * units.share
                    to = ((half * 2 + place) * far + away) * 2 + close
                    head[to * units.head_rows : (to + 1) * units.head_rows, :] = held[
                        pl.ds(pl.multiple_of(here, 8), units.head_rows), :
                    ]
                    to = ((place * 2 + half) * far + away) * 2 + close
                    late[to * units.late_rows : (to + 1) * units.late_rows, :] = held[
                        pl.ds(pl.multiple_of(here + units.head_rows, 8), units.late_rows), :
                    ]
    total = None
    lane = lax.broadcasted_iota(jnp.int32, (8, width), 1)
    for index, source in enumerate((piece, piece_core, piece_x, piece_both)):
        quarter = jnp.bitwise_xor(spots[1], index)
        to = pl.ds(pl.multiple_of(quarter * unit, 8), unit)
        first_grad[to, :] = source[0:unit, :].astype(f32)
        second_grad[to, :] = source[unit : 2 * unit, :].astype(f32)
    for quarter in range(4):
        row = head[3 * width + 8 + quarter : 3 * width + 9 + quarter, :]
        moved = shift + quarter * unit
        moved = jnp.where(moved >= width, moved - width, moved)
        row = pltpu.roll(jnp.broadcast_to(row, (8, width)), moved, 1)
        row = jnp.where((lane >= quarter * unit) & (lane < (quarter + 1) * unit), row, 0.0)
        total = row if total is None else total + row
    first_bias[...] = total[0:1, 0 : first_bias.shape[0]].reshape(first_bias.shape)
    f_grad[0:width, :] = head[0:width, :]
    f_grad[width : 2 * width + 4, :] = late[0 : width + 4, :]
    h_grad[...] = head[width : 2 * width, :]
    proj_grad[...] = head[2 * width : 3 * width, :]
    first = width + 8
    small_grad[...] = late[first : first + 9, :]
    middle_grad[...] = late[first + 9 : first + 34, :]
    large_grad[...] = late[first + 34 : first + taps, :]
    first = first + taps
    for out, source, row in (
        (h_bias, head, 3 * width),
        (proj_bias, head, 3 * width + 1),
        (ln2_gain, head, 3 * width + 2),
        (ln2_bias, head, 3 * width + 3),
        (second_bias, head, 3 * width + 4),
        (ln1_gain, late, first),
        (ln1_bias, late, first + 1),
    ):
        out[...] = source[row : row + 1, :].reshape(width)
    f_bias[0:width] = head[3 * width + 5 : 3 * width + 6, :].reshape(width)
    f_bias[width : 2 * width] = late[first + 2 : first + 3, :].reshape(width)
    f_bias[2 * width : 2 * width + 4] = late[first + 3 : first + 4, 0:4].reshape(4)


def call(kernel, name, outs, scratch, micros, room, *operands):
    spec = pl.BlockSpec(memory_space=pltpu.VMEM)
    outer = pl.BlockSpec(memory_space=pltpu.HBM)
    far_in = [isinstance(item, Far) for item in operands]
    far_out = [isinstance(item, Far) for item in outs]
    anywhere = [isinstance(item, Anywhere) for item in operands]
    raw = [isinstance(item, Raw) for item in operands]
    operands = [item.value if far else item for item, far in zip(operands, far_in)]
    operands = [
        pltpu.with_memory_space_constraint(item, pltpu.HBM) if far and not free else item
        for item, far, free in zip(operands, far_in, anywhere)
    ]
    raw_out = [isinstance(item, Raw) for item in outs]
    outs = [
        pltpu.HBM(item.value.shape, item.value.dtype) if far else item
        for item, far in zip(outs, far_out)
    ]
    specs = []
    for item, far, free in zip(operands, far_in, anywhere):
        if free:
            specs.append(pl.BlockSpec(memory_space=pl.ANY))
        elif item.dtype == jnp.int32:
            specs.append(pl.BlockSpec(memory_space=pltpu.SMEM))
        else:
            specs.append(outer if far else spec)
    out_specs = [outer if far else spec for far in far_out]
    if name not in plain:
        far_in = [far and not own for far, own in zip(far_in, raw)]
        far_out = [far and not own for far, own in zip(far_out, raw_out)]
        pairs = list(zip(operands, far_in)) + list(zip(outs, far_out))
        buffers = [pltpu.VMEM(item.shape, item.dtype) for item, far in pairs if far]
        extra = sum(raw) + sum(raw_out)
        semaphores = pltpu.SemaphoreType.DMA((max(len(buffers) + extra, 1),))
        scratch = list(scratch) + buffers + [semaphores]
        kernel = with_moves(kernel, far_in, far_out, extra)
    moved = sum(item.size * item.dtype.itemsize for item in operands)
    return pl.pallas_call(
        kernel,
        name=name,
        out_shape=outs,
        in_specs=specs,
        out_specs=out_specs,
        scratch_shapes=scratch,
        compiler_params=pltpu.CompilerParams(vmem_limit_bytes=room * 1024 * 1024),
        cost_estimate=pl.CostEstimate(
            flops=int(micros * 1.1e9), bytes_accessed=moved, transcendentals=0
        ),
    )(*operands)


plain = ("piece", "sum", "pair", "share", "unpack")


class Far:
    def __init__(self, value):
        self.value = value


class Anywhere(Far):
    pass


class Raw(Far):
    pass


def far_array(*dims, kind=jnp.float32):
    return Far(array(*dims, kind=kind))


def array(*dims, kind=jnp.float32):
    return jax.ShapeDtypeStruct(dims, kind)


def to_packed(values, shape):
    moved = with_layout_constraint(values.transpose(1, 2, 0, 3), Layout((0, 1, 2, 3)))
    moved = moved.reshape(shape.patches, shape.images, shape.tiles, lanes)
    moved = with_layout_constraint(moved, Layout((0, 2, 1, 3)))
    return moved.transpose(0, 2, 1, 3).reshape(shape.packed, lanes)


def from_packed(values, shape):
    moved = values.reshape(shape.patches, shape.tiles, shape.images, lanes).transpose(0, 2, 1, 3)
    moved = moved.reshape(shape.side, shape.side, shape.images, shape.width)
    return moved.transpose(2, 0, 1, 3)


everyone = ("x", "core", "a", "b")


def gather_plainly(units, first, bias, second):
    first = lax.all_gather(first, ("a", "b"), axis=0, tiled=True)
    second = lax.all_gather(second, ("a", "b"), axis=0, tiled=True)
    bias = lax.all_gather(bias, ("a", "b"), axis=0, tiled=True)
    width = first.shape[1]
    rows = jnp.pad(bias.reshape(4, 1, 1, width), ((0, 0), (0, units.shards - 1), (0, 15), (0, 0)))
    shape = (4, units.shards, units.unit, width)
    both = jnp.concatenate([first.reshape(shape), second.reshape(shape), rows], axis=2)
    both = both.reshape(4, units.shards * units.piece_rows, width)
    return [both[index] for index in range(4)]


def total_of(values, parts):
    rows = values.shape[0] // parts
    kernel = functools.partial(sum_kernel, parts)
    values = values.reshape(parts, rows, values.shape[1])
    return call(kernel, "sum", [array(rows, values.shape[2], kind=bf16)], [], 1, 4, values)[0]


def reduce_plainly(shape, units, feed, rest, late):
    width = shape.width
    unit = units.unit
    both = jnp.stack(feed).reshape(4, units.shards, units.feed_rows, width)
    first = both[:, :, :unit].reshape(4 * units.total, width)
    second = both[:, :, unit:].reshape(4 * units.total, width)

    def shared(values):
        part = lax.psum_scatter(values, ("a", "b"), scatter_dimension=0, tiled=True)
        return lax.psum(part, ("x", "core")).astype(f32)

    late = jnp.stack(late).reshape(2, 2, units.shards, units.late_rows, width)
    late = late.transpose(1, 0, 2, 3, 4).reshape(units.late_total, width)
    late = lax.psum(late, everyone).astype(f32)
    head = jnp.concatenate(rest).reshape(units.head_total, width)
    head = lax.psum(head, everyone).astype(f32)
    bias = head[3 * width + 8 : 3 * width + 12].reshape(-1)
    place = lax.axis_index("a") * 2 + lax.axis_index("b")
    size = bias.shape[0] // (lax.axis_size("a") * 2)
    bias = lax.dynamic_slice_in_dim(bias, place * size, size, 0)
    last = width + 8
    vectors = head[3 * width : 3 * width + 8]
    more = late[last + taps : last + taps + 4]
    return (
        more[0],
        more[1],
        jnp.concatenate([head[:width], late[: width + 4]]),
        jnp.concatenate([vectors[5], more[2], more[3, :4]]),
        late[last : last + 9],
        late[last + 9 : last + 34],
        late[last + 34 : last + taps],
        head[width : 2 * width],
        vectors[0],
        head[2 * width : 3 * width],
        vectors[1],
        vectors[2],
        vectors[3],
        shared(first),
        bias,
        shared(second),
        vectors[4],
    )


def shards(
    sizes,
    tokens,
    ln1_gain,
    ln1_bias,
    f_weight,
    f_bias,
    dw_small,
    dw_middle,
    dw_large,
    h_weight,
    h_bias,
    proj_weight,
    proj_bias,
    ln2_gain,
    ln2_bias,
    fc1_weight,
    fc1_bias,
    fc2_weight,
    fc2_bias,
    out_grad,
):
    images, side, _, width = tokens.shape
    shape = Shape(images, side, width)
    rows, grid, inner = shape.rows, shape.grid, shape.inner
    hidden = fc1_weight.shape[1] * sizes["a"] * sizes["b"]
    quick = sizes["x"] == 2 and sizes["a"] * sizes["b"] == 8
    units = Units(8, hidden // 32)
    f_turned = f_weight.T
    first, second = fc1_weight.T, fc2_weight
    scratch = pltpu.VMEM
    core = jnp.zeros((1,), jnp.int32)
    if quick:
        core = lax.axis_index("core").astype(jnp.int32).reshape(1)
        quarter = lax.axis_index("x") * 2 + core[0]
        shard = lax.axis_index("a") * 2 + lax.axis_index("b")
        turn = lax.rem(shard - quarter + units.shards, units.shards) * units.unit
        spots = jnp.stack([quarter, shard, turn]).astype(jnp.int32)
        (pieces,) = call(
            functools.partial(piece_kernel, units, units.shards),
            "piece",
            [array(units.shards * units.piece_rows, width, kind=bf16)],
            [
                scratch((2, units.unit, width), bf16),
                scratch(fc1_bias.shape, bf16),
                pltpu.SemaphoreType.DMA((3,)),
            ],
            1,
            6,
            spots,
            Far(first),
            Far(second),
            Far(fc1_bias),
        )
        weights = exchange(pieces, ("a", "b"))
    tokens_packed = to_packed(tokens, shape)

    def rows_array(kind=bf16):
        return far_array(rows, width, kind=kind)

    small, cot, inputs, normed, query, gates, context, one, slope_one = call(
        functools.partial(entry_kernel, shape),
        "entry",
        [
            far_array(96, width),
            rows_array(),
            array(rows, width),
            rows_array(),
            array(rows, width),
            array(rows, 4 * lanes),
            far_array(grid, lanes),
            array(grid, lanes),
            array(inner, lanes),
        ],
        [
            scratch((taps * sublanes, lanes), f32),
            scratch((shape.packed, lanes), f32),
            scratch((rows, width), f32),
        ],
        5,
        16,
        tokens_packed,
        f_turned,
        to_packed(out_grad, shape),
        dw_small,
        dw_middle,
        dw_large,
        ln1_gain,
        ln1_bias,
        f_bias,
        h_bias,
        proj_bias,
        ln2_gain,
        ln2_bias,
        fc2_bias,
    )
    if quick:
        cot_far = flip(cot, "x")
        cot_core = flip(cot)
    one, gates, query, slope_one, *results = call(
        functools.partial(modulation_kernel, shape),
        "modulation",
        [
            Raw(array(grid, lanes)),
            Raw(array(rows, 4 * lanes)),
            Raw(array(rows, width)),
            Raw(array(inner, lanes)),
            rows_array(f32),
            rows_array(),
            rows_array(),
            rows_array(f32),
            rows_array(),
            far_array(grid, lanes),
            far_array(grid, lanes),
            far_array(inner, lanes),
            far_array(inner, lanes),
            far_array(2 * sublanes, lanes),
        ],
        [scratch((rows, width), f32), scratch((taps * sublanes, lanes), f32)],
        8,
        20,
        one,
        Far(small),
        gates,
        Far(h_weight),
        query,
        inputs,
        Far(proj_weight),
        slope_one,
    )
    modulator, aggregated, mixed, middle, normed_two, *results = results
    two, three, slope_two, slope_three, pooled = results

    def feed(resumed, outs, *operands):
        return call(
            functools.partial(feed_kernel, shape, units, resumed),
            "feed",
            outs,
            [
                scratch((units.total, width), bf16),
                scratch((units.total, width), bf16),
                scratch((2 * units.total, width), f32),
                scratch((8, width), f32),
            ],
            6,
            24,
            *operands,
        )

    near_rows = array(rows, width, kind=bf16)
    feed_total = array(units.shards * units.feed_rows, width, kind=bf16)
    bias_total = array(8, width)
    if quick:
        cot_both = flip(after(cot_far, middle))
        normed_far = flip(normed_two, "x")
        normed_core = flip(normed_two)
        out_own, out_core, d_own, d_core, *carry = feed(
            False,
            [near_rows] * 4 + [array(2 * units.total, width), bias_total],
            weights,
            Far(normed_two),
            normed_core,
            Far(cot),
            cot_core,
        )
        out_core, d_core = flip(out_core), flip(d_core)
        normed_far = after(normed_far, d_own)
        normed_both = flip(normed_far)
        out_far, d_far, both, d_near, out_near, feed_grads, bias_grad = feed(
            True,
            [near_rows] * 2
            + [array(2 * rows, width, kind=bf16), rows_array(f32), rows_array(f32), feed_total]
            + [bias_total],
            weights,
            normed_far,
            normed_both,
            cot_far,
            cot_both,
            *carry,
            d_own,
            d_core,
            out_own,
            out_core,
        )
        arrived = flip(both)
        d_far, out_far = call(
            functools.partial(rows_kernel, shape),
            "rows",
            [near_rows, rows_array()],
            [],
            1,
            8,
            d_far,
            out_far,
            arrived,
        )
        feed_grads = after(feed_grads, d_far)
        d_far = flip(d_far, "x")
        feed_parts = exchange(feed_grads, ("a", "b"))
        mine = (jnp.arange(4) == quarter).astype(f32)
        bias_grads = (mine[:, None, None] * bias_grad).reshape(32, width)
    else:
        out_far = d_far = jnp.zeros((rows, width), bf16)
        out_near, d_near, feed_grads, bias_grads = jnp.zeros((rows, width), f32), 0.0, [], []
        for weights in gather_plainly(units, first, fc1_bias, second):
            out, d_out, grads, bias_grad = feed(
                None, [near_rows, near_rows, feed_total, bias_total], weights, normed_two, cot
            )
            bias_grads.append(bias_grad)
            out_near, d_near = out_near + out.astype(f32), d_near + d_out.astype(f32)
            feed_grads.append(grads)
        bias_grads = jnp.concatenate(bias_grads)
    rest = array(units.pieces, units.head_rows, width, kind=bf16)
    later = [small, gates, pooled, slope_three, slope_two, slope_one, one, two, three]
    d_middle, d_query, d_aggregated, own_rest, other_rest, *fetched = call(
        functools.partial(heads_kernel, shape, units),
        "heads",
        [rows_array(f32), rows_array(), array(rows, width), rest, rest]
        + [array(*item.shape) for item in later],
        [
            scratch((rows, width), f32),
            scratch((rows, width), bf16),
            scratch((units.head_total, width), f32),
            scratch((rows, width), bf16),
        ],
        5,
        16,
        core,
        Far(small),
        Far(cot),
        Far(middle),
        Far(d_near),
        d_far,
        bias_grads,
        Far(proj_weight),
        Far(query),
        Far(modulator),
        Far(h_weight),
        Far(normed),
        Far(aggregated),
        Far(mixed),
        *[Raw(item) for item in later],
    )
    if quick:
        out_far = flip(after(out_far, d_middle), "x")
        rest_arrived = flip(other_rest)
    d_one, d_two, d_three, rounded, d_gates = call(
        functools.partial(levels_back_kernel, shape),
        "levels_back",
        [
            far_array(grid, lanes),
            far_array(grid, lanes),
            far_array(grid, lanes),
            rows_array(),
            far_array(rows, lanes, kind=bf16),
        ],
        [
            scratch((taps * sublanes, lanes), f32),
            scratch((3 * inner, lanes), f32),
            scratch((rows, 4 * lanes), f32),
            scratch((rows, width), f32),
        ],
        8,
        24,
        fetched[0],
        fetched[1],
        d_aggregated,
        *fetched[2:],
    )
    if quick:
        (rest_half,) = call(pair_kernel, "pair", [rest], [], 1, 4, own_rest, rest_arrived)
        feed_parts = after(feed_parts, d_one)
        piece = total_of(feed_parts, units.shards)
        rest_half = after(rest_half, piece)
        d_one = after(d_one, rest_half, out_far)
        shares = rest_half.shape
        rest_parts = exchange(rest_half.reshape(-1, width), ("x", "a", "b")).reshape(shares)
    late = array(units.pieces, units.late_rows, width, kind=bf16)
    d_inputs, own_late, other_late = call(
        functools.partial(exit_kernel, shape, units),
        "exit",
        [array(rows, width), late, late],
        [
            scratch((shape.packed, lanes), f32),
            scratch((taps * sublanes, lanes), f32),
            scratch((rows, width), f32),
            scratch((rows, width), f32),
            scratch((units.late_total, width), f32),
            scratch((lanes, width), bf16),
        ],
        9,
        24,
        core,
        Far(two),
        Far(d_three),
        Far(one),
        Far(d_two),
        Far(context),
        Far(d_one),
        Far(rounded),
        Far(d_gates),
        Far(small),
        Far(normed),
        Far(f_turned),
        Far(d_query),
        Far(tokens_packed),
    )
    if quick:
        late_arrived = flip(other_late)
    tokens_grad, block_out = call(
        functools.partial(finish_kernel, shape),
        "finish",
        [far_array(shape.packed, lanes), far_array(shape.packed, lanes)],
        [scratch((rows, width), f32)],
        3,
        16,
        Far(d_middle),
        d_inputs,
        Far(small),
        Far(middle),
        Far(out_near),
        Anywhere(out_far),
    )
    if quick:
        rest_parts = after(rest_parts, tokens_grad)
        (late_half,) = call(pair_kernel, "pair", [late], [], 1, 4, own_late, late_arrived)
        late_half, rest_parts = lax.optimization_barrier((late_half, rest_parts))
        shares = late_half.shape
        late_parts = exchange(late_half.reshape(-1, width), ("x", "a", "b")).reshape(shares)
        piece = after(piece, late_half)
        piece_x = flip(piece, "x")
        piece_core, piece_both = flip(piece), flip(piece_x)
        (share,) = call(
            share_kernel,
            "share",
            [array(sizes["a"], units.share, width, kind=bf16)],
            [],
            1,
            6,
            rest_parts,
            late_parts,
        )
        share = after(share, piece_core, piece_both)
        own = exchange(share.reshape(-1, width), "a")
        held_b, held_x = flip(own, "b"), flip(own, "x")
        held_both = flip(held_b, "x")
        held = [own, held_b, held_x, held_both]
        held = held + [flip(item) for item in held]
        turn = lax.rem(units.shards - shard, units.shards) * units.unit
        spots = [core[0], quarter, turn] + [lax.axis_index(axis) for axis in ("x", "b")]
        spots = jnp.stack(spots).astype(jnp.int32)
        total = 4 * units.unit
        others = call(
            functools.partial(unpack_kernel, shape, units),
            "unpack",
            [
                array(width),
                array(width),
                array(2 * width + 4, width),
                array(2 * width + 4),
                array(9, width),
                array(25, width),
                array(49, width),
                array(width, width),
                array(width),
                array(width, width),
                array(width),
                array(width),
                array(width),
                array(total, width),
                array(total),
                array(total, width),
                array(width),
            ],
            [
                scratch((2 * units.pieces * units.share, width), f32),
                scratch((units.head_total, width), f32),
                scratch((units.late_total, width), f32),
            ],
            2,
            16,
            spots,
            piece,
            piece_x,
            piece_core,
            piece_both,
            *held,
        )
    else:
        others = reduce_plainly(
            shape, units, feed_grads, (own_rest, other_rest), (own_late, other_late)
        )
    others = list(others)
    others[2] = others[2].T
    others[13] = others[13].T
    return from_packed(block_out, shape), from_packed(tokens_grad, shape), *others


def solution(mesh):
    img, mlp = mesh.shape["img"], mesh.shape["mlp"]
    sizes = {"x": img // 2, "core": 2, "a": mlp // 2, "b": 2}
    finer = Mesh(mesh.devices.reshape(*sizes.values()), everyone)
    images = P(everyone, None, None, None)
    hidden = ("a", "b")
    return jax.shard_map(
        functools.partial(shards, sizes),
        mesh=finer,
        in_specs=(images,)
        + (P(),) * 13
        + (P(None, hidden), P(hidden), P(hidden, None), P(), images),
        out_specs=(images, images)
        + (P(),) * 13
        + (P(None, hidden), P(hidden), P(hidden, None), P()),
        check_vma=False,
    )
```

```python
import functools
import math

import jax
import jax.numpy as jnp
from jax import lax
from jax.experimental import pallas as pl
from jax.experimental.pallas import tpu as pltpu
from jax.experimental.layout import Layout, with_layout_constraint
from jax.sharding import Mesh
from jax.sharding import PartitionSpec as P

epsilon = 1e-05
lanes = 128
sublanes = 8
edge = 3
extents = (3, 5, 7)
starts = (0, 9, 34)
taps = 83
LN1_GAIN, LN1_BIAS, QUERY_BIAS, CONTEXT_BIAS, GATE_BIAS = 83, 84, 85, 86, 87
H_BIAS, PROJ_BIAS, LN2_GAIN, LN2_BIAS, FC2_BIAS = 88, 89, 90, 91, 92
erfc_terms = (0.254829592, -0.284496736, 1.421413741, -1.453152027, 1.061405429)
f32 = jnp.float32
bf16 = jnp.bfloat16


def flip(values, axis="core", size=2, bit=1):
    return lax.ppermute(values, axis, [(place, place ^ bit) for place in range(size)])


def exchange(values, axes):
    return lax.all_to_all(values, axes, split_axis=0, concat_axis=0, tiled=True)


def after(values, *others):
    return lax.optimization_barrier((values,) + others)[0]


def nn(left, right):
    return jnp.dot(left, right, preferred_element_type=f32)


def nt(left, right):
    return lax.dot_general(left, right, (((1,), (1,)), ((), ())), preferred_element_type=f32)


def tn(left, right):
    return lax.dot_general(left, right, (((0,), (0,)), ((), ())), preferred_element_type=f32)


def gelu_pair(values):
    step = 1.0 / (1.0 + jnp.abs(values) * (0.3275911 * math.sqrt(0.5)))
    power = jnp.exp(values * values * -0.5)
    tail = jnp.full_like(values, 0.5 * erfc_terms[-1])
    for term in erfc_terms[-2::-1]:
        tail = tail * step + 0.5 * term
    tail = tail * step * power
    below = jnp.where(values >= 0.0, 1.0 - tail, tail)
    return values * below, below + values * power * (1.0 / math.sqrt(2.0 * math.pi))


class Shape:
    def __init__(self, images, side, width):
        self.images, self.side, self.width = images, side, width
        self.tiles = width // lanes
        self.slots = images * self.tiles
        self.patches = side * side
        self.segment = -(-self.patches // 8) * 8
        self.rows = images * self.segment
        self.line = side * sublanes
        self.centre = edge * self.line
        self.grid = (side + 2 * edge) * self.line
        self.inner = side * self.line
        self.packed = self.patches * self.slots
        self.block = next(size for size in (80, 40, 16, 8) if self.rows % size == 0)

    def places(self):
        return [
            (image, tile, tile * self.images + image)
            for image in range(self.images)
            for tile in range(self.tiles)
        ]


def columns(tile):
    return slice(tile * lanes, (tile + 1) * lanes)


def unpack(shape, packed, rows):
    for image, tile, slot in shape.places():
        first = image * shape.segment
        rows[first : first + shape.patches, columns(tile)] = packed[
            pl.ds(slot, shape.patches, stride=shape.slots), :
        ]
    for image in range(shape.images):
        first = image * shape.segment
        spare = shape.segment - shape.patches
        if spare:
            rows[first + shape.patches : first + shape.segment, 0 : shape.width] = jnp.zeros(
                (spare, shape.width), f32
            )


def pack(shape, rows, packed):
    for image, tile, slot in shape.places():
        first = image * shape.segment
        packed[pl.ds(slot, shape.patches, stride=shape.slots), :] = rows[
            first : first + shape.patches, columns(tile)
        ]


def blocks(shape, body, init=None):
    def step(index, carry):
        first = pl.multiple_of(index * shape.block, shape.block)
        return body(pl.ds(first, shape.block), carry)

    return lax.fori_loop(0, shape.rows // shape.block, step, init)


def normalise(values):
    average = jnp.mean(values, axis=-1, keepdims=True)
    centred = values - average
    variance = jnp.mean(centred * centred, axis=-1, keepdims=True)
    scale = lax.rsqrt(variance + epsilon)
    return centred * scale, scale


def norm_back(values, grad, gain):
    unit, scale = normalise(values)
    inner = grad * gain
    first = jnp.mean(inner, axis=-1, keepdims=True)
    second = jnp.mean(inner * unit, axis=-1, keepdims=True)
    return scale * (inner - first - unit * second), grad * unit


def fold(values):
    return jnp.sum(values.reshape(values.shape[0] // 8, 8, values.shape[1]), axis=0)


def row_sum(values):
    return jnp.sum(values, axis=0, keepdims=True)


def spread_taps(shape, small, tap_ref):
    tap_ref[...] = jnp.zeros_like(tap_ref)
    for _, tile, slot in shape.places():
        tap_ref[pl.ds(slot, taps, stride=sublanes), :] = small[0:taps, columns(tile)]


def line_at(shape, ref, line):
    first = pl.multiple_of(line * shape.line, shape.line)
    values = ref[pl.ds(first, shape.line), :]
    return [values[w * sublanes : (w + 1) * sublanes] for w in range(shape.side)]


def correlate(shape, source, tap_ref, level, line, turned):
    extent = extents[level]
    reach = extent // 2
    totals = [None] * shape.side
    for down in range(extent):
        values = line_at(shape, source, line + down + edge - reach)
        for along in range(extent):
            entry = down * extent + along
            if turned:
                entry = extent * extent - 1 - entry
            tap = tap_ref[pl.ds((starts[level] + entry) * sublanes, sublanes), :]
            for w in range(shape.side):
                other = w + along - reach
                if 0 <= other < shape.side:
                    term = values[other] * tap
                    totals[w] = term if totals[w] is None else totals[w] + term
    return jnp.concatenate(totals, axis=0)


def tap_grads(shape, source, grad, level, out):
    extent = extents[level]
    reach = extent // 2
    for down in range(extent):

        def step(line, totals, down=down):
            values = line_at(shape, source, line + down + edge - reach)
            grads = line_at(shape, grad, line + edge)
            result = []
            for along in range(extent):
                total = totals[along]
                for w in range(shape.side):
                    other = w + along - reach
                    if 0 <= other < shape.side:
                        total = total + values[other] * grads[w]
                result.append(total)
            return tuple(result)

        zero = jnp.zeros((sublanes, lanes), f32)
        first, last = max(0, reach - down), min(shape.side, shape.side + reach - down)
        totals = lax.fori_loop(first, last, step, (zero,) * extent)
        for along in range(extent):
            out[pl.ds((starts[level] + down * extent + along) * sublanes, sublanes), :] = totals[
                along
            ]


def clear_edges(shape, ref):
    zeros = jnp.zeros((shape.centre, lanes), f32)
    ref[0 : shape.centre, :] = zeros
    ref[shape.centre + shape.inner : shape.grid, :] = zeros


def gate_values(shape, normed, f_turned, small, gates):
    weight = f_turned[2 * shape.width : 2 * shape.width + 4, :].astype(f32)
    wide = jnp.concatenate(
        [jnp.broadcast_to(weight[g : g + 1], (lanes, shape.width)) for g in range(4)]
    ).astype(bf16)
    bias = small[GATE_BIAS : GATE_BIAS + 1, :]
    wide_bias = jnp.concatenate(
        [jnp.broadcast_to(bias[:, g : g + 1], (1, lanes)) for g in range(4)], axis=1
    )
    gates[...] = nt(normed[...], wide) + wide_bias


def level_rows(shape, level, image, slot):
    return level[pl.ds(shape.centre + slot, shape.segment, stride=sublanes), :]


def run_levels(shape, moves, chain, tap_ref):
    total = jnp.zeros((sublanes, lanes), f32)
    for level, source, target, slope in chain:
        clear_edges(shape, target)

        def line_step(line, total, level=level, source=source, target=target, slope=slope):
            before = correlate(shape, source, tap_ref, level, line, False)
            value, rise = gelu_pair(before)
            here = pl.multiple_of((line + edge) * shape.line, shape.line)
            target[pl.ds(here, shape.line), :] = value
            slope[pl.ds(pl.multiple_of(line * shape.line, shape.line), shape.line), :] = rise
            if level == 2:
                total = total + fold(value)
            return total

        total = lax.fori_loop(0, shape.side, line_step, total)
        moves.leave(target, slope)
    return total


def entry_kernel(
    shape,
    moves,
    tokens,
    f_turned,
    out_grad,
    dw_small,
    dw_middle,
    dw_large,
    ln1_gain,
    ln1_bias,
    f_bias,
    h_bias,
    proj_bias,
    ln2_gain,
    ln2_bias,
    fc2_bias,
    small,
    cot,
    inputs,
    normed,
    query,
    gates,
    context,
    one,
    slope_one,
    tap_ref,
    packed,
    wide,
):
    width = shape.width
    for source, first in zip((dw_small, dw_middle, dw_large), starts):
        small[first : first + source.shape[0], :] = source[...].astype(f32)
    shared = f_bias[...].astype(f32).reshape(1, 2 * width + 4)
    vectors = {
        QUERY_BIAS: shared[:, 0:width],
        CONTEXT_BIAS: shared[:, width : 2 * width],
        GATE_BIAS: jnp.concatenate(
            [shared[:, 2 * width :], jnp.zeros((1, width - 4), f32)], axis=1
        ),
    }
    for row, source in (
        (LN1_GAIN, ln1_gain),
        (LN1_BIAS, ln1_bias),
        (H_BIAS, h_bias),
        (PROJ_BIAS, proj_bias),
        (LN2_GAIN, ln2_gain),
        (LN2_BIAS, ln2_bias),
        (FC2_BIAS, fc2_bias),
    ):
        vectors[row] = source[...].astype(f32).reshape(1, width)
    for row, value in vectors.items():
        small[row : row + 1, :] = value
    last = FC2_BIAS + 1
    small[last:, :] = jnp.zeros((small.shape[0] - last, width), f32)
    moves.leave(small)
    moves.arrive(tokens)
    packed[...] = tokens[...].astype(f32)
    unpack(shape, packed, inputs)
    moves.leave(inputs)
    spread_taps(shape, small, tap_ref)
    gain = small[LN1_GAIN : LN1_GAIN + 1, :]
    bias = small[LN1_BIAS : LN1_BIAS + 1, :]

    def first_norm(rows, carry):
        unit, _ = normalise(inputs[rows, :])
        normed[rows, :] = (unit * gain + bias).astype(bf16)
        return carry

    blocks(shape, first_norm, 0)
    moves.leave(normed)
    moves.arrive(out_grad)
    packed[...] = out_grad[...].astype(f32)
    unpack(shape, packed, wide)
    cot[...] = wide[...].astype(bf16)
    moves.leave(cot)
    moves.arrive(f_turned)
    wide[...] = (
        nt(normed[...], f_turned[width : 2 * width, :]) + small[CONTEXT_BIAS : CONTEXT_BIAS + 1, :]
    )
    context[...] = jnp.zeros_like(context)
    for image, tile, slot in shape.places():
        first = image * shape.segment
        context[pl.ds(shape.centre + slot, shape.patches, stride=sublanes), :] = wide[
            first : first + shape.patches, columns(tile)
        ]
    moves.leave(context)
    query[...] = nt(normed[...], f_turned[0:width, :]) + small[QUERY_BIAS : QUERY_BIAS + 1, :]
    moves.leave(query)
    gate_values(shape, normed, f_turned, small, gates)
    moves.leave(gates)
    run_levels(shape, moves, ((0, context, one, slope_one),), tap_ref)


def modulation_kernel(
    shape,
    moves,
    one,
    small,
    gates,
    h_weight,
    query,
    inputs,
    proj_weight,
    slope_one,
    far_one,
    far_gates,
    far_query,
    far_slope,
    modulator,
    aggregated,
    mixed,
    middle,
    normed_two,
    two,
    three,
    slope_two,
    slope_three,
    pooled,
    wide,
    tap_ref,
):
    chain = ((1, one, two, slope_two), (2, two, three, slope_three))
    moves.arrive(small)
    spread_taps(shape, small, tap_ref)
    moves.copy(one, far_one)
    moves.copy(gates, far_gates)
    moves.copy(query, far_query)
    moves.copy(slope_one, far_slope)
    total = run_levels(shape, moves, chain, tap_ref)
    value, rise = gelu_pair(total * (1.0 / shape.patches))
    pooled[0:sublanes, :] = value
    pooled[sublanes : 2 * sublanes, :] = rise * (1.0 / shape.patches)
    moves.leave(pooled)
    moves.arrive(h_weight, proj_weight)
    for image, tile, slot in shape.places():
        rows = pl.ds(image * shape.segment, shape.segment)
        wide[rows, columns(tile)] = (
            level_rows(shape, one, image, slot) * gates[rows, columns(0)]
            + level_rows(shape, two, image, slot) * gates[rows, columns(1)]
            + level_rows(shape, three, image, slot) * gates[rows, columns(2)]
            + value[slot : slot + 1] * gates[rows, columns(3)]
        )
    aggregated[...] = wide[...].astype(bf16)
    moves.leave(aggregated)
    modulator[...] = nn(aggregated[...], h_weight[...]) + small[H_BIAS : H_BIAS + 1, :]

    moves.leave(modulator)

    def mix(rows, carry):
        mixed[rows, :] = (query[rows, :] * modulator[rows, :]).astype(bf16)
        return carry

    blocks(shape, mix, 0)
    moves.leave(mixed)
    middle[...] = (
        inputs[...] + nn(mixed[...], proj_weight[...]) + small[PROJ_BIAS : PROJ_BIAS + 1, :]
    )
    moves.leave(middle)
    gain = small[LN2_GAIN : LN2_GAIN + 1, :]
    bias = small[LN2_BIAS : LN2_BIAS + 1, :]

    def second_norm(rows, carry):
        unit, _ = normalise(middle[rows, :])
        normed_two[rows, :] = (unit * gain + bias).astype(bf16)
        return carry

    blocks(shape, second_norm, 0)


class Moves:
    def __init__(self):
        self.incoming, self.outgoing = {}, {}
        self.started, self.free = [], []

    def copy(self, source, target):
        move = pltpu.make_async_copy(source, target, self.free.pop())
        move.start()
        self.started.append(move)

    def arrive(self, *buffers):
        for buffer in buffers:
            move = self.incoming.pop(id(buffer), None)
            if move is not None:
                move.wait()

    def leave(self, *buffers):
        for buffer in buffers:
            move = self.outgoing.pop(id(buffer), None)
            if move is not None:
                move.start()
                self.started.append(move)

    def finish(self):
        for move in list(self.incoming.values()):
            move.wait()
        for move in list(self.outgoing.values()):
            move.start()
            self.started.append(move)
        for move in self.started:
            move.wait()


def with_moves(kernel, far_in, far_out, extra):
    def run(*refs):
        refs = list(refs)
        ins, refs = refs[: len(far_in)], refs[len(far_in) :]
        outs, refs = refs[: len(far_out)], refs[len(far_out) :]
        semaphores = refs.pop()
        count = sum(far_in) + sum(far_out)
        buffers, scratch = refs[len(refs) - count :], refs[: len(refs) - count]
        moves = Moves()
        moves.free = [semaphores.at[count + spare] for spare in range(extra)]
        index = 0
        for group, flags, table in (
            (ins, far_in, moves.incoming),
            (outs, far_out, moves.outgoing),
        ):
            for place, far in enumerate(flags):
                if far:
                    buffer, outer = buffers[index], group[place]
                    pair = (outer, buffer) if group is ins else (buffer, outer)
                    move = pltpu.make_async_copy(*pair, semaphores.at[index])
                    if group is ins:
                        move.start()
                    table[id(buffer)] = move
                    group[place] = buffer
                    index += 1
        kernel(moves, *ins, *outs, *scratch)
        moves.finish()

    return run


class Units:
    def __init__(self, shards, unit):
        self.shards, self.unit = shards, unit
        self.piece_rows = 2 * unit + 16
        self.feed_rows = 2 * unit
        self.total = shards * unit
        self.head_rows, self.late_rows = 40, 16
        self.pieces = 2 * shards
        self.share = self.head_rows + self.late_rows
        self.head_total = 2 * self.pieces * self.head_rows
        self.late_total = 2 * self.pieces * self.late_rows


def sum_kernel(parts, source, out):
    size = out.shape[0]
    block = 16 if size % 16 == 0 else size

    def step(index, carry):
        rows = pl.ds(pl.multiple_of(index * block, block), block)
        total = source[0, rows, :].astype(f32)
        for part in range(1, parts):
            total = total + source[part, rows, :].astype(f32)
        out[rows, :] = total.astype(bf16)
        return carry

    lax.fori_loop(0, size // block, step, 0)


def pair_kernel(first, second, out):
    for part in range(out.shape[0]):
        total = first[part].astype(f32) + second[part].astype(f32)
        out[part] = total.astype(bf16)


def rows_kernel(shape, moves, first, second, arrived, first_out, second_out):
    def step(index, carry):
        rows = pl.ds(pl.multiple_of(index * 16, 16), 16)
        more = pl.ds(pl.multiple_of(index * 16 + shape.rows, 16), 16)
        first_out[rows, :] = (first[rows, :].astype(f32) + arrived[rows, :].astype(f32)).astype(bf16)
        second_out[rows, :] = (second[rows, :].astype(f32) + arrived[more, :].astype(f32)).astype(
            bf16
        )
        return carry

    lax.fori_loop(0, shape.rows // 16, step, 0)


def share_kernel(head_parts, late_parts, out):
    sums = []
    for parts in (head_parts, late_parts):
        total = parts[0].astype(f32)
        for part in range(1, parts.shape[0]):
            total = total + parts[part].astype(f32)
        sums.append(total)
    share = jnp.concatenate(sums).astype(bf16)
    for copy in range(out.shape[0]):
        out[copy] = share


def piece_kernel(units, copies, spots, first, second, far_bias, out, own, bias, semaphores):
    unit = units.unit
    width = first.shape[1]
    rows = pl.ds(pl.multiple_of(spots[0] * unit, 16), unit)
    moves = [
        pltpu.make_async_copy(source.at[rows, :], own.at[index], semaphores.at[index])
        for index, source in enumerate((first, second))
    ]
    moves.insert(0, pltpu.make_async_copy(far_bias, bias, semaphores.at[2]))
    for move in moves:
        move.start()
    moves.pop(0).wait()
    shard = spots[1]
    values = bias[...].astype(f32).reshape(1, bias.shape[0])
    values = jnp.concatenate([values, jnp.zeros((1, width - bias.shape[0]), f32)], axis=1)
    values = pltpu.roll(jnp.broadcast_to(values, (8, width)), spots[2], 1)
    lane = lax.broadcasted_iota(jnp.int32, (8, width), 1) - shard * unit
    row = lax.broadcasted_iota(jnp.int32, (8, width), 0)
    values = jnp.where((lane >= 0) & (lane < unit) & (row == 0), values, 0.0)
    line = jnp.concatenate([values, jnp.zeros((8, width), f32)]).astype(bf16)
    for move in moves:
        move.wait()
    for copy in range(copies):
        base = copy * units.piece_rows
        out[base : base + unit, :] = own[0]
        out[base + unit : base + 2 * unit, :] = own[1]
        out[base + 2 * unit : base + units.piece_rows, :] = line


def feed_kernel(shape, units, resumed, moves, weights, *refs):
    refs = list(refs)

    def take(count):
        taken = refs[:count]
        del refs[:count]
        return taken

    groups = 1 if resumed is None else 2
    closing = resumed is not False
    normed, cots = take(groups), take(groups)
    if resumed:
        old_grads, old_bias, *near = take(6)
    if resumed:
        out, d_out, both = take(3)
        outs = [out, both.at[shape.rows : 2 * shape.rows, :]]
        d_outs = [d_out, both.at[0 : shape.rows, :]]
        d_near, out_near = take(2)
    else:
        outs, d_outs = take(groups), take(groups)
    grads, bias_grad = take(2)
    first_weight, second_weight, total_grads, total_bias = take(4)
    unit, width = units.unit, shape.width
    bias = None
    for shard in range(units.shards):
        base, here = shard * units.piece_rows, shard * unit
        first_weight[here : here + unit, :] = weights[base : base + unit, :]
        second_weight[here : here + unit, :] = weights[base + unit : base + 2 * unit, :]
        term = weights[base + 2 * unit : base + units.piece_rows, :].astype(f32)
        bias = term if bias is None else bias + term
    bias = bias[0:1]
    if resumed:
        moves.arrive(*near)
        for target, own, arrived in ((d_near, near[0], near[1]), (out_near, near[2], near[3])):
            target[...] = own[...].astype(f32) + arrived[...].astype(f32)
            moves.leave(target)
    for group in range(groups):
        moves.arrive(normed[group], cots[group])
        rows, cot = normed[group], cots[group]
        value, rise = gelu_pair(nt(rows[...], first_weight[...]) + bias)
        hidden = value.astype(bf16)
        outs[group][...] = nn(hidden, second_weight[...]).astype(bf16)
        d_before = (nt(cot[...], second_weight[...]) * rise).astype(bf16)
        d_outs[group][...] = nn(d_before, first_weight[...]).astype(bf16)
        moves.leave(outs[group], d_outs[group])
        first, second = tn(d_before, rows[...]), tn(hidden, cot[...])
        line = fold(d_before.astype(f32))
        if group == 0 and not resumed:
            total_grads[0 : units.total, :] = first
            total_grads[units.total :, :] = second
            total_bias[...] = line
        elif group == 0:
            total_grads[0 : units.total, :] = old_grads[0 : units.total, :] + first
            total_grads[units.total :, :] = old_grads[units.total :, :] + second
            total_bias[...] = old_bias[...] + line
        else:
            total_grads[0 : units.total, :] += first
            total_grads[units.total :, :] += second
            total_bias[...] += line
    if not closing:
        grads[...] = total_grads[...]
        bias_grad[...] = total_bias[...]
        return
    bias_grad[...] = total_bias[...]
    for shard in range(units.shards):
        base, here = shard * units.feed_rows, shard * unit
        more = units.total + here
        grads[base : base + units.feed_rows, :] = jnp.concatenate(
            [total_grads[here : here + unit, :], total_grads[more : more + unit, :]]
        ).astype(bf16)


def heads_kernel(
    shape,
    units,
    moves,
    core,
    small,
    cot,
    middle,
    d_near,
    d_far,
    bias_grads,
    proj_weight,
    query,
    modulator,
    h_weight,
    normed,
    aggregated,
    mixed,
    *refs,
):
    later, refs = refs[:9], refs[9:]
    d_middle, d_query, d_aggregated, own_rest, other_rest, *refs = refs
    fetched, refs = refs[:9], refs[9:]
    heads_body(
        shape,
        units,
        moves,
        core,
        small,
        cot,
        middle,
        d_near,
        d_far,
        bias_grads,
        proj_weight,
        query,
        modulator,
        h_weight,
        normed,
        aggregated,
        mixed,
        list(zip(later, fetched)),
        d_middle,
        d_query,
        d_aggregated,
        own_rest,
        other_rest,
        *refs,
    )


def heads_body(
    shape,
    units,
    moves,
    core,
    small,
    cot,
    middle,
    d_near,
    d_far,
    bias_grads,
    proj_weight,
    query,
    modulator,
    h_weight,
    normed,
    aggregated,
    mixed,
    later,
    d_middle,
    d_query,
    d_aggregated,
    own_rest,
    other_rest,
    d_mixed,
    d_modulator,
    head,
    d_branch,
):
    width = shape.width
    zero = jnp.zeros((8, width), f32)
    moves.arrive(small, cot, middle, d_near)
    for source, target in later:
        moves.copy(source, target)
    gain = small[LN2_GAIN : LN2_GAIN + 1, :]

    def second_norm(rows, carry):
        grads = d_near[rows, :] + d_far[rows, :].astype(f32)
        cots = cot[rows, :].astype(f32)
        d_input, d_gain = norm_back(middle[rows, :], grads, gain)
        d_total = cots + d_input
        d_middle[rows, :] = d_total
        rounded = d_total.astype(bf16)
        d_branch[rows, :] = rounded
        added = (d_gain, grads, rounded.astype(f32), cots)
        return tuple(total + fold(item) for total, item in zip(carry, added))

    d_gain, d_bias, proj_bias, out_bias = blocks(shape, second_norm, (zero,) * 4)
    moves.leave(d_middle)
    moves.arrive(proj_weight)
    d_mixed[...] = nt(d_branch[...], proj_weight[...])
    moves.arrive(query, modulator)

    def split(rows, carry):
        values = d_mixed[rows, :]
        for_query = (values * modulator[rows, :]).astype(bf16)
        for_modulator = (values * query[rows, :]).astype(bf16)
        d_query[rows, :] = for_query
        d_modulator[rows, :] = for_modulator
        return carry[0] + fold(for_query.astype(f32)), carry[1] + fold(for_modulator.astype(f32))

    query_bias, h_bias = blocks(shape, split, (zero, zero))
    moves.leave(d_query)
    moves.arrive(h_weight)
    d_aggregated[...] = nt(d_modulator[...], h_weight[...])
    moves.leave(d_aggregated)
    moves.arrive(normed, aggregated, mixed)
    head[0:width, :] = tn(d_query[...], normed[...])
    head[width : 2 * width, :] = tn(aggregated[...], d_modulator[...])
    head[2 * width : 3 * width, :] = tn(mixed[...], d_branch[...])
    sums = (h_bias, proj_bias, d_gain, d_bias, out_bias, query_bias)
    head[3 * width :, :] = jnp.concatenate(
        [row_sum(item) for item in sums]
        + [jnp.zeros((2, width), f32)]
        + [row_sum(bias_grads[8 * index : 8 * index + 8, :]) for index in range(4)]
        + [jnp.zeros((units.head_total - 3 * width - 12, width), f32)]
    )
    for half, target in enumerate((own_rest, other_rest)):
        absolute = jnp.bitwise_xor(core[0], half)
        for piece in range(units.pieces):
            first = (absolute * units.pieces + piece) * units.head_rows
            target[piece] = head[pl.ds(pl.multiple_of(first, 8), units.head_rows), :].astype(bf16)


def levels_back_kernel(
    shape,
    moves,
    small,
    gates,
    d_aggregated,
    pooled,
    slope_three,
    slope_two,
    slope_one,
    one,
    two,
    three,
    d_one,
    d_two,
    d_three,
    rounded,
    d_gates,
    tap_ref,
    d_levels,
    products,
    d_context,
):
    width = shape.width
    inner = shape.inner
    moves.arrive(small)
    spread_taps(shape, small, tap_ref)
    for ref in (d_one, d_two, d_three):
        clear_edges(shape, ref)
    moves.arrive(gates, d_aggregated, pooled)
    pool_grad = [None] * sublanes
    for image in range(shape.images):
        rows = pl.ds(image * shape.segment, shape.segment)
        for tile in range(shape.tiles):
            slot = tile * shape.images + image
            values = d_aggregated[rows, columns(tile)]
            for level in range(3):
                d_levels[pl.ds(level * inner + slot, shape.patches, stride=sublanes), :] = (
                    values[: shape.patches] * gates[rows, columns(level)][: shape.patches]
                )
            pool_grad[slot] = jnp.sum(values * gates[rows, columns(3)], axis=0, keepdims=True)
    blank = jnp.zeros((1, lanes), f32)
    pool_grad = jnp.concatenate([blank if item is None else item for item in pool_grad])
    pool_grad = pool_grad * pooled[sublanes : 2 * sublanes, :]
    wide_pool = jnp.concatenate([pool_grad] * shape.side)

    def third(line, carry):
        here = pl.multiple_of(line * shape.line, shape.line)
        value = (d_levels[pl.ds(2 * inner + here, shape.line), :] + wide_pool) * slope_three[
            pl.ds(here, shape.line), :
        ]
        d_three[pl.ds(here + shape.centre, shape.line), :] = value
        return carry

    moves.arrive(slope_three)
    lax.fori_loop(0, shape.side, third, 0)
    moves.leave(d_three)
    moves.arrive(slope_two, slope_one)
    for level, source, target, slope in ((2, d_three, d_two, slope_two), (1, d_two, d_one, slope_one)):

        def back(line, carry, level=level, source=source, target=target, slope=slope):
            here = pl.multiple_of(line * shape.line, shape.line)
            value = correlate(shape, source, tap_ref, level, line, True)
            value = (value + d_levels[pl.ds((level - 1) * inner + here, shape.line), :]) * slope[
                pl.ds(here, shape.line), :
            ]
            target[pl.ds(here + shape.centre, shape.line), :] = value
            return carry

        lax.fori_loop(0, shape.side, back, 0)
        moves.leave(target)

    def back_context(line, carry):
        here = pl.multiple_of(line * shape.line, shape.line)
        d_levels[pl.ds(here, shape.line), :] = correlate(shape, d_one, tap_ref, 0, line, True)
        return carry

    lax.fori_loop(0, shape.side, back_context, 0)
    for image, tile, slot in shape.places():
        first = image * shape.segment
        d_context[first : first + shape.patches, columns(tile)] = d_levels[
            pl.ds(slot, shape.patches, stride=sublanes), :
        ]
        if tile == 0 and shape.segment > shape.patches:
            d_context[first + shape.patches : first + shape.segment, :] = jnp.zeros(
                (shape.segment - shape.patches, width), f32
            )
    rounded[...] = d_context[...].astype(bf16)
    moves.leave(rounded)
    moves.arrive(one, two, three)
    for image in range(shape.images):
        rows = pl.ds(image * shape.segment, shape.segment)
        totals = [None] * 4
        for tile in range(shape.tiles):
            slot = tile * shape.images + image
            values = d_aggregated[rows, columns(tile)]
            for level, ref in enumerate((one, two, three)):
                term = values * level_rows(shape, ref, image, slot)
                totals[level] = term if tile == 0 else totals[level] + term
            term = values * pooled[slot : slot + 1, :]
            totals[3] = term if tile == 0 else totals[3] + term
        for gate in range(4):
            products[rows, columns(gate)] = totals[gate]
    chooser = (
        lax.broadcasted_iota(jnp.int32, (4 * lanes, lanes), 0) // lanes
        == lax.broadcasted_iota(jnp.int32, (4 * lanes, lanes), 1)
    ).astype(f32).astype(bf16)
    d_gates[...] = nn(products[...].astype(bf16), chooser).astype(bf16)


def exit_kernel(
    shape,
    units,
    moves,
    core,
    two,
    d_three,
    one,
    d_two,
    context,
    d_one,
    rounded,
    d_gates,
    small,
    normed,
    f_turned,
    d_query,
    tokens,
    d_inputs,
    own_late,
    other_late,
    packed,
    tap_grad,
    inputs,
    d_context,
    gathered,
    gate_rows,
):
    width = shape.width
    moves.arrive(two, d_three)
    tap_grads(shape, two, d_three, 2, tap_grad)
    moves.arrive(one, d_two)
    tap_grads(shape, one, d_two, 1, tap_grad)
    moves.arrive(context, d_one)
    tap_grads(shape, context, d_one, 0, tap_grad)
    moves.arrive(rounded, d_gates, small, normed, f_turned, d_query, tokens)
    gathered[0:width, :] = tn(rounded[...], normed[...])
    gathered[width : width + 8, :] = tn(d_gates[...], normed[...])[0:8]
    for tile in range(shape.tiles):
        total = None
        for image in range(shape.images):
            slot = tile * shape.images + image
            term = tap_grad[pl.ds(slot, taps, stride=sublanes), :]
            total = term if total is None else total + term
        gathered[width + 8 : width + 8 + taps, columns(tile)] = total
    gate_rows[...] = jnp.concatenate(
        [
            f_turned[2 * width : 2 * width + 4, :].astype(f32),
            jnp.zeros((lanes - 4, width), f32),
        ]
    ).astype(bf16)
    d_normed = d_context
    gate_bias = row_sum(fold(d_gates[...].astype(f32)))
    context_bias = row_sum(fold(rounded[...].astype(f32)))
    d_normed[...] = (
        nn(d_query[...], f_turned[0:width, :])
        + nn(rounded[...], f_turned[width : 2 * width, :])
        + nn(d_gates[...], gate_rows[...])
    )
    packed[...] = tokens[...].astype(f32)
    unpack(shape, packed, inputs)
    gain = small[LN1_GAIN : LN1_GAIN + 1, :]
    zero = jnp.zeros((8, width), f32)

    def finish(rows, carry):
        values = d_normed[rows, :]
        d_input, d_gain = norm_back(inputs[rows, :], values, gain)
        d_inputs[rows, :] = d_input
        return carry[0] + fold(d_gain), carry[1] + fold(values)

    d_gain, d_bias = blocks(shape, finish, (zero, zero))
    moves.leave(d_inputs)
    last = width + 8 + taps
    rest = units.late_total - last - 4
    gathered[last:, :] = jnp.concatenate(
        [
            row_sum(d_gain),
            row_sum(d_bias),
            context_bias,
            jnp.concatenate([gate_bias, jnp.zeros((1, width - lanes), f32)], axis=1),
            jnp.zeros((rest, width), f32),
        ]
    )
    for half, target in enumerate((own_late, other_late)):
        absolute = jnp.bitwise_xor(core[0], half)
        for place in range(2):
            for spot in range(units.shards):
                first = ((place * 2 + absolute) * units.shards + spot) * units.late_rows
                target[place * units.shards + spot] = gathered[
                    pl.ds(pl.multiple_of(first, 16), units.late_rows), :
                ].astype(bf16)


def finish_kernel(
    shape,
    moves,
    d_middle,
    d_inputs,
    small,
    middle,
    out_near,
    out_far,
    tokens_grad,
    block_out,
    rows_ref,
):
    moves.arrive(d_middle, d_inputs)

    def add_grads(rows, carry):
        rows_ref[rows, :] = d_middle[rows, :] + d_inputs[rows, :]
        return carry

    blocks(shape, add_grads, 0)
    pack(shape, rows_ref, tokens_grad)
    moves.leave(tokens_grad)
    moves.arrive(small, middle, out_near, out_far)

    def add_outs(rows, carry):
        total = middle[rows, :] + small[FC2_BIAS : FC2_BIAS + 1, :]
        rows_ref[rows, :] = total + out_near[rows, :] + out_far[rows, :].astype(f32)
        return carry

    blocks(shape, add_outs, 0)
    pack(shape, rows_ref, block_out)


def unpack_kernel(
    shape,
    units,
    spots,
    piece,
    piece_x,
    piece_core,
    piece_both,
    own,
    own_b,
    own_x,
    own_both,
    core_own,
    core_b,
    core_x,
    core_both,
    ln1_gain,
    ln1_bias,
    f_grad,
    f_bias,
    small_grad,
    middle_grad,
    large_grad,
    h_grad,
    h_bias,
    proj_grad,
    proj_bias,
    ln2_gain,
    ln2_bias,
    first_grad,
    first_bias,
    second_grad,
    second_bias,
    held,
    head,
    late,
):
    width = shape.width
    unit = units.unit
    size = own.shape[0]
    parts = (own, own_b, own_x, own_both, core_own, core_b, core_x, core_both)
    for index, part in enumerate(parts):
        held[index * size : (index + 1) * size, :] = part[...].astype(f32)
    core, shift = spots[0], spots[2]
    far = units.shards // 2
    for half in range(2):
        for place in range(2):
            for close in range(2):
                slot = jnp.bitwise_xor(core, half) * 4 + jnp.bitwise_xor(spots[3], place) * 2
                base = (slot + jnp.bitwise_xor(spots[4], close)) * size
                for away in range(far):
                    here = base + away * units.share
                    to = ((half * 2 + place) * far + away) * 2 + close
                    head[to * units.head_rows : (to + 1) * units.head_rows, :] = held[
                        pl.ds(pl.multiple_of(here, 8), units.head_rows), :
                    ]
                    to = ((place * 2 + half) * far + away) * 2 + close
                    late[to * units.late_rows : (to + 1) * units.late_rows, :] = held[
                        pl.ds(pl.multiple_of(here + units.head_rows, 8), units.late_rows), :
                    ]
    total = None
    lane = lax.broadcasted_iota(jnp.int32, (8, width), 1)
    for index, source in enumerate((piece, piece_core, piece_x, piece_both)):
        quarter = jnp.bitwise_xor(spots[1], index)
        to = pl.ds(pl.multiple_of(quarter * unit, 8), unit)
        first_grad[to, :] = source[0:unit, :].astype(f32)
        second_grad[to, :] = source[unit : 2 * unit, :].astype(f32)
    for quarter in range(4):
        row = head[3 * width + 8 + quarter : 3 * width + 9 + quarter, :]
        moved = shift + quarter * unit
        moved = jnp.where(moved >= width, moved - width, moved)
        row = pltpu.roll(jnp.broadcast_to(row, (8, width)), moved, 1)
        row = jnp.where((lane >= quarter * unit) & (lane < (quarter + 1) * unit), row, 0.0)
        total = row if total is None else total + row
    first_bias[...] = total[0:1, 0 : first_bias.shape[0]].reshape(first_bias.shape)
    f_grad[0:width, :] = head[0:width, :]
    f_grad[width : 2 * width + 4, :] = late[0 : width + 4, :]
    h_grad[...] = head[width : 2 * width, :]
    proj_grad[...] = head[2 * width : 3 * width, :]
    first = width + 8
    small_grad[...] = late[first : first + 9, :]
    middle_grad[...] = late[first + 9 : first + 34, :]
    large_grad[...] = late[first + 34 : first + taps, :]
    first = first + taps
    for out, source, row in (
        (h_bias, head, 3 * width),
        (proj_bias, head, 3 * width + 1),
        (ln2_gain, head, 3 * width + 2),
        (ln2_bias, head, 3 * width + 3),
        (second_bias, head, 3 * width + 4),
        (ln1_gain, late, first),
        (ln1_bias, late, first + 1),
    ):
        out[...] = source[row : row + 1, :].reshape(width)
    f_bias[0:width] = head[3 * width + 5 : 3 * width + 6, :].reshape(width)
    f_bias[width : 2 * width] = late[first + 2 : first + 3, :].reshape(width)
    f_bias[2 * width : 2 * width + 4] = late[first + 3 : first + 4, 0:4].reshape(4)


def call(kernel, name, outs, scratch, micros, room, *operands):
    spec = pl.BlockSpec(memory_space=pltpu.VMEM)
    outer = pl.BlockSpec(memory_space=pltpu.HBM)
    far_in = [isinstance(item, Far) for item in operands]
    far_out = [isinstance(item, Far) for item in outs]
    anywhere = [isinstance(item, Anywhere) for item in operands]
    raw = [isinstance(item, Raw) for item in operands]
    operands = [item.value if far else item for item, far in zip(operands, far_in)]
    operands = [
        pltpu.with_memory_space_constraint(item, pltpu.HBM) if far and not free else item
        for item, far, free in zip(operands, far_in, anywhere)
    ]
    raw_out = [isinstance(item, Raw) for item in outs]
    outs = [
        pltpu.HBM(item.value.shape, item.value.dtype) if far else item
        for item, far in zip(outs, far_out)
    ]
    specs = []
    for item, far, free in zip(operands, far_in, anywhere):
        if free:
            specs.append(pl.BlockSpec(memory_space=pl.ANY))
        elif item.dtype == jnp.int32:
            specs.append(pl.BlockSpec(memory_space=pltpu.SMEM))
        else:
            specs.append(outer if far else spec)
    out_specs = [outer if far else spec for far in far_out]
    if name not in plain:
        far_in = [far and not own for far, own in zip(far_in, raw)]
        far_out = [far and not own for far, own in zip(far_out, raw_out)]
        pairs = list(zip(operands, far_in)) + list(zip(outs, far_out))
        buffers = [pltpu.VMEM(item.shape, item.dtype) for item, far in pairs if far]
        extra = sum(raw) + sum(raw_out)
        semaphores = pltpu.SemaphoreType.DMA((max(len(buffers) + extra, 1),))
        scratch = list(scratch) + buffers + [semaphores]
        kernel = with_moves(kernel, far_in, far_out, extra)
    moved = sum(item.size * item.dtype.itemsize for item in operands)
    return pl.pallas_call(
        kernel,
        name=name,
        out_shape=outs,
        in_specs=specs,
        out_specs=out_specs,
        scratch_shapes=scratch,
        compiler_params=pltpu.CompilerParams(vmem_limit_bytes=room * 1024 * 1024),
        cost_estimate=pl.CostEstimate(
            flops=int(micros * 1.1e9), bytes_accessed=moved, transcendentals=0
        ),
    )(*operands)


plain = ("piece", "sum", "pair", "share", "unpack")


class Far:
    def __init__(self, value):
        self.value = value


class Anywhere(Far):
    pass


class Raw(Far):
    pass


def far_array(*dims, kind=jnp.float32):
    return Far(array(*dims, kind=kind))


def array(*dims, kind=jnp.float32):
    return jax.ShapeDtypeStruct(dims, kind)


def to_packed(values, shape):
    moved = with_layout_constraint(values.transpose(1, 2, 0, 3), Layout((0, 1, 2, 3)))
    moved = moved.reshape(shape.patches, shape.images, shape.tiles, lanes)
    moved = with_layout_constraint(moved, Layout((0, 2, 1, 3)))
    return moved.transpose(0, 2, 1, 3).reshape(shape.packed, lanes)


def from_packed(values, shape):
    moved = values.reshape(shape.patches, shape.tiles, shape.images, lanes).transpose(0, 2, 1, 3)
    moved = moved.reshape(shape.side, shape.side, shape.images, shape.width)
    return moved.transpose(2, 0, 1, 3)


everyone = ("x", "core", "a", "b")


def gather_plainly(units, first, bias, second):
    first = lax.all_gather(first, ("a", "b"), axis=0, tiled=True)
    second = lax.all_gather(second, ("a", "b"), axis=0, tiled=True)
    bias = lax.all_gather(bias, ("a", "b"), axis=0, tiled=True)
    width = first.shape[1]
    rows = jnp.pad(bias.reshape(4, 1, 1, width), ((0, 0), (0, units.shards - 1), (0, 15), (0, 0)))
    shape = (4, units.shards, units.unit, width)
    both = jnp.concatenate([first.reshape(shape), second.reshape(shape), rows], axis=2)
    both = both.reshape(4, units.shards * units.piece_rows, width)
    return [both[index] for index in range(4)]


def total_of(values, parts):
    rows = values.shape[0] // parts
    kernel = functools.partial(sum_kernel, parts)
    values = values.reshape(parts, rows, values.shape[1])
    return call(kernel, "sum", [array(rows, values.shape[2], kind=bf16)], [], 1, 4, values)[0]


def reduce_plainly(shape, units, feed, rest, late):
    width = shape.width
    unit = units.unit
    both = jnp.stack(feed).reshape(4, units.shards, units.feed_rows, width)
    first = both[:, :, :unit].reshape(4 * units.total, width)
    second = both[:, :, unit:].reshape(4 * units.total, width)

    def shared(values):
        part = lax.psum_scatter(values, ("a", "b"), scatter_dimension=0, tiled=True)
        return lax.psum(part, ("x", "core")).astype(f32)

    late = jnp.stack(late).reshape(2, 2, units.shards, units.late_rows, width)
    late = late.transpose(1, 0, 2, 3, 4).reshape(units.late_total, width)
    late = lax.psum(late, everyone).astype(f32)
    head = jnp.concatenate(rest).reshape(units.head_total, width)
    head = lax.psum(head, everyone).astype(f32)
    bias = head[3 * width + 8 : 3 * width + 12].reshape(-1)
    place = lax.axis_index("a") * 2 + lax.axis_index("b")
    size = bias.shape[0] // (lax.axis_size("a") * 2)
    bias = lax.dynamic_slice_in_dim(bias, place * size, size, 0)
    last = width + 8
    vectors = head[3 * width : 3 * width + 8]
    more = late[last + taps : last + taps + 4]
    return (
        more[0],
        more[1],
        jnp.concatenate([head[:width], late[: width + 4]]),
        jnp.concatenate([vectors[5], more[2], more[3, :4]]),
        late[last : last + 9],
        late[last + 9 : last + 34],
        late[last + 34 : last + taps],
        head[width : 2 * width],
        vectors[0],
        head[2 * width : 3 * width],
        vectors[1],
        vectors[2],
        vectors[3],
        shared(first),
        bias,
        shared(second),
        vectors[4],
    )


def shards(
    sizes,
    tokens,
    ln1_gain,
    ln1_bias,
    f_weight,
    f_bias,
    dw_small,
    dw_middle,
    dw_large,
    h_weight,
    h_bias,
    proj_weight,
    proj_bias,
    ln2_gain,
    ln2_bias,
    fc1_weight,
    fc1_bias,
    fc2_weight,
    fc2_bias,
    out_grad,
):
    images, side, _, width = tokens.shape
    shape = Shape(images, side, width)
    rows, grid, inner = shape.rows, shape.grid, shape.inner
    hidden = fc1_weight.shape[1] * sizes["a"] * sizes["b"]
    quick = sizes["x"] == 2 and sizes["a"] * sizes["b"] == 8
    units = Units(8, hidden // 32)
    f_turned = f_weight.T
    first, second = fc1_weight.T, fc2_weight
    scratch = pltpu.VMEM
    core = jnp.zeros((1,), jnp.int32)
    if quick:
        core = lax.axis_index("core").astype(jnp.int32).reshape(1)
        quarter = lax.axis_index("x") * 2 + core[0]
        shard = lax.axis_index("a") * 2 + lax.axis_index("b")
        turn = lax.rem(shard - quarter + units.shards, units.shards) * units.unit
        spots = jnp.stack([quarter, shard, turn]).astype(jnp.int32)
        (pieces,) = call(
            functools.partial(piece_kernel, units, units.shards),
            "piece",
            [array(units.shards * units.piece_rows, width, kind=bf16)],
            [
                scratch((2, units.unit, width), bf16),
                scratch(fc1_bias.shape, bf16),
                pltpu.SemaphoreType.DMA((3,)),
            ],
            1,
            6,
            spots,
            Far(first),
            Far(second),
            Far(fc1_bias),
        )
        weights = exchange(pieces, ("a", "b"))
    tokens_packed = to_packed(tokens, shape)

    def rows_array(kind=bf16):
        return far_array(rows, width, kind=kind)

    small, cot, inputs, normed, query, gates, context, one, slope_one = call(
        functools.partial(entry_kernel, shape),
        "entry",
        [
            far_array(96, width),
            rows_array(),
            array(rows, width),
            rows_array(),
            array(rows, width),
            array(rows, 4 * lanes),
            far_array(grid, lanes),
            array(grid, lanes),
            array(inner, lanes),
        ],
        [
            scratch((taps * sublanes, lanes), f32),
            scratch((shape.packed, lanes), f32),
            scratch((rows, width), f32),
        ],
        5,
        16,
        tokens_packed,
        f_turned,
        to_packed(out_grad, shape),
        dw_small,
        dw_middle,
        dw_large,
        ln1_gain,
        ln1_bias,
        f_bias,
        h_bias,
        proj_bias,
        ln2_gain,
        ln2_bias,
        fc2_bias,
    )
    if quick:
        cot_far = flip(cot, "x")
        cot_core = flip(cot)
    one, gates, query, slope_one, *results = call(
        functools.partial(modulation_kernel, shape),
        "modulation",
        [
            Raw(array(grid, lanes)),
            Raw(array(rows, 4 * lanes)),
            Raw(array(rows, width)),
            Raw(array(inner, lanes)),
            rows_array(f32),
            rows_array(),
            rows_array(),
            rows_array(f32),
            rows_array(),
            far_array(grid, lanes),
            far_array(grid, lanes),
            far_array(inner, lanes),
            far_array(inner, lanes),
            far_array(2 * sublanes, lanes),
        ],
        [scratch((rows, width), f32), scratch((taps * sublanes, lanes), f32)],
        8,
        20,
        one,
        Far(small),
        gates,
        Far(h_weight),
        query,
        inputs,
        Far(proj_weight),
        slope_one,
    )
    modulator, aggregated, mixed, middle, normed_two, *results = results
    two, three, slope_two, slope_three, pooled = results

    def feed(resumed, outs, *operands):
        return call(
            functools.partial(feed_kernel, shape, units, resumed),
            "feed",
            outs,
            [
                scratch((units.total, width), bf16),
                scratch((units.total, width), bf16),
                scratch((2 * units.total, width), f32),
                scratch((8, width), f32),
            ],
            6,
            24,
            *operands,
        )

    near_rows = array(rows, width, kind=bf16)
    feed_total = array(units.shards * units.feed_rows, width, kind=bf16)
    bias_total = array(8, width)
    if quick:
        cot_both = flip(after(cot_far, middle))
        normed_far = flip(normed_two, "x")
        normed_core = flip(normed_two)
        out_own, out_core, d_own, d_core, *carry = feed(
            False,
            [near_rows] * 4 + [array(2 * units.total, width), bias_total],
            weights,
            Far(normed_two),
            normed_core,
            Far(cot),
            cot_core,
        )
        out_core, d_core = flip(out_core), flip(d_core)
        normed_far = after(normed_far, d_own)
        normed_both = flip(normed_far)
        out_far, d_far, both, d_near, out_near, feed_grads, bias_grad = feed(
            True,
            [near_rows] * 2
            + [array(2 * rows, width, kind=bf16), rows_array(f32), rows_array(f32), feed_total]
            + [bias_total],
            weights,
            normed_far,
            normed_both,
            cot_far,
            cot_both,
            *carry,
            d_own,
            d_core,
            out_own,
            out_core,
        )
        arrived = flip(both)
        d_far, out_far = call(
            functools.partial(rows_kernel, shape),
            "rows",
            [near_rows, rows_array()],
            [],
            1,
            8,
            d_far,
            out_far,
            arrived,
        )
        feed_grads = after(feed_grads, d_far)
        d_far = flip(d_far, "x")
        feed_parts = exchange(feed_grads, ("a", "b"))
        mine = (jnp.arange(4) == quarter).astype(f32)
        bias_grads = (mine[:, None, None] * bias_grad).reshape(32, width)
    else:
        out_far = d_far = jnp.zeros((rows, width), bf16)
        out_near, d_near, feed_grads, bias_grads = jnp.zeros((rows, width), f32), 0.0, [], []
        for weights in gather_plainly(units, first, fc1_bias, second):
            out, d_out, grads, bias_grad = feed(
                None, [near_rows, near_rows, feed_total, bias_total], weights, normed_two, cot
            )
            bias_grads.append(bias_grad)
            out_near, d_near = out_near + out.astype(f32), d_near + d_out.astype(f32)
            feed_grads.append(grads)
        bias_grads = jnp.concatenate(bias_grads)
    rest = array(units.pieces, units.head_rows, width, kind=bf16)
    later = [small, gates, pooled, slope_three, slope_two, slope_one, one, two, three]
    d_middle, d_query, d_aggregated, own_rest, other_rest, *fetched = call(
        functools.partial(heads_kernel, shape, units),
        "heads",
        [rows_array(f32), rows_array(), array(rows, width), rest, rest]
        + [array(*item.shape) for item in later],
        [
            scratch((rows, width), f32),
            scratch((rows, width), bf16),
            scratch((units.head_total, width), f32),
            scratch((rows, width), bf16),
        ],
        5,
        16,
        core,
        Far(small),
        Far(cot),
        Far(middle),
        Far(d_near),
        d_far,
        bias_grads,
        Far(proj_weight),
        Far(query),
        Far(modulator),
        Far(h_weight),
        Far(normed),
        Far(aggregated),
        Far(mixed),
        *[Raw(item) for item in later],
    )
    if quick:
        out_far = flip(after(out_far, d_middle), "x")
        rest_arrived = flip(other_rest)
    d_one, d_two, d_three, rounded, d_gates = call(
        functools.partial(levels_back_kernel, shape),
        "levels_back",
        [
            far_array(grid, lanes),
            far_array(grid, lanes),
            far_array(grid, lanes),
            rows_array(),
            far_array(rows, lanes, kind=bf16),
        ],
        [
            scratch((taps * sublanes, lanes), f32),
            scratch((3 * inner, lanes), f32),
            scratch((rows, 4 * lanes), f32),
            scratch((rows, width), f32),
        ],
        8,
        24,
        fetched[0],
        fetched[1],
        d_aggregated,
        *fetched[2:],
    )
    if quick:
        (rest_half,) = call(pair_kernel, "pair", [rest], [], 1, 4, own_rest, rest_arrived)
        feed_parts = after(feed_parts, d_one)
        piece = total_of(feed_parts, units.shards)
        rest_half = after(rest_half, piece)
        d_one = after(d_one, rest_half, out_far)
        shares = rest_half.shape
        rest_parts = exchange(rest_half.reshape(-1, width), ("x", "a", "b")).reshape(shares)
    late = array(units.pieces, units.late_rows, width, kind=bf16)
    d_inputs, own_late, other_late = call(
        functools.partial(exit_kernel, shape, units),
        "exit",
        [array(rows, width), late, late],
        [
            scratch((shape.packed, lanes), f32),
            scratch((taps * sublanes, lanes), f32),
            scratch((rows, width), f32),
            scratch((rows, width), f32),
            scratch((units.late_total, width), f32),
            scratch((lanes, width), bf16),
        ],
        9,
        24,
        core,
        Far(two),
        Far(d_three),
        Far(one),
        Far(d_two),
        Far(context),
        Far(d_one),
        Far(rounded),
        Far(d_gates),
        Far(small),
        Far(normed),
        Far(f_turned),
        Far(d_query),
        Far(tokens_packed),
    )
    if quick:
        late_arrived = flip(other_late)
    tokens_grad, block_out = call(
        functools.partial(finish_kernel, shape),
        "finish",
        [far_array(shape.packed, lanes), far_array(shape.packed, lanes)],
        [scratch((rows, width), f32)],
        3,
        16,
        Far(d_middle),
        d_inputs,
        Far(small),
        Far(middle),
        Far(out_near),
        Anywhere(out_far),
    )
    if quick:
        rest_parts = after(rest_parts, tokens_grad)
        (late_half,) = call(pair_kernel, "pair", [late], [], 1, 4, own_late, late_arrived)
        late_half, rest_parts = lax.optimization_barrier((late_half, rest_parts))
        shares = late_half.shape
        late_parts = exchange(late_half.reshape(-1, width), ("x", "a", "b")).reshape(shares)
        piece = after(piece, late_half)
        piece_x = flip(piece, "x")
        piece_core, piece_both = flip(piece), flip(piece_x)
        (share,) = call(
            share_kernel,
            "share",
            [array(sizes["a"], units.share, width, kind=bf16)],
            [],
            1,
            6,
            rest_parts,
            late_parts,
        )
        share = after(share, piece_core, piece_both)
        own = exchange(share.reshape(-1, width), "a")
        held_b, held_x = flip(own, "b"), flip(own, "x")
        held_both = flip(held_b, "x")
        held = [own, held_b, held_x, held_both]
        held = held + [flip(item) for item in held]
        turn = lax.rem(units.shards - shard, units.shards) * units.unit
        spots = [core[0], quarter, turn] + [lax.axis_index(axis) for axis in ("x", "b")]
        spots = jnp.stack(spots).astype(jnp.int32)
        total = 4 * units.unit
        others = call(
            functools.partial(unpack_kernel, shape, units),
            "unpack",
            [
                array(width),
                array(width),
                array(2 * width + 4, width),
                array(2 * width + 4),
                array(9, width),
                array(25, width),
                array(49, width),
                array(width, width),
                array(width),
                array(width, width),
                array(width),
                array(width),
                array(width),
                array(total, width),
                array(total),
                array(total, width),
                array(width),
            ],
            [
                scratch((2 * units.pieces * units.share, width), f32),
                scratch((units.head_total, width), f32),
                scratch((units.late_total, width), f32),
            ],
            2,
            16,
            spots,
            piece,
            piece_x,
            piece_core,
            piece_both,
            *held,
        )
    else:
        others = reduce_plainly(
            shape, units, feed_grads, (own_rest, other_rest), (own_late, other_late)
        )
    others = list(others)
    others[2] = others[2].T
    others[13] = others[13].T
    return from_packed(block_out, shape), from_packed(tokens_grad, shape), *others


def solution(mesh):
    img, mlp = mesh.shape["img"], mesh.shape["mlp"]
    sizes = {"x": img // 2, "core": 2, "a": mlp // 2, "b": 2}
    finer = Mesh(mesh.devices.reshape(*sizes.values()), everyone)
    images = P(everyone, None, None, None)
    hidden = ("a", "b")
    return jax.shard_map(
        functools.partial(shards, sizes),
        mesh=finer,
        in_specs=(images,)
        + (P(),) * 13
        + (P(None, hidden), P(hidden), P(hidden, None), P(), images),
        out_specs=(images, images)
        + (P(),) * 13
        + (P(None, hidden), P(hidden), P(hidden, None), P()),
        check_vma=False,
    )
```

```python
import functools
import math

import jax
import jax.numpy as jnp
from jax import lax
from jax.experimental import pallas as pl
from jax.experimental.pallas import tpu as pltpu
from jax.experimental.layout import Layout, with_layout_constraint
from jax.sharding import Mesh
from jax.sharding import PartitionSpec as P

epsilon = 1e-05
lanes = 128
sublanes = 8
edge = 3
extents = (3, 5, 7)
starts = (0, 9, 34)
taps = 83
LN1_GAIN, LN1_BIAS, QUERY_BIAS, CONTEXT_BIAS, GATE_BIAS = 83, 84, 85, 86, 87
H_BIAS, PROJ_BIAS, LN2_GAIN, LN2_BIAS, FC2_BIAS = 88, 89, 90, 91, 92
f32 = jnp.float32
bf16 = jnp.bfloat16


def flip(values, axis="core", size=2, bit=1):
    return lax.ppermute(values, axis, [(place, place ^ bit) for place in range(size)])


def exchange(values, axes):
    return lax.all_to_all(values, axes, split_axis=0, concat_axis=0, tiled=True)


def after(values, *others):
    return lax.optimization_barrier((values,) + others)[0]


def nn(left, right):
    return jnp.dot(left, right, preferred_element_type=f32)


def nt(left, right):
    return lax.dot_general(left, right, (((1,), (1,)), ((), ())), preferred_element_type=f32)


def tn(left, right):
    return lax.dot_general(left, right, (((0,), (0,)), ((), ())), preferred_element_type=f32)


def gelu_pair(values):
    below = 0.5 * (1.0 + lax.erf(values * math.sqrt(0.5)))
    density = jnp.exp(values * values * -0.5) * (1.0 / math.sqrt(2.0 * math.pi))
    return values * below, below + values * density


class Shape:
    def __init__(self, images, side, width):
        self.images, self.side, self.width = images, side, width
        self.tiles = width // lanes
        self.slots = images * self.tiles
        self.patches = side * side
        self.segment = -(-self.patches // 8) * 8
        self.rows = images * self.segment
        self.line = side * sublanes
        self.centre = edge * self.line
        self.grid = (side + 2 * edge) * self.line
        self.inner = side * self.line
        self.packed = self.patches * self.slots
        self.block = next(size for size in (80, 40, 16, 8) if self.rows % size == 0)

    def places(self):
        return [
            (image, tile, tile * self.images + image)
            for image in range(self.images)
            for tile in range(self.tiles)
        ]


def columns(tile):
    return slice(tile * lanes, (tile + 1) * lanes)


def unpack(shape, packed, rows):
    for image, tile, slot in shape.places():
        first = image * shape.segment
        rows[first : first + shape.patches, columns(tile)] = packed[
            pl.ds(slot, shape.patches, stride=shape.slots), :
        ]
    for image in range(shape.images):
        first = image * shape.segment
        spare = shape.segment - shape.patches
        if spare:
            rows[first + shape.patches : first + shape.segment, 0 : shape.width] = jnp.zeros(
                (spare, shape.width), f32
            )


def pack(shape, rows, packed):
    for image, tile, slot in shape.places():
        first = image * shape.segment
        packed[pl.ds(slot, shape.patches, stride=shape.slots), :] = rows[
            first : first + shape.patches, columns(tile)
        ]


def blocks(shape, body, init=None):
    def step(index, carry):
        first = pl.multiple_of(index * shape.block, shape.block)
        return body(pl.ds(first, shape.block), carry)

    return lax.fori_loop(0, shape.rows // shape.block, step, init)


def normalise(values):
    average = jnp.mean(values, axis=-1, keepdims=True)
    centred = values - average
    variance = jnp.mean(centred * centred, axis=-1, keepdims=True)
    scale = lax.rsqrt(variance + epsilon)
    return centred * scale, scale


def norm_back(values, grad, gain):
    unit, scale = normalise(values)
    inner = grad * gain
    first = jnp.mean(inner, axis=-1, keepdims=True)
    second = jnp.mean(inner * unit, axis=-1, keepdims=True)
    return scale * (inner - first - unit * second), grad * unit


def fold(values):
    return jnp.sum(values.reshape(values.shape[0] // 8, 8, values.shape[1]), axis=0)


def row_sum(values):
    return jnp.sum(values, axis=0, keepdims=True)


def spread_taps(shape, small, tap_ref):
    tap_ref[...] = jnp.zeros_like(tap_ref)
    for _, tile, slot in shape.places():
        tap_ref[pl.ds(slot, taps, stride=sublanes), :] = small[0:taps, columns(tile)]


def line_at(shape, ref, line):
    first = pl.multiple_of(line * shape.line, shape.line)
    values = ref[pl.ds(first, shape.line), :]
    return [values[w * sublanes : (w + 1) * sublanes] for w in range(shape.side)]


def correlate(shape, source, tap_ref, level, line, turned):
    extent = extents[level]
    reach = extent // 2
    totals = [None] * shape.side
    for down in range(extent):
        values = line_at(shape, source, line + down + edge - reach)
        for along in range(extent):
            entry = down * extent + along
            if turned:
                entry = extent * extent - 1 - entry
            tap = tap_ref[pl.ds((starts[level] + entry) * sublanes, sublanes), :]
            for w in range(shape.side):
                other = w + along - reach
                if 0 <= other < shape.side:
                    term = values[other] * tap
                    totals[w] = term if totals[w] is None else totals[w] + term
    return jnp.concatenate(totals, axis=0)


def tap_grads(shape, source, grad, level, out):
    extent = extents[level]
    reach = extent // 2
    for down in range(extent):

        def step(line, totals, down=down):
            values = line_at(shape, source, line + down + edge - reach)
            grads = line_at(shape, grad, line + edge)
            result = []
            for along in range(extent):
                total = totals[along]
                for w in range(shape.side):
                    other = w + along - reach
                    if 0 <= other < shape.side:
                        total = total + values[other] * grads[w]
                result.append(total)
            return tuple(result)

        zero = jnp.zeros((sublanes, lanes), f32)
        first, last = max(0, reach - down), min(shape.side, shape.side + reach - down)
        totals = lax.fori_loop(first, last, step, (zero,) * extent)
        for along in range(extent):
            out[pl.ds((starts[level] + down * extent + along) * sublanes, sublanes), :] = totals[
                along
            ]


def clear_edges(shape, ref):
    zeros = jnp.zeros((shape.centre, lanes), f32)
    ref[0 : shape.centre, :] = zeros
    ref[shape.centre + shape.inner : shape.grid, :] = zeros


def gate_values(shape, normed, f_turned, small, gates):
    weight = f_turned[2 * shape.width : 2 * shape.width + 4, :].astype(f32)
    wide = jnp.concatenate(
        [jnp.broadcast_to(weight[g : g + 1], (lanes, shape.width)) for g in range(4)]
    ).astype(bf16)
    bias = small[GATE_BIAS : GATE_BIAS + 1, :]
    wide_bias = jnp.concatenate(
        [jnp.broadcast_to(bias[:, g : g + 1], (1, lanes)) for g in range(4)], axis=1
    )
    gates[...] = nt(normed[...], wide) + wide_bias


def level_rows(shape, level, image, slot):
    return level[pl.ds(shape.centre + slot, shape.segment, stride=sublanes), :]


def run_levels(shape, moves, chain, tap_ref):
    total = jnp.zeros((sublanes, lanes), f32)
    for level, source, target, slope in chain:
        clear_edges(shape, target)

        def line_step(line, total, level=level, source=source, target=target, slope=slope):
            before = correlate(shape, source, tap_ref, level, line, False)
            value, rise = gelu_pair(before)
            here = pl.multiple_of((line + edge) * shape.line, shape.line)
            target[pl.ds(here, shape.line), :] = value
            slope[pl.ds(pl.multiple_of(line * shape.line, shape.line), shape.line), :] = rise
            if level == 2:
                total = total + fold(value)
            return total

        total = lax.fori_loop(0, shape.side, line_step, total)
        moves.leave(target, slope)
    return total


def entry_kernel(
    shape,
    moves,
    tokens,
    f_turned,
    out_grad,
    dw_small,
    dw_middle,
    dw_large,
    ln1_gain,
    ln1_bias,
    f_bias,
    h_bias,
    proj_bias,
    ln2_gain,
    ln2_bias,
    fc2_bias,
    small,
    cot,
    inputs,
    normed,
    query,
    gates,
    context,
    one,
    slope_one,
    tap_ref,
    packed,
    wide,
):
    width = shape.width
    for source, first in zip((dw_small, dw_middle, dw_large), starts):
        small[first : first + source.shape[0], :] = source[...].astype(f32)
    shared = f_bias[...].astype(f32).reshape(1, 2 * width + 4)
    vectors = {
        QUERY_BIAS: shared[:, 0:width],
        CONTEXT_BIAS: shared[:, width : 2 * width],
        GATE_BIAS: jnp.concatenate(
            [shared[:, 2 * width :], jnp.zeros((1, width - 4), f32)], axis=1
        ),
    }
    for row, source in (
        (LN1_GAIN, ln1_gain),
        (LN1_BIAS, ln1_bias),
        (H_BIAS, h_bias),
        (PROJ_BIAS, proj_bias),
        (LN2_GAIN, ln2_gain),
        (LN2_BIAS, ln2_bias),
        (FC2_BIAS, fc2_bias),
    ):
        vectors[row] = source[...].astype(f32).reshape(1, width)
    for row, value in vectors.items():
        small[row : row + 1, :] = value
    last = FC2_BIAS + 1
    small[last:, :] = jnp.zeros((small.shape[0] - last, width), f32)
    moves.leave(small)
    moves.arrive(tokens)
    packed[...] = tokens[...].astype(f32)
    unpack(shape, packed, inputs)
    moves.leave(inputs)
    spread_taps(shape, small, tap_ref)
    gain = small[LN1_GAIN : LN1_GAIN + 1, :]
    bias = small[LN1_BIAS : LN1_BIAS + 1, :]

    def first_norm(rows, carry):
        unit, _ = normalise(inputs[rows, :])
        normed[rows, :] = (unit * gain + bias).astype(bf16)
        return carry

    blocks(shape, first_norm, 0)
    moves.leave(normed)
    moves.arrive(out_grad)
    packed[...] = out_grad[...].astype(f32)
    unpack(shape, packed, wide)
    cot[...] = wide[...].astype(bf16)
    moves.leave(cot)
    moves.arrive(f_turned)
    wide[...] = (
        nt(normed[...], f_turned[width : 2 * width, :]) + small[CONTEXT_BIAS : CONTEXT_BIAS + 1, :]
    )
    context[...] = jnp.zeros_like(context)
    for image, tile, slot in shape.places():
        first = image * shape.segment
        context[pl.ds(shape.centre + slot, shape.patches, stride=sublanes), :] = wide[
            first : first + shape.patches, columns(tile)
        ]
    moves.leave(context)
    query[...] = nt(normed[...], f_turned[0:width, :]) + small[QUERY_BIAS : QUERY_BIAS + 1, :]
    moves.leave(query)
    gate_values(shape, normed, f_turned, small, gates)
    moves.leave(gates)
    run_levels(shape, moves, ((0, context, one, slope_one),), tap_ref)


def modulation_kernel(
    shape,
    moves,
    one,
    small,
    gates,
    h_weight,
    query,
    inputs,
    proj_weight,
    slope_one,
    far_one,
    far_gates,
    far_query,
    far_slope,
    modulator,
    aggregated,
    mixed,
    middle,
    normed_two,
    two,
    three,
    slope_two,
    slope_three,
    pooled,
    wide,
    tap_ref,
):
    chain = ((1, one, two, slope_two), (2, two, three, slope_three))
    moves.arrive(small)
    spread_taps(shape, small, tap_ref)
    moves.copy(one, far_one)
    moves.copy(gates, far_gates)
    moves.copy(query, far_query)
    moves.copy(slope_one, far_slope)
    total = run_levels(shape, moves, chain, tap_ref)
    value, rise = gelu_pair(total * (1.0 / shape.patches))
    pooled[0:sublanes, :] = value
    pooled[sublanes : 2 * sublanes, :] = rise * (1.0 / shape.patches)
    moves.leave(pooled)
    moves.arrive(h_weight, proj_weight)
    for image, tile, slot in shape.places():
        rows = pl.ds(image * shape.segment, shape.segment)
        wide[rows, columns(tile)] = (
            level_rows(shape, one, image, slot) * gates[rows, columns(0)]
            + level_rows(shape, two, image, slot) * gates[rows, columns(1)]
            + level_rows(shape, three, image, slot) * gates[rows, columns(2)]
            + value[slot : slot + 1] * gates[rows, columns(3)]
        )
    aggregated[...] = wide[...].astype(bf16)
    moves.leave(aggregated)
    modulator[...] = nn(aggregated[...], h_weight[...]) + small[H_BIAS : H_BIAS + 1, :]

    moves.leave(modulator)

    def mix(rows, carry):
        mixed[rows, :] = (query[rows, :] * modulator[rows, :]).astype(bf16)
        return carry

    blocks(shape, mix, 0)
    moves.leave(mixed)
    middle[...] = (
        inputs[...] + nn(mixed[...], proj_weight[...]) + small[PROJ_BIAS : PROJ_BIAS + 1, :]
    )
    moves.leave(middle)
    gain = small[LN2_GAIN : LN2_GAIN + 1, :]
    bias = small[LN2_BIAS : LN2_BIAS + 1, :]

    def second_norm(rows, carry):
        unit, _ = normalise(middle[rows, :])
        normed_two[rows, :] = (unit * gain + bias).astype(bf16)
        return carry

    blocks(shape, second_norm, 0)


class Moves:
    def __init__(self):
        self.incoming, self.outgoing = {}, {}
        self.started, self.free = [], []

    def copy(self, source, target):
        move = pltpu.make_async_copy(source, target, self.free.pop())
        move.start()
        self.started.append(move)

    def arrive(self, *buffers):
        for buffer in buffers:
            move = self.incoming.pop(id(buffer), None)
            if move is not None:
                move.wait()

    def leave(self, *buffers):
        for buffer in buffers:
            move = self.outgoing.pop(id(buffer), None)
            if move is not None:
                move.start()
                self.started.append(move)

    def finish(self):
        for move in list(self.incoming.values()):
            move.wait()
        for move in list(self.outgoing.values()):
            move.start()
            self.started.append(move)
        for move in self.started:
            move.wait()


def with_moves(kernel, far_in, far_out, extra):
    def run(*refs):
        refs = list(refs)
        ins, refs = refs[: len(far_in)], refs[len(far_in) :]
        outs, refs = refs[: len(far_out)], refs[len(far_out) :]
        semaphores = refs.pop()
        count = sum(far_in) + sum(far_out)
        buffers, scratch = refs[len(refs) - count :], refs[: len(refs) - count]
        moves = Moves()
        moves.free = [semaphores.at[count + spare] for spare in range(extra)]
        index = 0
        for group, flags, table in (
            (ins, far_in, moves.incoming),
            (outs, far_out, moves.outgoing),
        ):
            for place, far in enumerate(flags):
                if far:
                    buffer, outer = buffers[index], group[place]
                    pair = (outer, buffer) if group is ins else (buffer, outer)
                    move = pltpu.make_async_copy(*pair, semaphores.at[index])
                    if group is ins:
                        move.start()
                    table[id(buffer)] = move
                    group[place] = buffer
                    index += 1
        kernel(moves, *ins, *outs, *scratch)
        moves.finish()

    return run


class Units:
    def __init__(self, shards, unit):
        self.shards, self.unit = shards, unit
        self.piece_rows = 2 * unit + 16
        self.feed_rows = 2 * unit
        self.total = shards * unit
        self.head_rows, self.late_rows = 40, 16
        self.pieces = 2 * shards
        self.share = self.head_rows + self.late_rows
        self.head_total = 2 * self.pieces * self.head_rows
        self.late_total = 2 * self.pieces * self.late_rows


def sum_kernel(parts, source, out):
    size = out.shape[0]
    block = 16 if size % 16 == 0 else size

    def step(index, carry):
        rows = pl.ds(pl.multiple_of(index * block, block), block)
        total = source[0, rows, :].astype(f32)
        for part in range(1, parts):
            total = total + source[part, rows, :].astype(f32)
        out[rows, :] = total.astype(bf16)
        return carry

    lax.fori_loop(0, size // block, step, 0)


def pair_kernel(first, second, out):
    for part in range(out.shape[0]):
        total = first[part].astype(f32) + second[part].astype(f32)
        out[part] = total.astype(bf16)


def rows_kernel(shape, moves, first, second, arrived, first_out, second_out):
    def step(index, carry):
        rows = pl.ds(pl.multiple_of(index * 16, 16), 16)
        more = pl.ds(pl.multiple_of(index * 16 + shape.rows, 16), 16)
        first_out[rows, :] = (first[rows, :].astype(f32) + arrived[rows, :].astype(f32)).astype(bf16)
        second_out[rows, :] = (second[rows, :].astype(f32) + arrived[more, :].astype(f32)).astype(
            bf16
        )
        return carry

    lax.fori_loop(0, shape.rows // 16, step, 0)


def share_kernel(head_parts, late_parts, out):
    sums = []
    for parts in (head_parts, late_parts):
        total = parts[0].astype(f32)
        for part in range(1, parts.shape[0]):
            total = total + parts[part].astype(f32)
        sums.append(total)
    share = jnp.concatenate(sums).astype(bf16)
    for copy in range(out.shape[0]):
        out[copy] = share


def piece_kernel(units, copies, spots, first, second, far_bias, out, own, bias, semaphores):
    unit = units.unit
    width = first.shape[1]
    rows = pl.ds(pl.multiple_of(spots[0] * unit, 16), unit)
    moves = [
        pltpu.make_async_copy(source.at[rows, :], own.at[index], semaphores.at[index])
        for index, source in enumerate((first, second))
    ]
    moves.insert(0, pltpu.make_async_copy(far_bias, bias, semaphores.at[2]))
    for move in moves:
        move.start()
    moves.pop(0).wait()
    shard = spots[1]
    values = bias[...].astype(f32).reshape(1, bias.shape[0])
    values = jnp.concatenate([values, jnp.zeros((1, width - bias.shape[0]), f32)], axis=1)
    values = pltpu.roll(jnp.broadcast_to(values, (8, width)), spots[2], 1)
    lane = lax.broadcasted_iota(jnp.int32, (8, width), 1) - shard * unit
    row = lax.broadcasted_iota(jnp.int32, (8, width), 0)
    values = jnp.where((lane >= 0) & (lane < unit) & (row == 0), values, 0.0)
    line = jnp.concatenate([values, jnp.zeros((8, width), f32)]).astype(bf16)
    for move in moves:
        move.wait()
    for copy in range(copies):
        base = copy * units.piece_rows
        out[base : base + unit, :] = own[0]
        out[base + unit : base + 2 * unit, :] = own[1]
        out[base + 2 * unit : base + units.piece_rows, :] = line


def feed_kernel(shape, units, resumed, moves, weights, *refs):
    refs = list(refs)

    def take(count):
        taken = refs[:count]
        del refs[:count]
        return taken

    groups = 1 if resumed is None else 2
    closing = resumed is not False
    normed, cots = take(groups), take(groups)
    if resumed:
        old_grads, old_bias, *near = take(6)
    if resumed:
        out, d_out, both = take(3)
        outs = [out, both.at[shape.rows : 2 * shape.rows, :]]
        d_outs = [d_out, both.at[0 : shape.rows, :]]
        d_near, out_near = take(2)
    else:
        outs, d_outs = take(groups), take(groups)
    grads, bias_grad = take(2)
    first_weight, second_weight, total_grads, total_bias = take(4)
    unit, width = units.unit, shape.width
    bias = None
    for shard in range(units.shards):
        base, here = shard * units.piece_rows, shard * unit
        first_weight[here : here + unit, :] = weights[base : base + unit, :]
        second_weight[here : here + unit, :] = weights[base + unit : base + 2 * unit, :]
        term = weights[base + 2 * unit : base + units.piece_rows, :].astype(f32)
        bias = term if bias is None else bias + term
    bias = bias[0:1]
    if resumed:
        moves.arrive(*near)
        for target, own, arrived in ((d_near, near[0], near[1]), (out_near, near[2], near[3])):
            target[...] = own[...].astype(f32) + arrived[...].astype(f32)
            moves.leave(target)
    for group in range(groups):
        moves.arrive(normed[group], cots[group])
        rows, cot = normed[group], cots[group]
        value, rise = gelu_pair(nt(rows[...], first_weight[...]) + bias)
        hidden = value.astype(bf16)
        outs[group][...] = nn(hidden, second_weight[...]).astype(bf16)
        d_before = (nt(cot[...], second_weight[...]) * rise).astype(bf16)
        d_outs[group][...] = nn(d_before, first_weight[...]).astype(bf16)
        moves.leave(outs[group], d_outs[group])
        first, second = tn(d_before, rows[...]), tn(hidden, cot[...])
        line = fold(d_before.astype(f32))
        if group == 0 and not resumed:
            total_grads[0 : units.total, :] = first
            total_grads[units.total :, :] = second
            total_bias[...] = line
        elif group == 0:
            total_grads[0 : units.total, :] = old_grads[0 : units.total, :] + first
            total_grads[units.total :, :] = old_grads[units.total :, :] + second
            total_bias[...] = old_bias[...] + line
        else:
            total_grads[0 : units.total, :] += first
            total_grads[units.total :, :] += second
            total_bias[...] += line
    if not closing:
        grads[...] = total_grads[...]
        bias_grad[...] = total_bias[...]
        return
    bias_grad[...] = total_bias[...]
    for shard in range(units.shards):
        base, here = shard * units.feed_rows, shard * unit
        more = units.total + here
        grads[base : base + units.feed_rows, :] = jnp.concatenate(
            [total_grads[here : here + unit, :], total_grads[more : more + unit, :]]
        ).astype(bf16)


def heads_kernel(
    shape,
    units,
    moves,
    core,
    small,
    cot,
    middle,
    d_near,
    d_far,
    bias_grads,
    proj_weight,
    query,
    modulator,
    h_weight,
    normed,
    aggregated,
    mixed,
    *refs,
):
    later, refs = refs[:9], refs[9:]
    d_middle, d_query, d_aggregated, own_rest, other_rest, *refs = refs
    fetched, refs = refs[:9], refs[9:]
    heads_body(
        shape,
        units,
        moves,
        core,
        small,
        cot,
        middle,
        d_near,
        d_far,
        bias_grads,
        proj_weight,
        query,
        modulator,
        h_weight,
        normed,
        aggregated,
        mixed,
        list(zip(later, fetched)),
        d_middle,
        d_query,
        d_aggregated,
        own_rest,
        other_rest,
        *refs,
    )


def heads_body(
    shape,
    units,
    moves,
    core,
    small,
    cot,
    middle,
    d_near,
    d_far,
    bias_grads,
    proj_weight,
    query,
    modulator,
    h_weight,
    normed,
    aggregated,
    mixed,
    later,
    d_middle,
    d_query,
    d_aggregated,
    own_rest,
    other_rest,
    d_mixed,
    d_modulator,
    head,
    d_branch,
):
    width = shape.width
    zero = jnp.zeros((8, width), f32)
    moves.arrive(small, cot, middle, d_near)
    for source, target in later:
        moves.copy(source, target)
    gain = small[LN2_GAIN : LN2_GAIN + 1, :]

    def second_norm(rows, carry):
        grads = d_near[rows, :] + d_far[rows, :].astype(f32)
        cots = cot[rows, :].astype(f32)
        d_input, d_gain = norm_back(middle[rows, :], grads, gain)
        d_total = cots + d_input
        d_middle[rows, :] = d_total
        rounded = d_total.astype(bf16)
        d_branch[rows, :] = rounded
        added = (d_gain, grads, rounded.astype(f32), cots)
        return tuple(total + fold(item) for total, item in zip(carry, added))

    d_gain, d_bias, proj_bias, out_bias = blocks(shape, second_norm, (zero,) * 4)
    moves.leave(d_middle)
    moves.arrive(proj_weight)
    d_mixed[...] = nt(d_branch[...], proj_weight[...])
    moves.arrive(query, modulator)

    def split(rows, carry):
        values = d_mixed[rows, :]
        for_query = (values * modulator[rows, :]).astype(bf16)
        for_modulator = (values * query[rows, :]).astype(bf16)
        d_query[rows, :] = for_query
        d_modulator[rows, :] = for_modulator
        return carry[0] + fold(for_query.astype(f32)), carry[1] + fold(for_modulator.astype(f32))

    query_bias, h_bias = blocks(shape, split, (zero, zero))
    moves.leave(d_query)
    moves.arrive(h_weight)
    d_aggregated[...] = nt(d_modulator[...], h_weight[...])
    moves.leave(d_aggregated)
    moves.arrive(normed, aggregated, mixed)
    head[0:width, :] = tn(d_query[...], normed[...])
    head[width : 2 * width, :] = tn(aggregated[...], d_modulator[...])
    head[2 * width : 3 * width, :] = tn(mixed[...], d_branch[...])
    sums = (h_bias, proj_bias, d_gain, d_bias, out_bias, query_bias)
    head[3 * width :, :] = jnp.concatenate(
        [row_sum(item) for item in sums]
        + [jnp.zeros((2, width), f32)]
        + [row_sum(bias_grads[8 * index : 8 * index + 8, :]) for index in range(4)]
        + [jnp.zeros((units.head_total - 3 * width - 12, width), f32)]
    )
    for half, target in enumerate((own_rest, other_rest)):
        absolute = jnp.bitwise_xor(core[0], half)
        for piece in range(units.pieces):
            first = (absolute * units.pieces + piece) * units.head_rows
            target[piece] = head[pl.ds(pl.multiple_of(first, 8), units.head_rows), :].astype(bf16)


def levels_back_kernel(
    shape,
    moves,
    small,
    gates,
    d_aggregated,
    pooled,
    slope_three,
    slope_two,
    slope_one,
    one,
    two,
    three,
    d_one,
    d_two,
    d_three,
    rounded,
    d_gates,
    tap_ref,
    d_levels,
    products,
    d_context,
):
    width = shape.width
    inner = shape.inner
    moves.arrive(small)
    spread_taps(shape, small, tap_ref)
    for ref in (d_one, d_two, d_three):
        clear_edges(shape, ref)
    moves.arrive(gates, d_aggregated, pooled)
    pool_grad = [None] * sublanes
    for image in range(shape.images):
        rows = pl.ds(image * shape.segment, shape.segment)
        for tile in range(shape.tiles):
            slot = tile * shape.images + image
            values = d_aggregated[rows, columns(tile)]
            for level in range(3):
                d_levels[pl.ds(level * inner + slot, shape.patches, stride=sublanes), :] = (
                    values[: shape.patches] * gates[rows, columns(level)][: shape.patches]
                )
            pool_grad[slot] = jnp.sum(values * gates[rows, columns(3)], axis=0, keepdims=True)
    blank = jnp.zeros((1, lanes), f32)
    pool_grad = jnp.concatenate([blank if item is None else item for item in pool_grad])
    pool_grad = pool_grad * pooled[sublanes : 2 * sublanes, :]
    wide_pool = jnp.concatenate([pool_grad] * shape.side)

    def third(line, carry):
        here = pl.multiple_of(line * shape.line, shape.line)
        value = (d_levels[pl.ds(2 * inner + here, shape.line), :] + wide_pool) * slope_three[
            pl.ds(here, shape.line), :
        ]
        d_three[pl.ds(here + shape.centre, shape.line), :] = value
        return carry

    moves.arrive(slope_three)
    lax.fori_loop(0, shape.side, third, 0)
    moves.leave(d_three)
    moves.arrive(slope_two, slope_one)
    for level, source, target, slope in ((2, d_three, d_two, slope_two), (1, d_two, d_one, slope_one)):

        def back(line, carry, level=level, source=source, target=target, slope=slope):
            here = pl.multiple_of(line * shape.line, shape.line)
            value = correlate(shape, source, tap_ref, level, line, True)
            value = (value + d_levels[pl.ds((level - 1) * inner + here, shape.line), :]) * slope[
                pl.ds(here, shape.line), :
            ]
            target[pl.ds(here + shape.centre, shape.line), :] = value
            return carry

        lax.fori_loop(0, shape.side, back, 0)
        moves.leave(target)

    def back_context(line, carry):
        here = pl.multiple_of(line * shape.line, shape.line)
        d_levels[pl.ds(here, shape.line), :] = correlate(shape, d_one, tap_ref, 0, line, True)
        return carry

    lax.fori_loop(0, shape.side, back_context, 0)
    for image, tile, slot in shape.places():
        first = image * shape.segment
        d_context[first : first + shape.patches, columns(tile)] = d_levels[
            pl.ds(slot, shape.patches, stride=sublanes), :
        ]
        if tile == 0 and shape.segment > shape.patches:
            d_context[first + shape.patches : first + shape.segment, :] = jnp.zeros(
                (shape.segment - shape.patches, width), f32
            )
    rounded[...] = d_context[...].astype(bf16)
    moves.leave(rounded)
    moves.arrive(one, two, three)
    for image in range(shape.images):
        rows = pl.ds(image * shape.segment, shape.segment)
        totals = [None] * 4
        for tile in range(shape.tiles):
            slot = tile * shape.images + image
            values = d_aggregated[rows, columns(tile)]
            for level, ref in enumerate((one, two, three)):
                term = values * level_rows(shape, ref, image, slot)
                totals[level] = term if tile == 0 else totals[level] + term
            term = values * pooled[slot : slot + 1, :]
            totals[3] = term if tile == 0 else totals[3] + term
        for gate in range(4):
            products[rows, columns(gate)] = totals[gate]
    chooser = (
        lax.broadcasted_iota(jnp.int32, (4 * lanes, lanes), 0) // lanes
        == lax.broadcasted_iota(jnp.int32, (4 * lanes, lanes), 1)
    ).astype(f32).astype(bf16)
    d_gates[...] = nn(products[...].astype(bf16), chooser).astype(bf16)


def exit_kernel(
    shape,
    units,
    moves,
    core,
    two,
    d_three,
    one,
    d_two,
    context,
    d_one,
    rounded,
    d_gates,
    small,
    normed,
    f_turned,
    d_query,
    tokens,
    d_inputs,
    own_late,
    other_late,
    packed,
    tap_grad,
    inputs,
    d_context,
    gathered,
    gate_rows,
):
    width = shape.width
    moves.arrive(two, d_three)
    tap_grads(shape, two, d_three, 2, tap_grad)
    moves.arrive(one, d_two)
    tap_grads(shape, one, d_two, 1, tap_grad)
    moves.arrive(context, d_one)
    tap_grads(shape, context, d_one, 0, tap_grad)
    moves.arrive(rounded, d_gates, small, normed, f_turned, d_query, tokens)
    gathered[0:width, :] = tn(rounded[...], normed[...])
    gathered[width : width + 8, :] = tn(d_gates[...], normed[...])[0:8]
    for tile in range(shape.tiles):
        total = None
        for image in range(shape.images):
            slot = tile * shape.images + image
            term = tap_grad[pl.ds(slot, taps, stride=sublanes), :]
            total = term if total is None else total + term
        gathered[width + 8 : width + 8 + taps, columns(tile)] = total
    gate_rows[...] = jnp.concatenate(
        [
            f_turned[2 * width : 2 * width + 4, :].astype(f32),
            jnp.zeros((lanes - 4, width), f32),
        ]
    ).astype(bf16)
    d_normed = d_context
    gate_bias = row_sum(fold(d_gates[...].astype(f32)))
    context_bias = row_sum(fold(rounded[...].astype(f32)))
    d_normed[...] = (
        nn(d_query[...], f_turned[0:width, :])
        + nn(rounded[...], f_turned[width : 2 * width, :])
        + nn(d_gates[...], gate_rows[...])
    )
    packed[...] = tokens[...].astype(f32)
    unpack(shape, packed, inputs)
    gain = small[LN1_GAIN : LN1_GAIN + 1, :]
    zero = jnp.zeros((8, width), f32)

    def finish(rows, carry):
        values = d_normed[rows, :]
        d_input, d_gain = norm_back(inputs[rows, :], values, gain)
        d_inputs[rows, :] = d_input
        return carry[0] + fold(d_gain), carry[1] + fold(values)

    d_gain, d_bias = blocks(shape, finish, (zero, zero))
    moves.leave(d_inputs)
    last = width + 8 + taps
    rest = units.late_total - last - 4
    gathered[last:, :] = jnp.concatenate(
        [
            row_sum(d_gain),
            row_sum(d_bias),
            context_bias,
            jnp.concatenate([gate_bias, jnp.zeros((1, width - lanes), f32)], axis=1),
            jnp.zeros((rest, width), f32),
        ]
    )
    for half, target in enumerate((own_late, other_late)):
        absolute = jnp.bitwise_xor(core[0], half)
        for piece in range(units.pieces):
            first = (absolute * units.pieces + piece) * units.late_rows
            target[piece] = gathered[
                pl.ds(pl.multiple_of(first, 16), units.late_rows), :
            ].astype(bf16)


def finish_kernel(
    shape,
    moves,
    d_middle,
    d_inputs,
    small,
    middle,
    out_near,
    out_far,
    tokens_grad,
    block_out,
    rows_ref,
):
    moves.arrive(d_middle, d_inputs)

    def add_grads(rows, carry):
        rows_ref[rows, :] = d_middle[rows, :] + d_inputs[rows, :]
        return carry

    blocks(shape, add_grads, 0)
    pack(shape, rows_ref, tokens_grad)
    moves.leave(tokens_grad)
    moves.arrive(small, middle, out_near, out_far)

    def add_outs(rows, carry):
        total = middle[rows, :] + small[FC2_BIAS : FC2_BIAS + 1, :]
        rows_ref[rows, :] = total + out_near[rows, :] + out_far[rows, :].astype(f32)
        return carry

    blocks(shape, add_outs, 0)
    pack(shape, rows_ref, block_out)


def unpack_kernel(
    shape,
    units,
    spots,
    piece,
    piece_x,
    piece_core,
    piece_both,
    own,
    own_b,
    own_x,
    own_both,
    core_own,
    core_b,
    core_x,
    core_both,
    ln1_gain,
    ln1_bias,
    f_grad,
    f_bias,
    small_grad,
    middle_grad,
    large_grad,
    h_grad,
    h_bias,
    proj_grad,
    proj_bias,
    ln2_gain,
    ln2_bias,
    first_grad,
    first_bias,
    second_grad,
    second_bias,
    held,
    head,
    late,
):
    width = shape.width
    unit = units.unit
    size = own.shape[0]
    parts = (own, own_b, own_x, own_both, core_own, core_b, core_x, core_both)
    for index, part in enumerate(parts):
        held[index * size : (index + 1) * size, :] = part[...].astype(f32)
    core, shift = spots[0], spots[2]
    far = units.shards // 2
    for half in range(2):
        for place in range(2):
            for close in range(2):
                slot = jnp.bitwise_xor(core, half) * 4 + jnp.bitwise_xor(spots[3], place) * 2
                base = (slot + jnp.bitwise_xor(spots[4], close)) * size
                to = (half * 2 + place) * 2 + close
                rows = far * units.head_rows
                head[to * rows : (to + 1) * rows, :] = held[
                    pl.ds(pl.multiple_of(base, 8), rows), :
                ]
                first = pl.multiple_of(base + rows, 8)
                rows = far * units.late_rows
                late[to * rows : (to + 1) * rows, :] = held[pl.ds(first, rows), :]
    total = None
    lane = lax.broadcasted_iota(jnp.int32, (8, width), 1)
    for index, source in enumerate((piece, piece_core, piece_x, piece_both)):
        quarter = jnp.bitwise_xor(spots[1], index)
        to = pl.ds(pl.multiple_of(quarter * unit, 8), unit)
        first_grad[to, :] = source[0:unit, :].astype(f32)
        second_grad[to, :] = source[unit : 2 * unit, :].astype(f32)
    for quarter in range(4):
        row = head[3 * width + 8 + quarter : 3 * width + 9 + quarter, :]
        moved = shift + quarter * unit
        moved = jnp.where(moved >= width, moved - width, moved)
        row = pltpu.roll(jnp.broadcast_to(row, (8, width)), moved, 1)
        row = jnp.where((lane >= quarter * unit) & (lane < (quarter + 1) * unit), row, 0.0)
        total = row if total is None else total + row
    first_bias[...] = total[0:1, 0 : first_bias.shape[0]].reshape(first_bias.shape)
    f_grad[0:width, :] = head[0:width, :]
    f_grad[width : 2 * width + 4, :] = late[0 : width + 4, :]
    h_grad[...] = head[width : 2 * width, :]
    proj_grad[...] = head[2 * width : 3 * width, :]
    first = width + 8
    small_grad[...] = late[first : first + 9, :]
    middle_grad[...] = late[first + 9 : first + 34, :]
    large_grad[...] = late[first + 34 : first + taps, :]
    first = first + taps
    for out, source, row in (
        (h_bias, head, 3 * width),
        (proj_bias, head, 3 * width + 1),
        (ln2_gain, head, 3 * width + 2),
        (ln2_bias, head, 3 * width + 3),
        (second_bias, head, 3 * width + 4),
        (ln1_gain, late, first),
        (ln1_bias, late, first + 1),
    ):
        out[...] = source[row : row + 1, :].reshape(width)
    f_bias[0:width] = head[3 * width + 5 : 3 * width + 6, :].reshape(width)
    f_bias[width : 2 * width] = late[first + 2 : first + 3, :].reshape(width)
    f_bias[2 * width : 2 * width + 4] = late[first + 3 : first + 4, 0:4].reshape(4)


def call(kernel, name, outs, scratch, micros, room, *operands):
    spec = pl.BlockSpec(memory_space=pltpu.VMEM)
    outer = pl.BlockSpec(memory_space=pltpu.HBM)
    far_in = [isinstance(item, Far) for item in operands]
    far_out = [isinstance(item, Far) for item in outs]
    anywhere = [isinstance(item, Anywhere) for item in operands]
    raw = [isinstance(item, Raw) for item in operands]
    operands = [item.value if far else item for item, far in zip(operands, far_in)]
    operands = [
        pltpu.with_memory_space_constraint(item, pltpu.HBM) if far and not free else item
        for item, far, free in zip(operands, far_in, anywhere)
    ]
    raw_out = [isinstance(item, Raw) for item in outs]
    outs = [
        pltpu.HBM(item.value.shape, item.value.dtype) if far else item
        for item, far in zip(outs, far_out)
    ]
    specs = []
    for item, far, free in zip(operands, far_in, anywhere):
        if free:
            specs.append(pl.BlockSpec(memory_space=pl.ANY))
        elif item.dtype == jnp.int32:
            specs.append(pl.BlockSpec(memory_space=pltpu.SMEM))
        else:
            specs.append(outer if far else spec)
    out_specs = [outer if far else spec for far in far_out]
    if name not in plain:
        far_in = [far and not own for far, own in zip(far_in, raw)]
        far_out = [far and not own for far, own in zip(far_out, raw_out)]
        pairs = list(zip(operands, far_in)) + list(zip(outs, far_out))
        buffers = [pltpu.VMEM(item.shape, item.dtype) for item, far in pairs if far]
        extra = sum(raw) + sum(raw_out)
        semaphores = pltpu.SemaphoreType.DMA((max(len(buffers) + extra, 1),))
        scratch = list(scratch) + buffers + [semaphores]
        kernel = with_moves(kernel, far_in, far_out, extra)
    moved = sum(item.size * item.dtype.itemsize for item in operands)
    return pl.pallas_call(
        kernel,
        name=name,
        out_shape=outs,
        in_specs=specs,
        out_specs=out_specs,
        scratch_shapes=scratch,
        compiler_params=pltpu.CompilerParams(vmem_limit_bytes=room * 1024 * 1024),
        cost_estimate=pl.CostEstimate(
            flops=int(micros * 1.1e9), bytes_accessed=moved, transcendentals=0
        ),
    )(*operands)


plain = ("piece", "sum", "pair", "share", "unpack")


class Far:
    def __init__(self, value):
        self.value = value


class Anywhere(Far):
    pass


class Raw(Far):
    pass


def far_array(*dims, kind=jnp.float32):
    return Far(array(*dims, kind=kind))


def array(*dims, kind=jnp.float32):
    return jax.ShapeDtypeStruct(dims, kind)


def to_packed(values, shape):
    moved = with_layout_constraint(values.transpose(1, 2, 0, 3), Layout((0, 1, 2, 3)))
    moved = moved.reshape(shape.patches, shape.images, shape.tiles, lanes)
    moved = with_layout_constraint(moved, Layout((0, 2, 1, 3)))
    return moved.transpose(0, 2, 1, 3).reshape(shape.packed, lanes)


def from_packed(values, shape):
    moved = values.reshape(shape.patches, shape.tiles, shape.images, lanes).transpose(0, 2, 1, 3)
    moved = moved.reshape(shape.side, shape.side, shape.images, shape.width)
    return moved.transpose(2, 0, 1, 3)


everyone = ("x", "core", "a", "b")


def gather_plainly(units, first, bias, second):
    first = lax.all_gather(first, ("a", "b"), axis=0, tiled=True)
    second = lax.all_gather(second, ("a", "b"), axis=0, tiled=True)
    bias = lax.all_gather(bias, ("a", "b"), axis=0, tiled=True)
    width = first.shape[1]
    rows = jnp.pad(bias.reshape(4, 1, 1, width), ((0, 0), (0, units.shards - 1), (0, 15), (0, 0)))
    shape = (4, units.shards, units.unit, width)
    both = jnp.concatenate([first.reshape(shape), second.reshape(shape), rows], axis=2)
    both = both.reshape(4, units.shards * units.piece_rows, width)
    return [both[index] for index in range(4)]


def total_of(values, parts):
    rows = values.shape[0] // parts
    kernel = functools.partial(sum_kernel, parts)
    values = values.reshape(parts, rows, values.shape[1])
    return call(kernel, "sum", [array(rows, values.shape[2], kind=bf16)], [], 1, 4, values)[0]


def reduce_plainly(shape, units, feed, rest, late):
    width = shape.width
    unit = units.unit
    both = jnp.stack(feed).reshape(4, units.shards, units.feed_rows, width)
    first = both[:, :, :unit].reshape(4 * units.total, width)
    second = both[:, :, unit:].reshape(4 * units.total, width)

    def shared(values):
        part = lax.psum_scatter(values, ("a", "b"), scatter_dimension=0, tiled=True)
        return lax.psum(part, ("x", "core")).astype(f32)

    late = jnp.concatenate(late).reshape(units.late_total, width)
    late = lax.psum(late, everyone).astype(f32)
    head = jnp.concatenate(rest).reshape(units.head_total, width)
    head = lax.psum(head, everyone).astype(f32)
    bias = head[3 * width + 8 : 3 * width + 12].reshape(-1)
    place = lax.axis_index("a") * 2 + lax.axis_index("b")
    size = bias.shape[0] // (lax.axis_size("a") * 2)
    bias = lax.dynamic_slice_in_dim(bias, place * size, size, 0)
    last = width + 8
    vectors = head[3 * width : 3 * width + 8]
    more = late[last + taps : last + taps + 4]
    return (
        more[0],
        more[1],
        jnp.concatenate([head[:width], late[: width + 4]]),
        jnp.concatenate([vectors[5], more[2], more[3, :4]]),
        late[last : last + 9],
        late[last + 9 : last + 34],
        late[last + 34 : last + taps],
        head[width : 2 * width],
        vectors[0],
        head[2 * width : 3 * width],
        vectors[1],
        vectors[2],
        vectors[3],
        shared(first),
        bias,
        shared(second),
        vectors[4],
    )


def shards(
    sizes,
    tokens,
    ln1_gain,
    ln1_bias,
    f_weight,
    f_bias,
    dw_small,
    dw_middle,
    dw_large,
    h_weight,
    h_bias,
    proj_weight,
    proj_bias,
    ln2_gain,
    ln2_bias,
    fc1_weight,
    fc1_bias,
    fc2_weight,
    fc2_bias,
    out_grad,
):
    images, side, _, width = tokens.shape
    shape = Shape(images, side, width)
    rows, grid, inner = shape.rows, shape.grid, shape.inner
    hidden = fc1_weight.shape[1] * sizes["a"] * sizes["b"]
    quick = sizes["x"] == 2 and sizes["a"] * sizes["b"] == 8
    units = Units(8, hidden // 32)
    f_turned = f_weight.T
    first, second = fc1_weight.T, fc2_weight
    scratch = pltpu.VMEM
    core = jnp.zeros((1,), jnp.int32)
    if quick:
        core = lax.axis_index("core").astype(jnp.int32).reshape(1)
        quarter = lax.axis_index("x") * 2 + core[0]
        shard = lax.axis_index("a") * 2 + lax.axis_index("b")
        turn = lax.rem(shard - quarter + units.shards, units.shards) * units.unit
        spots = jnp.stack([quarter, shard, turn]).astype(jnp.int32)
        (pieces,) = call(
            functools.partial(piece_kernel, units, units.shards),
            "piece",
            [array(units.shards * units.piece_rows, width, kind=bf16)],
            [
                scratch((2, units.unit, width), bf16),
                scratch(fc1_bias.shape, bf16),
                pltpu.SemaphoreType.DMA((3,)),
            ],
            1,
            6,
            spots,
            Far(first),
            Far(second),
            Far(fc1_bias),
        )
        weights = exchange(pieces, ("a", "b"))
    tokens_packed = to_packed(tokens, shape)

    def rows_array(kind=bf16):
        return far_array(rows, width, kind=kind)

    small, cot, inputs, normed, query, gates, context, one, slope_one = call(
        functools.partial(entry_kernel, shape),
        "entry",
        [
            far_array(96, width),
            rows_array(),
            array(rows, width),
            rows_array(),
            array(rows, width),
            array(rows, 4 * lanes),
            far_array(grid, lanes),
            array(grid, lanes),
            array(inner, lanes),
        ],
        [
            scratch((taps * sublanes, lanes), f32),
            scratch((shape.packed, lanes), f32),
            scratch((rows, width), f32),
        ],
        5,
        16,
        tokens_packed,
        f_turned,
        to_packed(out_grad, shape),
        dw_small,
        dw_middle,
        dw_large,
        ln1_gain,
        ln1_bias,
        f_bias,
        h_bias,
        proj_bias,
        ln2_gain,
        ln2_bias,
        fc2_bias,
    )
    if quick:
        cot_far = flip(cot, "x")
        cot_core = flip(cot)
    one, gates, query, slope_one, *results = call(
        functools.partial(modulation_kernel, shape),
        "modulation",
        [
            Raw(array(grid, lanes)),
            Raw(array(rows, 4 * lanes)),
            Raw(array(rows, width)),
            Raw(array(inner, lanes)),
            rows_array(f32),
            rows_array(),
            rows_array(),
            rows_array(f32),
            rows_array(),
            far_array(grid, lanes),
            far_array(grid, lanes),
            far_array(inner, lanes),
            far_array(inner, lanes),
            far_array(2 * sublanes, lanes),
        ],
        [scratch((rows, width), f32), scratch((taps * sublanes, lanes), f32)],
        8,
        20,
        one,
        Far(small),
        gates,
        Far(h_weight),
        query,
        inputs,
        Far(proj_weight),
        slope_one,
    )
    modulator, aggregated, mixed, middle, normed_two, *results = results
    two, three, slope_two, slope_three, pooled = results

    def feed(resumed, outs, *operands):
        return call(
            functools.partial(feed_kernel, shape, units, resumed),
            "feed",
            outs,
            [
                scratch((units.total, width), bf16),
                scratch((units.total, width), bf16),
                scratch((2 * units.total, width), f32),
                scratch((8, width), f32),
            ],
            6,
            24,
            *operands,
        )

    near_rows = array(rows, width, kind=bf16)
    feed_total = array(units.shards * units.feed_rows, width, kind=bf16)
    bias_total = array(8, width)
    if quick:
        cot_both = flip(after(cot_far, middle))
        normed_far = flip(normed_two, "x")
        normed_core = flip(normed_two)
        out_own, out_core, d_own, d_core, *carry = feed(
            False,
            [near_rows] * 4 + [array(2 * units.total, width), bias_total],
            weights,
            Far(normed_two),
            normed_core,
            Far(cot),
            cot_core,
        )
        out_core, d_core = flip(out_core), flip(d_core)
        normed_far = after(normed_far, d_own)
        normed_both = flip(normed_far)
        out_far, d_far, both, d_near, out_near, feed_grads, bias_grad = feed(
            True,
            [near_rows] * 2
            + [array(2 * rows, width, kind=bf16), rows_array(f32), rows_array(f32), feed_total]
            + [bias_total],
            weights,
            normed_far,
            normed_both,
            cot_far,
            cot_both,
            *carry,
            d_own,
            d_core,
            out_own,
            out_core,
        )
        arrived = flip(both)
        d_far, out_far = call(
            functools.partial(rows_kernel, shape),
            "rows",
            [near_rows, rows_array()],
            [],
            1,
            8,
            d_far,
            out_far,
            arrived,
        )
        feed_grads = after(feed_grads, d_far)
        d_far = flip(d_far, "x")
        feed_parts = exchange(feed_grads, ("a", "b"))
        mine = (jnp.arange(4) == quarter).astype(f32)
        bias_grads = (mine[:, None, None] * bias_grad).reshape(32, width)
    else:
        out_far = d_far = jnp.zeros((rows, width), bf16)
        out_near, d_near, feed_grads, bias_grads = jnp.zeros((rows, width), f32), 0.0, [], []
        for weights in gather_plainly(units, first, fc1_bias, second):
            out, d_out, grads, bias_grad = feed(
                None, [near_rows, near_rows, feed_total, bias_total], weights, normed_two, cot
            )
            bias_grads.append(bias_grad)
            out_near, d_near = out_near + out.astype(f32), d_near + d_out.astype(f32)
            feed_grads.append(grads)
        bias_grads = jnp.concatenate(bias_grads)
    rest = array(units.pieces, units.head_rows, width, kind=bf16)
    later = [small, gates, pooled, slope_three, slope_two, slope_one, one, two, three]
    d_middle, d_query, d_aggregated, own_rest, other_rest, *fetched = call(
        functools.partial(heads_kernel, shape, units),
        "heads",
        [rows_array(f32), rows_array(), array(rows, width), rest, rest]
        + [array(*item.shape) for item in later],
        [
            scratch((rows, width), f32),
            scratch((rows, width), bf16),
            scratch((units.head_total, width), f32),
            scratch((rows, width), bf16),
        ],
        5,
        16,
        core,
        Far(small),
        Far(cot),
        Far(middle),
        Far(d_near),
        d_far,
        bias_grads,
        Far(proj_weight),
        Far(query),
        Far(modulator),
        Far(h_weight),
        Far(normed),
        Far(aggregated),
        Far(mixed),
        *[Raw(item) for item in later],
    )
    if quick:
        out_far = flip(after(out_far, d_middle), "x")
        rest_arrived = flip(other_rest)
    d_one, d_two, d_three, rounded, d_gates = call(
        functools.partial(levels_back_kernel, shape),
        "levels_back",
        [
            far_array(grid, lanes),
            far_array(grid, lanes),
            far_array(grid, lanes),
            rows_array(),
            far_array(rows, lanes, kind=bf16),
        ],
        [
            scratch((taps * sublanes, lanes), f32),
            scratch((3 * inner, lanes), f32),
            scratch((rows, 4 * lanes), f32),
            scratch((rows, width), f32),
        ],
        8,
        24,
        fetched[0],
        fetched[1],
        d_aggregated,
        *fetched[2:],
    )
    if quick:
        (rest_half,) = call(pair_kernel, "pair", [rest], [], 1, 4, own_rest, rest_arrived)
        feed_parts = after(feed_parts, d_one)
        piece = total_of(feed_parts, units.shards)
        rest_half = after(rest_half, piece)
        d_one = after(d_one, rest_half, out_far)
        shares = rest_half.shape
        rest_parts = exchange(rest_half.reshape(-1, width), ("x", "b"))
        rest_parts = rest_parts.reshape(4, shares[0] * shares[1] // 4, width)
    late = array(units.pieces, units.late_rows, width, kind=bf16)
    d_inputs, own_late, other_late = call(
        functools.partial(exit_kernel, shape, units),
        "exit",
        [rows_array(f32), late, late],
        [
            scratch((shape.packed, lanes), f32),
            scratch((taps * sublanes, lanes), f32),
            scratch((rows, width), f32),
            scratch((rows, width), f32),
            scratch((units.late_total, width), f32),
            scratch((lanes, width), bf16),
        ],
        9,
        24,
        core,
        Far(two),
        Far(d_three),
        Far(one),
        Far(d_two),
        Far(context),
        Far(d_one),
        Far(rounded),
        Far(d_gates),
        Far(small),
        Far(normed),
        Far(f_turned),
        Far(d_query),
        Far(tokens_packed),
    )
    if quick:
        late_arrived = flip(other_late)
        rest_parts = after(rest_parts, own_late)
        (late_half,) = call(pair_kernel, "pair", [late], [], 1, 4, own_late, late_arrived)
        late_half, rest_parts = lax.optimization_barrier((late_half, rest_parts))
        late_parts = exchange(late_half.reshape(-1, width), ("x", "b"))
        late_parts = late_parts.reshape(4, units.pieces * units.late_rows // 4, width)
        d_inputs = after(d_inputs, late_half)
    tokens_grad, block_out = call(
        functools.partial(finish_kernel, shape),
        "finish",
        [far_array(shape.packed, lanes), far_array(shape.packed, lanes)],
        [scratch((rows, width), f32)],
        3,
        16,
        Far(d_middle),
        Far(d_inputs),
        Far(small),
        Far(middle),
        Far(out_near),
        Anywhere(out_far),
    )
    if quick:
        late_parts = after(late_parts, tokens_grad)
        share_rows = units.pieces * units.share // 4
        (share,) = call(
            share_kernel,
            "share",
            [array(sizes["a"], share_rows, width, kind=bf16)],
            [],
            1,
            8,
            rest_parts,
            late_parts,
        )
        piece = after(piece, share)
        piece_x = flip(piece, "x")
        piece_core, piece_both = flip(piece), flip(piece_x)
        parts = exchange(share.reshape(-1, width), "a")
        parts = after(parts, piece_core, piece_both)
        own = total_of(parts, sizes["a"])
        held_b, held_x = flip(own, "b"), flip(own, "x")
        held_both = flip(held_b, "x")
        held = [own, held_b, held_x, held_both]
        held = held + [flip(item) for item in held]
        turn = lax.rem(units.shards - shard, units.shards) * units.unit
        spots = [core[0], quarter, turn] + [lax.axis_index(axis) for axis in ("x", "b")]
        spots = jnp.stack(spots).astype(jnp.int32)
        total = 4 * units.unit
        others = call(
            functools.partial(unpack_kernel, shape, units),
            "unpack",
            [
                array(width),
                array(width),
                array(2 * width + 4, width),
                array(2 * width + 4),
                array(9, width),
                array(25, width),
                array(49, width),
                array(width, width),
                array(width),
                array(width, width),
                array(width),
                array(width),
                array(width),
                array(total, width),
                array(total),
                array(total, width),
                array(width),
            ],
            [
                scratch((2 * units.pieces * units.share, width), f32),
                scratch((units.head_total, width), f32),
                scratch((units.late_total, width), f32),
            ],
            2,
            16,
            spots,
            piece,
            piece_x,
            piece_core,
            piece_both,
            *held,
        )
    else:
        others = reduce_plainly(
            shape, units, feed_grads, (own_rest, other_rest), (own_late, other_late)
        )
    others = list(others)
    others[2] = others[2].T
    others[13] = others[13].T
    return from_packed(block_out, shape), from_packed(tokens_grad, shape), *others


def solution(mesh):
    img, mlp = mesh.shape["img"], mesh.shape["mlp"]
    sizes = {"x": img // 2, "core": 2, "a": mlp // 2, "b": 2}
    finer = Mesh(mesh.devices.reshape(*sizes.values()), everyone)
    images = P(everyone, None, None, None)
    hidden = ("a", "b")
    return jax.shard_map(
        functools.partial(shards, sizes),
        mesh=finer,
        in_specs=(images,)
        + (P(),) * 13
        + (P(None, hidden), P(hidden), P(hidden, None), P(), images),
        out_specs=(images, images)
        + (P(),) * 13
        + (P(None, hidden), P(hidden), P(hidden, None), P()),
        check_vma=False,
    )
```

```python
import functools
import math

import jax
import jax.numpy as jnp
from jax import lax
from jax.experimental import pallas as pl
from jax.experimental.pallas import tpu as pltpu
from jax.experimental.layout import Layout, with_layout_constraint
from jax.sharding import Mesh
from jax.sharding import PartitionSpec as P

epsilon = 1e-05
lanes = 128
sublanes = 8
edge = 3
extents = (3, 5, 7)
starts = (0, 9, 34)
taps = 83
LN1_GAIN, LN1_BIAS, QUERY_BIAS, CONTEXT_BIAS, GATE_BIAS = 83, 84, 85, 86, 87
H_BIAS, PROJ_BIAS, LN2_GAIN, LN2_BIAS, FC2_BIAS = 88, 89, 90, 91, 92
f32 = jnp.float32
bf16 = jnp.bfloat16


def flip(values, axis="core", size=2, bit=1):
    return lax.ppermute(values, axis, [(place, place ^ bit) for place in range(size)])


def exchange(values, axes):
    return lax.all_to_all(values, axes, split_axis=0, concat_axis=0, tiled=True)


def after(values, *others):
    return lax.optimization_barrier((values,) + others)[0]


def nn(left, right):
    return jnp.dot(left, right, preferred_element_type=f32)


def nt(left, right):
    return lax.dot_general(left, right, (((1,), (1,)), ((), ())), preferred_element_type=f32)


def tn(left, right):
    return lax.dot_general(left, right, (((0,), (0,)), ((), ())), preferred_element_type=f32)


def gelu_pair(values):
    below = 0.5 * (1.0 + lax.erf(values * math.sqrt(0.5)))
    density = jnp.exp(values * values * -0.5) * (1.0 / math.sqrt(2.0 * math.pi))
    return values * below, below + values * density


class Shape:
    def __init__(self, images, side, width):
        self.images, self.side, self.width = images, side, width
        self.tiles = width // lanes
        self.slots = images * self.tiles
        self.patches = side * side
        self.segment = -(-self.patches // 8) * 8
        self.rows = images * self.segment
        self.line = side * sublanes
        self.centre = edge * self.line
        self.grid = (side + 2 * edge) * self.line
        self.inner = side * self.line
        self.packed = self.patches * self.slots
        self.block = next(size for size in (80, 40, 16, 8) if self.rows % size == 0)

    def places(self):
        return [
            (image, tile, tile * self.images + image)
            for image in range(self.images)
            for tile in range(self.tiles)
        ]


def columns(tile):
    return slice(tile * lanes, (tile + 1) * lanes)


def unpack(shape, packed, rows):
    for image, tile, slot in shape.places():
        first = image * shape.segment
        rows[first : first + shape.patches, columns(tile)] = packed[
            pl.ds(slot, shape.patches, stride=shape.slots), :
        ]
    for image in range(shape.images):
        first = image * shape.segment
        spare = shape.segment - shape.patches
        if spare:
            rows[first + shape.patches : first + shape.segment, 0 : shape.width] = jnp.zeros(
                (spare, shape.width), f32
            )


def pack(shape, rows, packed):
    for image, tile, slot in shape.places():
        first = image * shape.segment
        packed[pl.ds(slot, shape.patches, stride=shape.slots), :] = rows[
            first : first + shape.patches, columns(tile)
        ]


def blocks(shape, body, init=None):
    def step(index, carry):
        first = pl.multiple_of(index * shape.block, shape.block)
        return body(pl.ds(first, shape.block), carry)

    return lax.fori_loop(0, shape.rows // shape.block, step, init)


def normalise(values):
    average = jnp.mean(values, axis=-1, keepdims=True)
    centred = values - average
    variance = jnp.mean(centred * centred, axis=-1, keepdims=True)
    scale = lax.rsqrt(variance + epsilon)
    return centred * scale, scale


def norm_back(values, grad, gain):
    unit, scale = normalise(values)
    inner = grad * gain
    first = jnp.mean(inner, axis=-1, keepdims=True)
    second = jnp.mean(inner * unit, axis=-1, keepdims=True)
    return scale * (inner - first - unit * second), grad * unit


def fold(values):
    return jnp.sum(values.reshape(values.shape[0] // 8, 8, values.shape[1]), axis=0)


def row_sum(values):
    return jnp.sum(values, axis=0, keepdims=True)


def spread_taps(shape, small, tap_ref):
    tap_ref[...] = jnp.zeros_like(tap_ref)
    for _, tile, slot in shape.places():
        tap_ref[pl.ds(slot, taps, stride=sublanes), :] = small[0:taps, columns(tile)]


def line_at(shape, ref, line):
    first = pl.multiple_of(line * shape.line, shape.line)
    values = ref[pl.ds(first, shape.line), :]
    return [values[w * sublanes : (w + 1) * sublanes] for w in range(shape.side)]


def correlate(shape, source, tap_ref, level, line, turned):
    extent = extents[level]
    reach = extent // 2
    totals = [None] * shape.side
    for down in range(extent):
        values = line_at(shape, source, line + down + edge - reach)
        for along in range(extent):
            entry = down * extent + along
            if turned:
                entry = extent * extent - 1 - entry
            tap = tap_ref[pl.ds((starts[level] + entry) * sublanes, sublanes), :]
            for w in range(shape.side):
                other = w + along - reach
                if 0 <= other < shape.side:
                    term = values[other] * tap
                    totals[w] = term if totals[w] is None else totals[w] + term
    return jnp.concatenate(totals, axis=0)


def tap_grads(shape, source, grad, level, out):
    extent = extents[level]
    reach = extent // 2
    for down in range(extent):

        def step(line, totals, down=down):
            values = line_at(shape, source, line + down + edge - reach)
            grads = line_at(shape, grad, line + edge)
            result = []
            for along in range(extent):
                total = totals[along]
                for w in range(shape.side):
                    other = w + along - reach
                    if 0 <= other < shape.side:
                        total = total + values[other] * grads[w]
                result.append(total)
            return tuple(result)

        zero = jnp.zeros((sublanes, lanes), f32)
        first, last = max(0, reach - down), min(shape.side, shape.side + reach - down)
        totals = lax.fori_loop(first, last, step, (zero,) * extent)
        for along in range(extent):
            out[pl.ds((starts[level] + down * extent + along) * sublanes, sublanes), :] = totals[
                along
            ]


def clear_edges(shape, ref):
    zeros = jnp.zeros((shape.centre, lanes), f32)
    ref[0 : shape.centre, :] = zeros
    ref[shape.centre + shape.inner : shape.grid, :] = zeros


def gate_values(shape, normed, f_turned, small, gates):
    weight = f_turned[2 * shape.width : 2 * shape.width + 4, :].astype(f32)
    wide = jnp.concatenate(
        [jnp.broadcast_to(weight[g : g + 1], (lanes, shape.width)) for g in range(4)]
    ).astype(bf16)
    bias = small[GATE_BIAS : GATE_BIAS + 1, :]
    wide_bias = jnp.concatenate(
        [jnp.broadcast_to(bias[:, g : g + 1], (1, lanes)) for g in range(4)], axis=1
    )
    gates[...] = nt(normed[...], wide) + wide_bias


def level_rows(shape, level, image, slot):
    return level[pl.ds(shape.centre + slot, shape.segment, stride=sublanes), :]


def run_levels(shape, moves, chain, tap_ref):
    total = jnp.zeros((sublanes, lanes), f32)
    for level, source, target, slope in chain:
        clear_edges(shape, target)

        def line_step(line, total, level=level, source=source, target=target, slope=slope):
            before = correlate(shape, source, tap_ref, level, line, False)
            value, rise = gelu_pair(before)
            here = pl.multiple_of((line + edge) * shape.line, shape.line)
            target[pl.ds(here, shape.line), :] = value
            slope[pl.ds(pl.multiple_of(line * shape.line, shape.line), shape.line), :] = rise
            if level == 2:
                total = total + fold(value)
            return total

        total = lax.fori_loop(0, shape.side, line_step, total)
        moves.leave(target, slope)
    return total


def entry_kernel(
    shape,
    moves,
    tokens,
    f_turned,
    out_grad,
    dw_small,
    dw_middle,
    dw_large,
    ln1_gain,
    ln1_bias,
    f_bias,
    h_bias,
    proj_bias,
    ln2_gain,
    ln2_bias,
    fc2_bias,
    small,
    cot,
    inputs,
    normed,
    query,
    gates,
    context,
    one,
    slope_one,
    tap_ref,
    packed,
    wide,
):
    width = shape.width
    for source, first in zip((dw_small, dw_middle, dw_large), starts):
        small[first : first + source.shape[0], :] = source[...].astype(f32)
    shared = f_bias[...].astype(f32).reshape(1, 2 * width + 4)
    vectors = {
        QUERY_BIAS: shared[:, 0:width],
        CONTEXT_BIAS: shared[:, width : 2 * width],
        GATE_BIAS: jnp.concatenate(
            [shared[:, 2 * width :], jnp.zeros((1, width - 4), f32)], axis=1
        ),
    }
    for row, source in (
        (LN1_GAIN, ln1_gain),
        (LN1_BIAS, ln1_bias),
        (H_BIAS, h_bias),
        (PROJ_BIAS, proj_bias),
        (LN2_GAIN, ln2_gain),
        (LN2_BIAS, ln2_bias),
        (FC2_BIAS, fc2_bias),
    ):
        vectors[row] = source[...].astype(f32).reshape(1, width)
    for row, value in vectors.items():
        small[row : row + 1, :] = value
    last = FC2_BIAS + 1
    small[last:, :] = jnp.zeros((small.shape[0] - last, width), f32)
    moves.leave(small)
    moves.arrive(tokens)
    packed[...] = tokens[...].astype(f32)
    unpack(shape, packed, inputs)
    moves.leave(inputs)
    spread_taps(shape, small, tap_ref)
    gain = small[LN1_GAIN : LN1_GAIN + 1, :]
    bias = small[LN1_BIAS : LN1_BIAS + 1, :]

    def first_norm(rows, carry):
        unit, _ = normalise(inputs[rows, :])
        normed[rows, :] = (unit * gain + bias).astype(bf16)
        return carry

    blocks(shape, first_norm, 0)
    moves.leave(normed)
    moves.arrive(out_grad)
    packed[...] = out_grad[...].astype(f32)
    unpack(shape, packed, wide)
    cot[...] = wide[...].astype(bf16)
    moves.leave(cot)
    moves.arrive(f_turned)
    wide[...] = (
        nt(normed[...], f_turned[width : 2 * width, :]) + small[CONTEXT_BIAS : CONTEXT_BIAS + 1, :]
    )
    context[...] = jnp.zeros_like(context)
    for image, tile, slot in shape.places():
        first = image * shape.segment
        context[pl.ds(shape.centre + slot, shape.patches, stride=sublanes), :] = wide[
            first : first + shape.patches, columns(tile)
        ]
    moves.leave(context)
    query[...] = nt(normed[...], f_turned[0:width, :]) + small[QUERY_BIAS : QUERY_BIAS + 1, :]
    moves.leave(query)
    gate_values(shape, normed, f_turned, small, gates)
    moves.leave(gates)
    run_levels(shape, moves, ((0, context, one, slope_one),), tap_ref)


def modulation_kernel(
    shape,
    moves,
    one,
    small,
    gates,
    h_weight,
    query,
    inputs,
    proj_weight,
    slope_one,
    far_one,
    far_gates,
    far_query,
    far_slope,
    modulator,
    aggregated,
    mixed,
    middle,
    normed_two,
    two,
    three,
    slope_two,
    slope_three,
    pooled,
    wide,
    tap_ref,
):
    chain = ((1, one, two, slope_two), (2, two, three, slope_three))
    moves.arrive(small)
    spread_taps(shape, small, tap_ref)
    moves.copy(one, far_one)
    moves.copy(gates, far_gates)
    moves.copy(query, far_query)
    moves.copy(slope_one, far_slope)
    total = run_levels(shape, moves, chain, tap_ref)
    value, rise = gelu_pair(total * (1.0 / shape.patches))
    pooled[0:sublanes, :] = value
    pooled[sublanes : 2 * sublanes, :] = rise * (1.0 / shape.patches)
    moves.leave(pooled)
    moves.arrive(h_weight, proj_weight)
    for image, tile, slot in shape.places():
        rows = pl.ds(image * shape.segment, shape.segment)
        wide[rows, columns(tile)] = (
            level_rows(shape, one, image, slot) * gates[rows, columns(0)]
            + level_rows(shape, two, image, slot) * gates[rows, columns(1)]
            + level_rows(shape, three, image, slot) * gates[rows, columns(2)]
            + value[slot : slot + 1] * gates[rows, columns(3)]
        )
    aggregated[...] = wide[...].astype(bf16)
    moves.leave(aggregated)
    modulator[...] = nn(aggregated[...], h_weight[...]) + small[H_BIAS : H_BIAS + 1, :]

    moves.leave(modulator)

    def mix(rows, carry):
        mixed[rows, :] = (query[rows, :] * modulator[rows, :]).astype(bf16)
        return carry

    blocks(shape, mix, 0)
    moves.leave(mixed)
    middle[...] = (
        inputs[...] + nn(mixed[...], proj_weight[...]) + small[PROJ_BIAS : PROJ_BIAS + 1, :]
    )
    moves.leave(middle)
    gain = small[LN2_GAIN : LN2_GAIN + 1, :]
    bias = small[LN2_BIAS : LN2_BIAS + 1, :]

    def second_norm(rows, carry):
        unit, _ = normalise(middle[rows, :])
        normed_two[rows, :] = (unit * gain + bias).astype(bf16)
        return carry

    blocks(shape, second_norm, 0)


class Moves:
    def __init__(self):
        self.incoming, self.outgoing = {}, {}
        self.started, self.free = [], []

    def copy(self, source, target):
        move = pltpu.make_async_copy(source, target, self.free.pop())
        move.start()
        self.started.append(move)

    def arrive(self, *buffers):
        for buffer in buffers:
            move = self.incoming.pop(id(buffer), None)
            if move is not None:
                move.wait()

    def leave(self, *buffers):
        for buffer in buffers:
            move = self.outgoing.pop(id(buffer), None)
            if move is not None:
                move.start()
                self.started.append(move)

    def finish(self):
        for move in list(self.incoming.values()):
            move.wait()
        for move in list(self.outgoing.values()):
            move.start()
            self.started.append(move)
        for move in self.started:
            move.wait()


def with_moves(kernel, far_in, far_out, extra):
    def run(*refs):
        refs = list(refs)
        ins, refs = refs[: len(far_in)], refs[len(far_in) :]
        outs, refs = refs[: len(far_out)], refs[len(far_out) :]
        semaphores = refs.pop()
        count = sum(far_in) + sum(far_out)
        buffers, scratch = refs[len(refs) - count :], refs[: len(refs) - count]
        moves = Moves()
        moves.free = [semaphores.at[count + spare] for spare in range(extra)]
        index = 0
        for group, flags, table in (
            (ins, far_in, moves.incoming),
            (outs, far_out, moves.outgoing),
        ):
            for place, far in enumerate(flags):
                if far:
                    buffer, outer = buffers[index], group[place]
                    pair = (outer, buffer) if group is ins else (buffer, outer)
                    move = pltpu.make_async_copy(*pair, semaphores.at[index])
                    if group is ins:
                        move.start()
                    table[id(buffer)] = move
                    group[place] = buffer
                    index += 1
        kernel(moves, *ins, *outs, *scratch)
        moves.finish()

    return run


class Units:
    def __init__(self, shards, unit):
        self.shards, self.unit = shards, unit
        self.piece_rows = 2 * unit + 16
        self.feed_rows = 2 * unit
        self.total = shards * unit
        self.head_rows, self.late_rows = 40, 16
        self.pieces = 2 * shards
        self.share = self.head_rows + self.late_rows
        self.head_total = 2 * self.pieces * self.head_rows
        self.late_total = 2 * self.pieces * self.late_rows


def sum_kernel(parts, source, out):
    size = out.shape[0]
    block = 16 if size % 16 == 0 else size

    def step(index, carry):
        rows = pl.ds(pl.multiple_of(index * block, block), block)
        total = source[0, rows, :].astype(f32)
        for part in range(1, parts):
            total = total + source[part, rows, :].astype(f32)
        out[rows, :] = total.astype(bf16)
        return carry

    lax.fori_loop(0, size // block, step, 0)


def pair_kernel(first, second, out):
    for part in range(out.shape[0]):
        total = first[part].astype(f32) + second[part].astype(f32)
        out[part] = total.astype(bf16)


def rows_kernel(shape, moves, first, second, arrived, first_out, second_out):
    def step(index, carry):
        rows = pl.ds(pl.multiple_of(index * 16, 16), 16)
        more = pl.ds(pl.multiple_of(index * 16 + shape.rows, 16), 16)
        first_out[rows, :] = (first[rows, :].astype(f32) + arrived[rows, :].astype(f32)).astype(bf16)
        second_out[rows, :] = (second[rows, :].astype(f32) + arrived[more, :].astype(f32)).astype(
            bf16
        )
        return carry

    lax.fori_loop(0, shape.rows // 16, step, 0)


def share_kernel(head_parts, late_parts, out):
    sums = []
    for parts in (head_parts, late_parts):
        total = parts[0].astype(f32)
        for part in range(1, parts.shape[0]):
            total = total + parts[part].astype(f32)
        sums.append(total)
    out[...] = jnp.concatenate(sums).astype(bf16)


def add_kernel(first, second, out):
    out[...] = (first[...].astype(f32) + second[...].astype(f32)).astype(bf16)


def piece_kernel(units, copies, spots, first, second, far_bias, out, own, bias, semaphores):
    unit = units.unit
    width = first.shape[1]
    rows = pl.ds(pl.multiple_of(spots[0] * unit, 16), unit)
    moves = [
        pltpu.make_async_copy(source.at[rows, :], own.at[index], semaphores.at[index])
        for index, source in enumerate((first, second))
    ]
    moves.insert(0, pltpu.make_async_copy(far_bias, bias, semaphores.at[2]))
    for move in moves:
        move.start()
    moves.pop(0).wait()
    shard = spots[1]
    values = bias[...].astype(f32).reshape(1, bias.shape[0])
    values = jnp.concatenate([values, jnp.zeros((1, width - bias.shape[0]), f32)], axis=1)
    values = pltpu.roll(jnp.broadcast_to(values, (8, width)), spots[2], 1)
    lane = lax.broadcasted_iota(jnp.int32, (8, width), 1) - shard * unit
    row = lax.broadcasted_iota(jnp.int32, (8, width), 0)
    values = jnp.where((lane >= 0) & (lane < unit) & (row == 0), values, 0.0)
    line = jnp.concatenate([values, jnp.zeros((8, width), f32)]).astype(bf16)
    for move in moves:
        move.wait()
    for copy in range(copies):
        base = copy * units.piece_rows
        out[base : base + unit, :] = own[0]
        out[base + unit : base + 2 * unit, :] = own[1]
        out[base + 2 * unit : base + units.piece_rows, :] = line


def feed_kernel(shape, units, resumed, moves, weights, *refs):
    refs = list(refs)

    def take(count):
        taken = refs[:count]
        del refs[:count]
        return taken

    groups = 1 if resumed is None else 2
    closing = resumed is not False
    normed, cots = take(groups), take(groups)
    if resumed:
        old_grads, old_bias, *near = take(6)
    if resumed:
        out, d_out, both = take(3)
        outs = [out, both.at[shape.rows : 2 * shape.rows, :]]
        d_outs = [d_out, both.at[0 : shape.rows, :]]
        d_near, out_near = take(2)
    else:
        outs, d_outs = take(groups), take(groups)
    grads, bias_grad = take(2)
    first_weight, second_weight, total_grads, total_bias = take(4)
    unit, width = units.unit, shape.width
    bias = None
    for shard in range(units.shards):
        base, here = shard * units.piece_rows, shard * unit
        first_weight[here : here + unit, :] = weights[base : base + unit, :]
        second_weight[here : here + unit, :] = weights[base + unit : base + 2 * unit, :]
        term = weights[base + 2 * unit : base + units.piece_rows, :].astype(f32)
        bias = term if bias is None else bias + term
    bias = bias[0:1]
    if resumed:
        moves.arrive(*near)
        for target, own, arrived in ((d_near, near[0], near[1]), (out_near, near[2], near[3])):
            target[...] = own[...].astype(f32) + arrived[...].astype(f32)
            moves.leave(target)
    for group in range(groups):
        moves.arrive(normed[group], cots[group])
        rows, cot = normed[group], cots[group]
        value, rise = gelu_pair(nt(rows[...], first_weight[...]) + bias)
        hidden = value.astype(bf16)
        outs[group][...] = nn(hidden, second_weight[...]).astype(bf16)
        d_before = (nt(cot[...], second_weight[...]) * rise).astype(bf16)
        d_outs[group][...] = nn(d_before, first_weight[...]).astype(bf16)
        moves.leave(outs[group], d_outs[group])
        first, second = tn(d_before, rows[...]), tn(hidden, cot[...])
        line = fold(d_before.astype(f32))
        if group == 0 and not resumed:
            total_grads[0 : units.total, :] = first
            total_grads[units.total :, :] = second
            total_bias[...] = line
        elif group == 0:
            total_grads[0 : units.total, :] = old_grads[0 : units.total, :] + first
            total_grads[units.total :, :] = old_grads[units.total :, :] + second
            total_bias[...] = old_bias[...] + line
        else:
            total_grads[0 : units.total, :] += first
            total_grads[units.total :, :] += second
            total_bias[...] += line
    if not closing:
        grads[...] = total_grads[...]
        bias_grad[...] = total_bias[...]
        return
    bias_grad[...] = total_bias[...]
    for shard in range(units.shards):
        base, here = shard * units.feed_rows, shard * unit
        more = units.total + here
        grads[base : base + units.feed_rows, :] = jnp.concatenate(
            [total_grads[here : here + unit, :], total_grads[more : more + unit, :]]
        ).astype(bf16)


def heads_kernel(
    shape,
    units,
    moves,
    core,
    small,
    cot,
    middle,
    d_near,
    d_far,
    bias_grads,
    proj_weight,
    query,
    modulator,
    h_weight,
    normed,
    aggregated,
    mixed,
    *refs,
):
    later, refs = refs[:9], refs[9:]
    d_middle, d_query, d_aggregated, own_rest, other_rest, *refs = refs
    fetched, refs = refs[:9], refs[9:]
    heads_body(
        shape,
        units,
        moves,
        core,
        small,
        cot,
        middle,
        d_near,
        d_far,
        bias_grads,
        proj_weight,
        query,
        modulator,
        h_weight,
        normed,
        aggregated,
        mixed,
        list(zip(later, fetched)),
        d_middle,
        d_query,
        d_aggregated,
        own_rest,
        other_rest,
        *refs,
    )


def heads_body(
    shape,
    units,
    moves,
    core,
    small,
    cot,
    middle,
    d_near,
    d_far,
    bias_grads,
    proj_weight,
    query,
    modulator,
    h_weight,
    normed,
    aggregated,
    mixed,
    later,
    d_middle,
    d_query,
    d_aggregated,
    own_rest,
    other_rest,
    d_mixed,
    d_modulator,
    head,
    d_branch,
):
    width = shape.width
    zero = jnp.zeros((8, width), f32)
    moves.arrive(small, cot, middle, d_near)
    for source, target in later:
        moves.copy(source, target)
    gain = small[LN2_GAIN : LN2_GAIN + 1, :]

    def second_norm(rows, carry):
        grads = d_near[rows, :] + d_far[rows, :].astype(f32)
        cots = cot[rows, :].astype(f32)
        d_input, d_gain = norm_back(middle[rows, :], grads, gain)
        d_total = cots + d_input
        d_middle[rows, :] = d_total
        rounded = d_total.astype(bf16)
        d_branch[rows, :] = rounded
        added = (d_gain, grads, rounded.astype(f32), cots)
        return tuple(total + fold(item) for total, item in zip(carry, added))

    d_gain, d_bias, proj_bias, out_bias = blocks(shape, second_norm, (zero,) * 4)
    moves.leave(d_middle)
    moves.arrive(proj_weight)
    d_mixed[...] = nt(d_branch[...], proj_weight[...])
    moves.arrive(query, modulator)

    def split(rows, carry):
        values = d_mixed[rows, :]
        for_query = (values * modulator[rows, :]).astype(bf16)
        for_modulator = (values * query[rows, :]).astype(bf16)
        d_query[rows, :] = for_query
        d_modulator[rows, :] = for_modulator
        return carry[0] + fold(for_query.astype(f32)), carry[1] + fold(for_modulator.astype(f32))

    query_bias, h_bias = blocks(shape, split, (zero, zero))
    moves.leave(d_query)
    moves.arrive(h_weight)
    d_aggregated[...] = nt(d_modulator[...], h_weight[...])
    moves.leave(d_aggregated)
    moves.arrive(normed, aggregated, mixed)
    head[0:width, :] = tn(d_query[...], normed[...])
    head[width : 2 * width, :] = tn(aggregated[...], d_modulator[...])
    head[2 * width : 3 * width, :] = tn(mixed[...], d_branch[...])
    sums = (h_bias, proj_bias, d_gain, d_bias, out_bias, query_bias)
    head[3 * width :, :] = jnp.concatenate(
        [row_sum(item) for item in sums]
        + [jnp.zeros((2, width), f32)]
        + [row_sum(bias_grads[8 * index : 8 * index + 8, :]) for index in range(4)]
        + [jnp.zeros((units.head_total - 3 * width - 12, width), f32)]
    )
    for half, target in enumerate((own_rest, other_rest)):
        absolute = jnp.bitwise_xor(core[0], half)
        for piece in range(units.pieces):
            first = (absolute * units.pieces + piece) * units.head_rows
            target[piece] = head[pl.ds(pl.multiple_of(first, 8), units.head_rows), :].astype(bf16)


def levels_back_kernel(
    shape,
    moves,
    small,
    gates,
    d_aggregated,
    pooled,
    slope_three,
    slope_two,
    slope_one,
    one,
    two,
    three,
    d_one,
    d_two,
    d_three,
    rounded,
    d_gates,
    tap_ref,
    d_levels,
    products,
    d_context,
):
    width = shape.width
    inner = shape.inner
    moves.arrive(small)
    spread_taps(shape, small, tap_ref)
    for ref in (d_one, d_two, d_three):
        clear_edges(shape, ref)
    moves.arrive(gates, d_aggregated, pooled)
    pool_grad = [None] * sublanes
    for image in range(shape.images):
        rows = pl.ds(image * shape.segment, shape.segment)
        for tile in range(shape.tiles):
            slot = tile * shape.images + image
            values = d_aggregated[rows, columns(tile)]
            for level in range(3):
                d_levels[pl.ds(level * inner + slot, shape.patches, stride=sublanes), :] = (
                    values[: shape.patches] * gates[rows, columns(level)][: shape.patches]
                )
            pool_grad[slot] = jnp.sum(values * gates[rows, columns(3)], axis=0, keepdims=True)
    blank = jnp.zeros((1, lanes), f32)
    pool_grad = jnp.concatenate([blank if item is None else item for item in pool_grad])
    pool_grad = pool_grad * pooled[sublanes : 2 * sublanes, :]
    wide_pool = jnp.concatenate([pool_grad] * shape.side)

    def third(line, carry):
        here = pl.multiple_of(line * shape.line, shape.line)
        value = (d_levels[pl.ds(2 * inner + here, shape.line), :] + wide_pool) * slope_three[
            pl.ds(here, shape.line), :
        ]
        d_three[pl.ds(here + shape.centre, shape.line), :] = value
        return carry

    moves.arrive(slope_three)
    lax.fori_loop(0, shape.side, third, 0)
    moves.leave(d_three)
    moves.arrive(slope_two, slope_one)
    for level, source, target, slope in ((2, d_three, d_two, slope_two), (1, d_two, d_one, slope_one)):

        def back(line, carry, level=level, source=source, target=target, slope=slope):
            here = pl.multiple_of(line * shape.line, shape.line)
            value = correlate(shape, source, tap_ref, level, line, True)
            value = (value + d_levels[pl.ds((level - 1) * inner + here, shape.line), :]) * slope[
                pl.ds(here, shape.line), :
            ]
            target[pl.ds(here + shape.centre, shape.line), :] = value
            return carry

        lax.fori_loop(0, shape.side, back, 0)
        moves.leave(target)

    def back_context(line, carry):
        here = pl.multiple_of(line * shape.line, shape.line)
        d_levels[pl.ds(here, shape.line), :] = correlate(shape, d_one, tap_ref, 0, line, True)
        return carry

    lax.fori_loop(0, shape.side, back_context, 0)
    for image, tile, slot in shape.places():
        first = image * shape.segment
        d_context[first : first + shape.patches, columns(tile)] = d_levels[
            pl.ds(slot, shape.patches, stride=sublanes), :
        ]
        if tile == 0 and shape.segment > shape.patches:
            d_context[first + shape.patches : first + shape.segment, :] = jnp.zeros(
                (shape.segment - shape.patches, width), f32
            )
    rounded[...] = d_context[...].astype(bf16)
    moves.leave(rounded)
    moves.arrive(one, two, three)
    for image in range(shape.images):
        rows = pl.ds(image * shape.segment, shape.segment)
        totals = [None] * 4
        for tile in range(shape.tiles):
            slot = tile * shape.images + image
            values = d_aggregated[rows, columns(tile)]
            for level, ref in enumerate((one, two, three)):
                term = values * level_rows(shape, ref, image, slot)
                totals[level] = term if tile == 0 else totals[level] + term
            term = values * pooled[slot : slot + 1, :]
            totals[3] = term if tile == 0 else totals[3] + term
        for gate in range(4):
            products[rows, columns(gate)] = totals[gate]
    chooser = (
        lax.broadcasted_iota(jnp.int32, (4 * lanes, lanes), 0) // lanes
        == lax.broadcasted_iota(jnp.int32, (4 * lanes, lanes), 1)
    ).astype(f32).astype(bf16)
    d_gates[...] = nn(products[...].astype(bf16), chooser).astype(bf16)


def exit_kernel(
    shape,
    units,
    moves,
    core,
    two,
    d_three,
    one,
    d_two,
    context,
    d_one,
    rounded,
    d_gates,
    small,
    normed,
    f_turned,
    d_query,
    tokens,
    d_inputs,
    own_late,
    other_late,
    packed,
    tap_grad,
    inputs,
    d_context,
    gathered,
    gate_rows,
):
    width = shape.width
    moves.arrive(two, d_three)
    tap_grads(shape, two, d_three, 2, tap_grad)
    moves.arrive(one, d_two)
    tap_grads(shape, one, d_two, 1, tap_grad)
    moves.arrive(context, d_one)
    tap_grads(shape, context, d_one, 0, tap_grad)
    moves.arrive(rounded, d_gates, small, normed, f_turned, d_query, tokens)
    gathered[0:width, :] = tn(rounded[...], normed[...])
    gathered[width : width + 8, :] = tn(d_gates[...], normed[...])[0:8]
    for tile in range(shape.tiles):
        total = None
        for image in range(shape.images):
            slot = tile * shape.images + image
            term = tap_grad[pl.ds(slot, taps, stride=sublanes), :]
            total = term if total is None else total + term
        gathered[width + 8 : width + 8 + taps, columns(tile)] = total
    gate_rows[...] = jnp.concatenate(
        [
            f_turned[2 * width : 2 * width + 4, :].astype(f32),
            jnp.zeros((lanes - 4, width), f32),
        ]
    ).astype(bf16)
    d_normed = d_context
    gate_bias = row_sum(fold(d_gates[...].astype(f32)))
    context_bias = row_sum(fold(rounded[...].astype(f32)))
    d_normed[...] = (
        nn(d_query[...], f_turned[0:width, :])
        + nn(rounded[...], f_turned[width : 2 * width, :])
        + nn(d_gates[...], gate_rows[...])
    )
    packed[...] = tokens[...].astype(f32)
    unpack(shape, packed, inputs)
    gain = small[LN1_GAIN : LN1_GAIN + 1, :]
    zero = jnp.zeros((8, width), f32)

    def finish(rows, carry):
        values = d_normed[rows, :]
        d_input, d_gain = norm_back(inputs[rows, :], values, gain)
        d_inputs[rows, :] = d_input
        return carry[0] + fold(d_gain), carry[1] + fold(values)

    d_gain, d_bias = blocks(shape, finish, (zero, zero))
    moves.leave(d_inputs)
    last = width + 8 + taps
    rest = units.late_total - last - 4
    gathered[last:, :] = jnp.concatenate(
        [
            row_sum(d_gain),
            row_sum(d_bias),
            context_bias,
            jnp.concatenate([gate_bias, jnp.zeros((1, width - lanes), f32)], axis=1),
            jnp.zeros((rest, width), f32),
        ]
    )
    for half, target in enumerate((own_late, other_late)):
        absolute = jnp.bitwise_xor(core[0], half)
        for piece in range(units.pieces):
            first = (absolute * units.pieces + piece) * units.late_rows
            target[piece] = gathered[
                pl.ds(pl.multiple_of(first, 16), units.late_rows), :
            ].astype(bf16)


def finish_kernel(
    shape,
    moves,
    d_middle,
    d_inputs,
    small,
    middle,
    out_near,
    out_far,
    tokens_grad,
    block_out,
    rows_ref,
):
    moves.arrive(d_middle, d_inputs)

    def add_grads(rows, carry):
        rows_ref[rows, :] = d_middle[rows, :] + d_inputs[rows, :]
        return carry

    blocks(shape, add_grads, 0)
    pack(shape, rows_ref, tokens_grad)
    moves.leave(tokens_grad)
    moves.arrive(small, middle, out_near, out_far)

    def add_outs(rows, carry):
        total = middle[rows, :] + small[FC2_BIAS : FC2_BIAS + 1, :]
        rows_ref[rows, :] = total + out_near[rows, :] + out_far[rows, :].astype(f32)
        return carry

    blocks(shape, add_outs, 0)
    pack(shape, rows_ref, block_out)


def unpack_kernel(
    shape,
    units,
    spots,
    piece,
    piece_x,
    piece_core,
    piece_both,
    own,
    own_b,
    own_x,
    own_both,
    core_own,
    core_b,
    core_x,
    core_both,
    ln1_gain,
    ln1_bias,
    f_grad,
    f_bias,
    small_grad,
    middle_grad,
    large_grad,
    h_grad,
    h_bias,
    proj_grad,
    proj_bias,
    ln2_gain,
    ln2_bias,
    first_grad,
    first_bias,
    second_grad,
    second_bias,
    held,
    head,
    late,
):
    width = shape.width
    unit = units.unit
    size = own.shape[0]
    parts = (own, own_b, own_x, own_both, core_own, core_b, core_x, core_both)
    for index, part in enumerate(parts):
        held[index * size : (index + 1) * size, :] = part[...].astype(f32)
    core, shift = spots[0], spots[2]
    far = units.shards // 2
    for half in range(2):
        for place in range(2):
            for close in range(2):
                slot = jnp.bitwise_xor(core, half) * 4 + jnp.bitwise_xor(spots[3], place) * 2
                base = (slot + jnp.bitwise_xor(spots[4], close)) * size
                to = (half * 2 + place) * 2 + close
                rows = far * units.head_rows
                head[to * rows : (to + 1) * rows, :] = held[
                    pl.ds(pl.multiple_of(base, 8), rows), :
                ]
                first = pl.multiple_of(base + rows, 8)
                rows = far * units.late_rows
                late[to * rows : (to + 1) * rows, :] = held[pl.ds(first, rows), :]
    total = None
    lane = lax.broadcasted_iota(jnp.int32, (8, width), 1)
    for index, source in enumerate((piece, piece_core, piece_x, piece_both)):
        quarter = jnp.bitwise_xor(spots[1], index)
        to = pl.ds(pl.multiple_of(quarter * unit, 8), unit)
        first_grad[to, :] = source[0:unit, :].astype(f32)
        second_grad[to, :] = source[unit : 2 * unit, :].astype(f32)
    for quarter in range(4):
        row = head[3 * width + 8 + quarter : 3 * width + 9 + quarter, :]
        moved = shift + quarter * unit
        moved = jnp.where(moved >= width, moved - width, moved)
        row = pltpu.roll(jnp.broadcast_to(row, (8, width)), moved, 1)
        row = jnp.where((lane >= quarter * unit) & (lane < (quarter + 1) * unit), row, 0.0)
        total = row if total is None else total + row
    first_bias[...] = total[0:1, 0 : first_bias.shape[0]].reshape(first_bias.shape)
    f_grad[0:width, :] = head[0:width, :]
    f_grad[width : 2 * width + 4, :] = late[0 : width + 4, :]
    h_grad[...] = head[width : 2 * width, :]
    proj_grad[...] = head[2 * width : 3 * width, :]
    first = width + 8
    small_grad[...] = late[first : first + 9, :]
    middle_grad[...] = late[first + 9 : first + 34, :]
    large_grad[...] = late[first + 34 : first + taps, :]
    first = first + taps
    for out, source, row in (
        (h_bias, head, 3 * width),
        (proj_bias, head, 3 * width + 1),
        (ln2_gain, head, 3 * width + 2),
        (ln2_bias, head, 3 * width + 3),
        (second_bias, head, 3 * width + 4),
        (ln1_gain, late, first),
        (ln1_bias, late, first + 1),
    ):
        out[...] = source[row : row + 1, :].reshape(width)
    f_bias[0:width] = head[3 * width + 5 : 3 * width + 6, :].reshape(width)
    f_bias[width : 2 * width] = late[first + 2 : first + 3, :].reshape(width)
    f_bias[2 * width : 2 * width + 4] = late[first + 3 : first + 4, 0:4].reshape(4)


def call(kernel, name, outs, scratch, micros, room, *operands):
    spec = pl.BlockSpec(memory_space=pltpu.VMEM)
    outer = pl.BlockSpec(memory_space=pltpu.HBM)
    far_in = [isinstance(item, Far) for item in operands]
    far_out = [isinstance(item, Far) for item in outs]
    anywhere = [isinstance(item, Anywhere) for item in operands]
    raw = [isinstance(item, Raw) for item in operands]
    operands = [item.value if far else item for item, far in zip(operands, far_in)]
    operands = [
        pltpu.with_memory_space_constraint(item, pltpu.HBM) if far and not free else item
        for item, far, free in zip(operands, far_in, anywhere)
    ]
    raw_out = [isinstance(item, Raw) for item in outs]
    outs = [
        pltpu.HBM(item.value.shape, item.value.dtype) if far else item
        for item, far in zip(outs, far_out)
    ]
    specs = []
    for item, far, free in zip(operands, far_in, anywhere):
        if free:
            specs.append(pl.BlockSpec(memory_space=pl.ANY))
        elif item.dtype == jnp.int32:
            specs.append(pl.BlockSpec(memory_space=pltpu.SMEM))
        else:
            specs.append(outer if far else spec)
    out_specs = [outer if far else spec for far in far_out]
    if name not in plain:
        far_in = [far and not own for far, own in zip(far_in, raw)]
        far_out = [far and not own for far, own in zip(far_out, raw_out)]
        pairs = list(zip(operands, far_in)) + list(zip(outs, far_out))
        buffers = [pltpu.VMEM(item.shape, item.dtype) for item, far in pairs if far]
        extra = sum(raw) + sum(raw_out)
        semaphores = pltpu.SemaphoreType.DMA((max(len(buffers) + extra, 1),))
        scratch = list(scratch) + buffers + [semaphores]
        kernel = with_moves(kernel, far_in, far_out, extra)
    moved = sum(item.size * item.dtype.itemsize for item in operands)
    return pl.pallas_call(
        kernel,
        name=name,
        out_shape=outs,
        in_specs=specs,
        out_specs=out_specs,
        scratch_shapes=scratch,
        compiler_params=pltpu.CompilerParams(vmem_limit_bytes=room * 1024 * 1024),
        cost_estimate=pl.CostEstimate(
            flops=int(micros * 1.1e9), bytes_accessed=moved, transcendentals=0
        ),
    )(*operands)


plain = ("piece", "sum", "pair", "share", "add", "unpack")


class Far:
    def __init__(self, value):
        self.value = value


class Anywhere(Far):
    pass


class Raw(Far):
    pass


def far_array(*dims, kind=jnp.float32):
    return Far(array(*dims, kind=kind))


def array(*dims, kind=jnp.float32):
    return jax.ShapeDtypeStruct(dims, kind)


def to_packed(values, shape):
    moved = with_layout_constraint(values.transpose(1, 2, 0, 3), Layout((0, 1, 2, 3)))
    moved = moved.reshape(shape.patches, shape.images, shape.tiles, lanes)
    moved = with_layout_constraint(moved, Layout((0, 2, 1, 3)))
    return moved.transpose(0, 2, 1, 3).reshape(shape.packed, lanes)


def from_packed(values, shape):
    moved = values.reshape(shape.patches, shape.tiles, shape.images, lanes).transpose(0, 2, 1, 3)
    moved = moved.reshape(shape.side, shape.side, shape.images, shape.width)
    return moved.transpose(2, 0, 1, 3)


everyone = ("x", "core", "a", "b")


def gather_plainly(units, first, bias, second):
    first = lax.all_gather(first, ("a", "b"), axis=0, tiled=True)
    second = lax.all_gather(second, ("a", "b"), axis=0, tiled=True)
    bias = lax.all_gather(bias, ("a", "b"), axis=0, tiled=True)
    width = first.shape[1]
    rows = jnp.pad(bias.reshape(4, 1, 1, width), ((0, 0), (0, units.shards - 1), (0, 15), (0, 0)))
    shape = (4, units.shards, units.unit, width)
    both = jnp.concatenate([first.reshape(shape), second.reshape(shape), rows], axis=2)
    both = both.reshape(4, units.shards * units.piece_rows, width)
    return [both[index] for index in range(4)]


def total_of(values, parts):
    rows = values.shape[0] // parts
    kernel = functools.partial(sum_kernel, parts)
    values = values.reshape(parts, rows, values.shape[1])
    return call(kernel, "sum", [array(rows, values.shape[2], kind=bf16)], [], 1, 4, values)[0]


def reduce_plainly(shape, units, feed, rest, late):
    width = shape.width
    unit = units.unit
    both = jnp.stack(feed).reshape(4, units.shards, units.feed_rows, width)
    first = both[:, :, :unit].reshape(4 * units.total, width)
    second = both[:, :, unit:].reshape(4 * units.total, width)

    def shared(values):
        part = lax.psum_scatter(values, ("a", "b"), scatter_dimension=0, tiled=True)
        return lax.psum(part, ("x", "core")).astype(f32)

    late = jnp.concatenate(late).reshape(units.late_total, width)
    late = lax.psum(late, everyone).astype(f32)
    head = jnp.concatenate(rest).reshape(units.head_total, width)
    head = lax.psum(head, everyone).astype(f32)
    bias = head[3 * width + 8 : 3 * width + 12].reshape(-1)
    place = lax.axis_index("a") * 2 + lax.axis_index("b")
    size = bias.shape[0] // (lax.axis_size("a") * 2)
    bias = lax.dynamic_slice_in_dim(bias, place * size, size, 0)
    last = width + 8
    vectors = head[3 * width : 3 * width + 8]
    more = late[last + taps : last + taps + 4]
    return (
        more[0],
        more[1],
        jnp.concatenate([head[:width], late[: width + 4]]),
        jnp.concatenate([vectors[5], more[2], more[3, :4]]),
        late[last : last + 9],
        late[last + 9 : last + 34],
        late[last + 34 : last + taps],
        head[width : 2 * width],
        vectors[0],
        head[2 * width : 3 * width],
        vectors[1],
        vectors[2],
        vectors[3],
        shared(first),
        bias,
        shared(second),
        vectors[4],
    )


def shards(
    sizes,
    tokens,
    ln1_gain,
    ln1_bias,
    f_weight,
    f_bias,
    dw_small,
    dw_middle,
    dw_large,
    h_weight,
    h_bias,
    proj_weight,
    proj_bias,
    ln2_gain,
    ln2_bias,
    fc1_weight,
    fc1_bias,
    fc2_weight,
    fc2_bias,
    out_grad,
):
    images, side, _, width = tokens.shape
    shape = Shape(images, side, width)
    rows, grid, inner = shape.rows, shape.grid, shape.inner
    hidden = fc1_weight.shape[1] * sizes["a"] * sizes["b"]
    quick = sizes["x"] == 2 and sizes["a"] * sizes["b"] == 8
    units = Units(8, hidden // 32)
    f_turned = f_weight.T
    first, second = fc1_weight.T, fc2_weight
    scratch = pltpu.VMEM
    core = jnp.zeros((1,), jnp.int32)
    if quick:
        core = lax.axis_index("core").astype(jnp.int32).reshape(1)
        quarter = lax.axis_index("x") * 2 + core[0]
        shard = lax.axis_index("a") * 2 + lax.axis_index("b")
        turn = lax.rem(shard - quarter + units.shards, units.shards) * units.unit
        spots = jnp.stack([quarter, shard, turn]).astype(jnp.int32)
        (pieces,) = call(
            functools.partial(piece_kernel, units, units.shards),
            "piece",
            [array(units.shards * units.piece_rows, width, kind=bf16)],
            [
                scratch((2, units.unit, width), bf16),
                scratch(fc1_bias.shape, bf16),
                pltpu.SemaphoreType.DMA((3,)),
            ],
            1,
            6,
            spots,
            Far(first),
            Far(second),
            Far(fc1_bias),
        )
        weights = exchange(pieces, ("a", "b"))
    tokens_packed = to_packed(tokens, shape)

    def rows_array(kind=bf16):
        return far_array(rows, width, kind=kind)

    small, cot, inputs, normed, query, gates, context, one, slope_one = call(
        functools.partial(entry_kernel, shape),
        "entry",
        [
            far_array(96, width),
            rows_array(),
            array(rows, width),
            rows_array(),
            array(rows, width),
            array(rows, 4 * lanes),
            far_array(grid, lanes),
            array(grid, lanes),
            array(inner, lanes),
        ],
        [
            scratch((taps * sublanes, lanes), f32),
            scratch((shape.packed, lanes), f32),
            scratch((rows, width), f32),
        ],
        5,
        16,
        tokens_packed,
        f_turned,
        to_packed(out_grad, shape),
        dw_small,
        dw_middle,
        dw_large,
        ln1_gain,
        ln1_bias,
        f_bias,
        h_bias,
        proj_bias,
        ln2_gain,
        ln2_bias,
        fc2_bias,
    )
    if quick:
        cot_far = flip(cot, "x")
        cot_core = flip(cot)
    one, gates, query, slope_one, *results = call(
        functools.partial(modulation_kernel, shape),
        "modulation",
        [
            Raw(array(grid, lanes)),
            Raw(array(rows, 4 * lanes)),
            Raw(array(rows, width)),
            Raw(array(inner, lanes)),
            rows_array(f32),
            rows_array(),
            rows_array(),
            rows_array(f32),
            rows_array(),
            far_array(grid, lanes),
            far_array(grid, lanes),
            far_array(inner, lanes),
            far_array(inner, lanes),
            far_array(2 * sublanes, lanes),
        ],
        [scratch((rows, width), f32), scratch((taps * sublanes, lanes), f32)],
        8,
        20,
        one,
        Far(small),
        gates,
        Far(h_weight),
        query,
        inputs,
        Far(proj_weight),
        slope_one,
    )
    modulator, aggregated, mixed, middle, normed_two, *results = results
    two, three, slope_two, slope_three, pooled = results

    def feed(resumed, outs, *operands):
        return call(
            functools.partial(feed_kernel, shape, units, resumed),
            "feed",
            outs,
            [
                scratch((units.total, width), bf16),
                scratch((units.total, width), bf16),
                scratch((2 * units.total, width), f32),
                scratch((8, width), f32),
            ],
            6,
            24,
            *operands,
        )

    near_rows = array(rows, width, kind=bf16)
    feed_total = array(units.shards * units.feed_rows, width, kind=bf16)
    bias_total = array(8, width)
    if quick:
        cot_both = flip(after(cot_far, middle))
        normed_far = flip(normed_two, "x")
        normed_core = flip(normed_two)
        out_own, out_core, d_own, d_core, *carry = feed(
            False,
            [near_rows] * 4 + [array(2 * units.total, width), bias_total],
            weights,
            Far(normed_two),
            normed_core,
            Far(cot),
            cot_core,
        )
        out_core, d_core = flip(out_core), flip(d_core)
        normed_far = after(normed_far, d_own)
        normed_both = flip(normed_far)
        out_far, d_far, both, d_near, out_near, feed_grads, bias_grad = feed(
            True,
            [near_rows] * 2
            + [array(2 * rows, width, kind=bf16), rows_array(f32), rows_array(f32), feed_total]
            + [bias_total],
            weights,
            normed_far,
            normed_both,
            cot_far,
            cot_both,
            *carry,
            d_own,
            d_core,
            out_own,
            out_core,
        )
        arrived = flip(both)
        d_far, out_far = call(
            functools.partial(rows_kernel, shape),
            "rows",
            [near_rows, rows_array()],
            [],
            1,
            8,
            d_far,
            out_far,
            arrived,
        )
        feed_grads = after(feed_grads, d_far)
        d_far = flip(d_far, "x")
        feed_parts = exchange(feed_grads, ("a", "b"))
        mine = (jnp.arange(4) == quarter).astype(f32)
        bias_grads = (mine[:, None, None] * bias_grad).reshape(32, width)
    else:
        out_far = d_far = jnp.zeros((rows, width), bf16)
        out_near, d_near, feed_grads, bias_grads = jnp.zeros((rows, width), f32), 0.0, [], []
        for weights in gather_plainly(units, first, fc1_bias, second):
            out, d_out, grads, bias_grad = feed(
                None, [near_rows, near_rows, feed_total, bias_total], weights, normed_two, cot
            )
            bias_grads.append(bias_grad)
            out_near, d_near = out_near + out.astype(f32), d_near + d_out.astype(f32)
            feed_grads.append(grads)
        bias_grads = jnp.concatenate(bias_grads)
    rest = array(units.pieces, units.head_rows, width, kind=bf16)
    later = [small, gates, pooled, slope_three, slope_two, slope_one, one, two, three]
    d_middle, d_query, d_aggregated, own_rest, other_rest, *fetched = call(
        functools.partial(heads_kernel, shape, units),
        "heads",
        [rows_array(f32), rows_array(), array(rows, width), rest, rest]
        + [array(*item.shape) for item in later],
        [
            scratch((rows, width), f32),
            scratch((rows, width), bf16),
            scratch((units.head_total, width), f32),
            scratch((rows, width), bf16),
        ],
        5,
        16,
        core,
        Far(small),
        Far(cot),
        Far(middle),
        Far(d_near),
        d_far,
        bias_grads,
        Far(proj_weight),
        Far(query),
        Far(modulator),
        Far(h_weight),
        Far(normed),
        Far(aggregated),
        Far(mixed),
        *[Raw(item) for item in later],
    )
    if quick:
        out_far = flip(after(out_far, d_middle), "x")
        rest_arrived = flip(other_rest)
    d_one, d_two, d_three, rounded, d_gates = call(
        functools.partial(levels_back_kernel, shape),
        "levels_back",
        [
            far_array(grid, lanes),
            far_array(grid, lanes),
            far_array(grid, lanes),
            rows_array(),
            far_array(rows, lanes, kind=bf16),
        ],
        [
            scratch((taps * sublanes, lanes), f32),
            scratch((3 * inner, lanes), f32),
            scratch((rows, 4 * lanes), f32),
            scratch((rows, width), f32),
        ],
        8,
        24,
        fetched[0],
        fetched[1],
        d_aggregated,
        *fetched[2:],
    )
    if quick:
        (rest_half,) = call(pair_kernel, "pair", [rest], [], 1, 4, own_rest, rest_arrived)
        feed_parts = after(feed_parts, d_one)
        piece = total_of(feed_parts, units.shards)
        rest_half = after(rest_half, piece)
        d_one = after(d_one, rest_half, out_far)
        shares = rest_half.shape
        rest_parts = exchange(rest_half.reshape(-1, width), ("x", "b"))
        rest_parts = rest_parts.reshape(4, shares[0] * shares[1] // 4, width)
    late = array(units.pieces, units.late_rows, width, kind=bf16)
    d_inputs, own_late, other_late = call(
        functools.partial(exit_kernel, shape, units),
        "exit",
        [rows_array(f32), late, late],
        [
            scratch((shape.packed, lanes), f32),
            scratch((taps * sublanes, lanes), f32),
            scratch((rows, width), f32),
            scratch((rows, width), f32),
            scratch((units.late_total, width), f32),
            scratch((lanes, width), bf16),
        ],
        9,
        24,
        core,
        Far(two),
        Far(d_three),
        Far(one),
        Far(d_two),
        Far(context),
        Far(d_one),
        Far(rounded),
        Far(d_gates),
        Far(small),
        Far(normed),
        Far(f_turned),
        Far(d_query),
        Far(tokens_packed),
    )
    if quick:
        late_arrived = flip(other_late)
        rest_parts = after(rest_parts, own_late)
        (late_half,) = call(pair_kernel, "pair", [late], [], 1, 4, own_late, late_arrived)
        late_half, rest_parts = lax.optimization_barrier((late_half, rest_parts))
        late_parts = exchange(late_half.reshape(-1, width), ("x", "b"))
        late_parts = late_parts.reshape(4, units.pieces * units.late_rows // 4, width)
        d_inputs = after(d_inputs, late_half)
    tokens_grad, block_out = call(
        functools.partial(finish_kernel, shape),
        "finish",
        [far_array(shape.packed, lanes), far_array(shape.packed, lanes)],
        [scratch((rows, width), f32)],
        3,
        16,
        Far(d_middle),
        Far(d_inputs),
        Far(small),
        Far(middle),
        Far(out_near),
        Anywhere(out_far),
    )
    if quick:
        late_parts = after(late_parts, tokens_grad)
        share_rows = units.pieces * units.share // 4
        (share,) = call(
            share_kernel,
            "share",
            [array(share_rows, width, kind=bf16)],
            [],
            1,
            8,
            rest_parts,
            late_parts,
        )
        piece = after(piece, share)
        piece_x = flip(piece, "x")
        piece_core, piece_both = flip(piece), flip(piece_x)
        own = share
        for bit in (1, 2):
            arrived = flip(own, "a", sizes["a"], bit)
            if bit == 2:
                arrived = after(arrived, piece_core, piece_both)
            (own,) = call(
                add_kernel, "add", [array(share_rows, width, kind=bf16)], [], 1, 6, own, arrived
            )
        held_b, held_x = flip(own, "b"), flip(own, "x")
        held_both = flip(held_b, "x")
        held = [own, held_b, held_x, held_both]
        held = held + [flip(item) for item in held]
        turn = lax.rem(units.shards - shard, units.shards) * units.unit
        spots = [core[0], quarter, turn] + [lax.axis_index(axis) for axis in ("x", "b")]
        spots = jnp.stack(spots).astype(jnp.int32)
        total = 4 * units.unit
        others = call(
            functools.partial(unpack_kernel, shape, units),
            "unpack",
            [
                array(width),
                array(width),
                array(2 * width + 4, width),
                array(2 * width + 4),
                array(9, width),
                array(25, width),
                array(49, width),
                array(width, width),
                array(width),
                array(width, width),
                array(width),
                array(width),
                array(width),
                array(total, width),
                array(total),
                array(total, width),
                array(width),
            ],
            [
                scratch((2 * units.pieces * units.share, width), f32),
                scratch((units.head_total, width), f32),
                scratch((units.late_total, width), f32),
            ],
            2,
            16,
            spots,
            piece,
            piece_x,
            piece_core,
            piece_both,
            *held,
        )
    else:
        others = reduce_plainly(
            shape, units, feed_grads, (own_rest, other_rest), (own_late, other_late)
        )
    others = list(others)
    others[2] = others[2].T
    others[13] = others[13].T
    return from_packed(block_out, shape), from_packed(tokens_grad, shape), *others


def solution(mesh):
    img, mlp = mesh.shape["img"], mesh.shape["mlp"]
    sizes = {"x": img // 2, "core": 2, "a": mlp // 2, "b": 2}
    finer = Mesh(mesh.devices.reshape(*sizes.values()), everyone)
    images = P(everyone, None, None, None)
    hidden = ("a", "b")
    return jax.shard_map(
        functools.partial(shards, sizes),
        mesh=finer,
        in_specs=(images,)
        + (P(),) * 13
        + (P(None, hidden), P(hidden), P(hidden, None), P(), images),
        out_specs=(images, images)
        + (P(),) * 13
        + (P(None, hidden), P(hidden), P(hidden, None), P()),
        check_vma=False,
    )
```

```python
import functools
import math

import jax
import jax.numpy as jnp
from jax import lax
from jax.experimental import pallas as pl
from jax.experimental.pallas import tpu as pltpu
from jax.experimental.layout import Layout, with_layout_constraint
from jax.sharding import Mesh
from jax.sharding import PartitionSpec as P

epsilon = 1e-05
lanes = 128
sublanes = 8
edge = 3
extents = (3, 5, 7)
starts = (0, 9, 34)
taps = 83
LN1_GAIN, LN1_BIAS, QUERY_BIAS, CONTEXT_BIAS, GATE_BIAS = 83, 84, 85, 86, 87
H_BIAS, PROJ_BIAS, LN2_GAIN, LN2_BIAS, FC2_BIAS = 88, 89, 90, 91, 92
f32 = jnp.float32
bf16 = jnp.bfloat16


def flip(values, axis="core", size=2, bit=1):
    return lax.ppermute(values, axis, [(place, place ^ bit) for place in range(size)])


def exchange(values, axes):
    return lax.all_to_all(values, axes, split_axis=0, concat_axis=0, tiled=True)


def after(values, *others):
    return lax.optimization_barrier((values,) + others)[0]


def nn(left, right):
    return jnp.dot(left, right, preferred_element_type=f32)


def nt(left, right):
    return lax.dot_general(left, right, (((1,), (1,)), ((), ())), preferred_element_type=f32)


def tn(left, right):
    return lax.dot_general(left, right, (((0,), (0,)), ((), ())), preferred_element_type=f32)


def gelu_pair(values):
    below = 0.5 * (1.0 + lax.erf(values * math.sqrt(0.5)))
    density = jnp.exp(values * values * -0.5) * (1.0 / math.sqrt(2.0 * math.pi))
    return values * below, below + values * density


class Shape:
    def __init__(self, images, side, width):
        self.images, self.side, self.width = images, side, width
        self.tiles = width // lanes
        self.slots = images * self.tiles
        self.patches = side * side
        self.segment = -(-self.patches // 8) * 8
        self.rows = images * self.segment
        self.line = side * sublanes
        self.centre = edge * self.line
        self.grid = (side + 2 * edge) * self.line
        self.inner = side * self.line
        self.packed = self.patches * self.slots
        self.block = next(size for size in (80, 40, 16, 8) if self.rows % size == 0)

    def places(self):
        return [
            (image, tile, tile * self.images + image)
            for image in range(self.images)
            for tile in range(self.tiles)
        ]


def columns(tile):
    return slice(tile * lanes, (tile + 1) * lanes)


def unpack(shape, packed, rows):
    for image, tile, slot in shape.places():
        first = image * shape.segment
        rows[first : first + shape.patches, columns(tile)] = packed[
            pl.ds(slot, shape.patches, stride=shape.slots), :
        ]
    for image in range(shape.images):
        first = image * shape.segment
        spare = shape.segment - shape.patches
        if spare:
            rows[first + shape.patches : first + shape.segment, 0 : shape.width] = jnp.zeros(
                (spare, shape.width), f32
            )


def pack(shape, rows, packed):
    for image, tile, slot in shape.places():
        first = image * shape.segment
        packed[pl.ds(slot, shape.patches, stride=shape.slots), :] = rows[
            first : first + shape.patches, columns(tile)
        ]


def blocks(shape, body, init=None):
    def step(index, carry):
        first = pl.multiple_of(index * shape.block, shape.block)
        return body(pl.ds(first, shape.block), carry)

    return lax.fori_loop(0, shape.rows // shape.block, step, init)


def normalise(values):
    average = jnp.mean(values, axis=-1, keepdims=True)
    centred = values - average
    variance = jnp.mean(centred * centred, axis=-1, keepdims=True)
    scale = lax.rsqrt(variance + epsilon)
    return centred * scale, scale


def norm_back(values, grad, gain):
    unit, scale = normalise(values)
    inner = grad * gain
    first = jnp.mean(inner, axis=-1, keepdims=True)
    second = jnp.mean(inner * unit, axis=-1, keepdims=True)
    return scale * (inner - first - unit * second), grad * unit


def fold(values):
    return jnp.sum(values.reshape(values.shape[0] // 8, 8, values.shape[1]), axis=0)


def row_sum(values):
    return jnp.sum(values, axis=0, keepdims=True)


def spread_taps(shape, small, tap_ref):
    tap_ref[...] = jnp.zeros_like(tap_ref)
    for _, tile, slot in shape.places():
        tap_ref[pl.ds(slot, taps, stride=sublanes), :] = small[0:taps, columns(tile)]


def line_at(shape, ref, line):
    first = pl.multiple_of(line * shape.line, shape.line)
    values = ref[pl.ds(first, shape.line), :]
    return [values[w * sublanes : (w + 1) * sublanes] for w in range(shape.side)]


def correlate(shape, source, tap_ref, level, line, turned):
    extent = extents[level]
    reach = extent // 2
    totals = [None] * shape.side
    for down in range(extent):
        values = line_at(shape, source, line + down + edge - reach)
        for along in range(extent):
            entry = down * extent + along
            if turned:
                entry = extent * extent - 1 - entry
            tap = tap_ref[pl.ds((starts[level] + entry) * sublanes, sublanes), :]
            for w in range(shape.side):
                other = w + along - reach
                if 0 <= other < shape.side:
                    term = values[other] * tap
                    totals[w] = term if totals[w] is None else totals[w] + term
    return jnp.concatenate(totals, axis=0)


def tap_grads(shape, source, grad, level, out):
    extent = extents[level]
    reach = extent // 2
    for down in range(extent):

        def step(line, totals, down=down):
            values = line_at(shape, source, line + down + edge - reach)
            grads = line_at(shape, grad, line + edge)
            result = []
            for along in range(extent):
                total = totals[along]
                for w in range(shape.side):
                    other = w + along - reach
                    if 0 <= other < shape.side:
                        total = total + values[other] * grads[w]
                result.append(total)
            return tuple(result)

        zero = jnp.zeros((sublanes, lanes), f32)
        first, last = max(0, reach - down), min(shape.side, shape.side + reach - down)
        totals = lax.fori_loop(first, last, step, (zero,) * extent)
        for along in range(extent):
            out[pl.ds((starts[level] + down * extent + along) * sublanes, sublanes), :] = totals[
                along
            ]


def clear_edges(shape, ref):
    zeros = jnp.zeros((shape.centre, lanes), f32)
    ref[0 : shape.centre, :] = zeros
    ref[shape.centre + shape.inner : shape.grid, :] = zeros


def gate_values(shape, normed, f_turned, small, gates):
    weight = f_turned[2 * shape.width : 2 * shape.width + 4, :].astype(f32)
    wide = jnp.concatenate(
        [jnp.broadcast_to(weight[g : g + 1], (lanes, shape.width)) for g in range(4)]
    ).astype(bf16)
    bias = small[GATE_BIAS : GATE_BIAS + 1, :]
    wide_bias = jnp.concatenate(
        [jnp.broadcast_to(bias[:, g : g + 1], (1, lanes)) for g in range(4)], axis=1
    )
    gates[...] = nt(normed[...], wide) + wide_bias


def level_rows(shape, level, image, slot):
    return level[pl.ds(shape.centre + slot, shape.segment, stride=sublanes), :]


def run_levels(shape, moves, chain, tap_ref):
    total = jnp.zeros((sublanes, lanes), f32)
    for level, source, target, slope in chain:
        clear_edges(shape, target)

        def line_step(line, total, level=level, source=source, target=target, slope=slope):
            before = correlate(shape, source, tap_ref, level, line, False)
            value, rise = gelu_pair(before)
            here = pl.multiple_of((line + edge) * shape.line, shape.line)
            target[pl.ds(here, shape.line), :] = value
            slope[pl.ds(pl.multiple_of(line * shape.line, shape.line), shape.line), :] = rise
            if level == 2:
                total = total + fold(value)
            return total

        total = lax.fori_loop(0, shape.side, line_step, total)
        moves.leave(target, slope)
    return total


def entry_kernel(
    shape,
    moves,
    tokens,
    f_turned,
    out_grad,
    dw_small,
    dw_middle,
    dw_large,
    ln1_gain,
    ln1_bias,
    f_bias,
    h_bias,
    proj_bias,
    ln2_gain,
    ln2_bias,
    fc2_bias,
    small,
    cot,
    inputs,
    normed,
    query,
    gates,
    context,
    one,
    slope_one,
    tap_ref,
    packed,
    wide,
):
    width = shape.width
    for source, first in zip((dw_small, dw_middle, dw_large), starts):
        small[first : first + source.shape[0], :] = source[...].astype(f32)
    shared = f_bias[...].astype(f32).reshape(1, 2 * width + 4)
    vectors = {
        QUERY_BIAS: shared[:, 0:width],
        CONTEXT_BIAS: shared[:, width : 2 * width],
        GATE_BIAS: jnp.concatenate(
            [shared[:, 2 * width :], jnp.zeros((1, width - 4), f32)], axis=1
        ),
    }
    for row, source in (
        (LN1_GAIN, ln1_gain),
        (LN1_BIAS, ln1_bias),
        (H_BIAS, h_bias),
        (PROJ_BIAS, proj_bias),
        (LN2_GAIN, ln2_gain),
        (LN2_BIAS, ln2_bias),
        (FC2_BIAS, fc2_bias),
    ):
        vectors[row] = source[...].astype(f32).reshape(1, width)
    for row, value in vectors.items():
        small[row : row + 1, :] = value
    last = FC2_BIAS + 1
    small[last:, :] = jnp.zeros((small.shape[0] - last, width), f32)
    moves.leave(small)
    moves.arrive(tokens)
    packed[...] = tokens[...].astype(f32)
    unpack(shape, packed, inputs)
    moves.leave(inputs)
    spread_taps(shape, small, tap_ref)
    gain = small[LN1_GAIN : LN1_GAIN + 1, :]
    bias = small[LN1_BIAS : LN1_BIAS + 1, :]

    def first_norm(rows, carry):
        unit, _ = normalise(inputs[rows, :])
        normed[rows, :] = (unit * gain + bias).astype(bf16)
        return carry

    blocks(shape, first_norm, 0)
    moves.leave(normed)
    moves.arrive(out_grad)
    packed[...] = out_grad[...].astype(f32)
    unpack(shape, packed, wide)
    cot[...] = wide[...].astype(bf16)
    moves.leave(cot)
    moves.arrive(f_turned)
    wide[...] = (
        nt(normed[...], f_turned[width : 2 * width, :]) + small[CONTEXT_BIAS : CONTEXT_BIAS + 1, :]
    )
    context[...] = jnp.zeros_like(context)
    for image, tile, slot in shape.places():
        first = image * shape.segment
        context[pl.ds(shape.centre + slot, shape.patches, stride=sublanes), :] = wide[
            first : first + shape.patches, columns(tile)
        ]
    moves.leave(context)
    query[...] = nt(normed[...], f_turned[0:width, :]) + small[QUERY_BIAS : QUERY_BIAS + 1, :]
    moves.leave(query)
    gate_values(shape, normed, f_turned, small, gates)
    moves.leave(gates)
    run_levels(shape, moves, ((0, context, one, slope_one),), tap_ref)


def modulation_kernel(
    shape,
    moves,
    one,
    small,
    gates,
    h_weight,
    query,
    inputs,
    proj_weight,
    slope_one,
    far_one,
    far_gates,
    far_query,
    far_slope,
    modulator,
    aggregated,
    mixed,
    middle,
    normed_two,
    two,
    three,
    slope_two,
    slope_three,
    pooled,
    wide,
    tap_ref,
):
    chain = ((1, one, two, slope_two), (2, two, three, slope_three))
    moves.arrive(small)
    spread_taps(shape, small, tap_ref)
    moves.copy(one, far_one)
    moves.copy(gates, far_gates)
    moves.copy(query, far_query)
    moves.copy(slope_one, far_slope)
    total = run_levels(shape, moves, chain, tap_ref)
    value, rise = gelu_pair(total * (1.0 / shape.patches))
    pooled[0:sublanes, :] = value
    pooled[sublanes : 2 * sublanes, :] = rise * (1.0 / shape.patches)
    moves.leave(pooled)
    moves.arrive(h_weight, proj_weight)
    for image, tile, slot in shape.places():
        rows = pl.ds(image * shape.segment, shape.segment)
        wide[rows, columns(tile)] = (
            level_rows(shape, one, image, slot) * gates[rows, columns(0)]
            + level_rows(shape, two, image, slot) * gates[rows, columns(1)]
            + level_rows(shape, three, image, slot) * gates[rows, columns(2)]
            + value[slot : slot + 1] * gates[rows, columns(3)]
        )
    aggregated[...] = wide[...].astype(bf16)
    moves.leave(aggregated)
    modulator[...] = nn(aggregated[...], h_weight[...]) + small[H_BIAS : H_BIAS + 1, :]

    moves.leave(modulator)

    def mix(rows, carry):
        mixed[rows, :] = (query[rows, :] * modulator[rows, :]).astype(bf16)
        return carry

    blocks(shape, mix, 0)
    moves.leave(mixed)
    middle[...] = (
        inputs[...] + nn(mixed[...], proj_weight[...]) + small[PROJ_BIAS : PROJ_BIAS + 1, :]
    )
    moves.leave(middle)
    gain = small[LN2_GAIN : LN2_GAIN + 1, :]
    bias = small[LN2_BIAS : LN2_BIAS + 1, :]

    def second_norm(rows, carry):
        unit, _ = normalise(middle[rows, :])
        normed_two[rows, :] = (unit * gain + bias).astype(bf16)
        return carry

    blocks(shape, second_norm, 0)


class Moves:
    def __init__(self):
        self.incoming, self.outgoing = {}, {}
        self.started, self.free = [], []

    def copy(self, source, target):
        move = pltpu.make_async_copy(source, target, self.free.pop())
        move.start()
        self.started.append(move)

    def arrive(self, *buffers):
        for buffer in buffers:
            move = self.incoming.pop(id(buffer), None)
            if move is not None:
                move.wait()

    def leave(self, *buffers):
        for buffer in buffers:
            move = self.outgoing.pop(id(buffer), None)
            if move is not None:
                move.start()
                self.started.append(move)

    def finish(self):
        for move in list(self.incoming.values()):
            move.wait()
        for move in list(self.outgoing.values()):
            move.start()
            self.started.append(move)
        for move in self.started:
            move.wait()


def with_moves(kernel, far_in, far_out, extra):
    def run(*refs):
        refs = list(refs)
        ins, refs = refs[: len(far_in)], refs[len(far_in) :]
        outs, refs = refs[: len(far_out)], refs[len(far_out) :]
        semaphores = refs.pop()
        count = sum(far_in) + sum(far_out)
        buffers, scratch = refs[len(refs) - count :], refs[: len(refs) - count]
        moves = Moves()
        moves.free = [semaphores.at[count + spare] for spare in range(extra)]
        index = 0
        for group, flags, table in (
            (ins, far_in, moves.incoming),
            (outs, far_out, moves.outgoing),
        ):
            for place, far in enumerate(flags):
                if far:
                    buffer, outer = buffers[index], group[place]
                    pair = (outer, buffer) if group is ins else (buffer, outer)
                    move = pltpu.make_async_copy(*pair, semaphores.at[index])
                    if group is ins:
                        move.start()
                    table[id(buffer)] = move
                    group[place] = buffer
                    index += 1
        kernel(moves, *ins, *outs, *scratch)
        moves.finish()

    return run


class Units:
    def __init__(self, shards, unit):
        self.shards, self.unit = shards, unit
        self.piece_rows = 2 * unit + 16
        self.feed_rows = 2 * unit
        self.total = shards * unit
        self.head_rows, self.late_rows = 40, 16
        self.pieces = 2 * shards
        self.share = self.head_rows + self.late_rows
        self.head_total = 2 * self.pieces * self.head_rows
        self.late_total = 2 * self.pieces * self.late_rows


def sum_kernel(parts, source, out):
    size = out.shape[0]
    block = 16 if size % 16 == 0 else size

    def step(index, carry):
        rows = pl.ds(pl.multiple_of(index * block, block), block)
        total = source[0, rows, :].astype(f32)
        for part in range(1, parts):
            total = total + source[part, rows, :].astype(f32)
        out[rows, :] = total.astype(bf16)
        return carry

    lax.fori_loop(0, size // block, step, 0)


def pair_kernel(first, second, out):
    for part in range(out.shape[0]):
        total = first[part].astype(f32) + second[part].astype(f32)
        out[part] = total.astype(bf16)


def rows_kernel(shape, moves, first, second, arrived, first_out, second_out):
    def step(index, carry):
        rows = pl.ds(pl.multiple_of(index * 16, 16), 16)
        more = pl.ds(pl.multiple_of(index * 16 + shape.rows, 16), 16)
        first_out[rows, :] = (first[rows, :].astype(f32) + arrived[rows, :].astype(f32)).astype(bf16)
        second_out[rows, :] = (second[rows, :].astype(f32) + arrived[more, :].astype(f32)).astype(
            bf16
        )
        return carry

    lax.fori_loop(0, shape.rows // 16, step, 0)


def share_kernel(head_parts, late_parts, out):
    sums = []
    for parts in (head_parts, late_parts):
        total = parts[0].astype(f32)
        for part in range(1, parts.shape[0]):
            total = total + parts[part].astype(f32)
        sums.append(total)
    out[...] = jnp.concatenate(sums).astype(bf16)


def add_kernel(first, second, out):
    out[...] = (first[...].astype(f32) + second[...].astype(f32)).astype(bf16)


def piece_kernel(units, copies, spots, first, second, far_bias, out, own, bias, semaphores):
    unit = units.unit
    width = first.shape[1]
    rows = pl.ds(pl.multiple_of(spots[0] * unit, 16), unit)
    moves = [
        pltpu.make_async_copy(source.at[rows, :], own.at[index], semaphores.at[index])
        for index, source in enumerate((first, second))
    ]
    moves.insert(0, pltpu.make_async_copy(far_bias, bias, semaphores.at[2]))
    for move in moves:
        move.start()
    moves.pop(0).wait()
    shard = spots[1]
    values = bias[...].astype(f32).reshape(1, bias.shape[0])
    values = jnp.concatenate([values, jnp.zeros((1, width - bias.shape[0]), f32)], axis=1)
    values = pltpu.roll(jnp.broadcast_to(values, (8, width)), spots[2], 1)
    lane = lax.broadcasted_iota(jnp.int32, (8, width), 1) - shard * unit
    row = lax.broadcasted_iota(jnp.int32, (8, width), 0)
    values = jnp.where((lane >= 0) & (lane < unit) & (row == 0), values, 0.0)
    line = jnp.concatenate([values, jnp.zeros((8, width), f32)]).astype(bf16)
    for move in moves:
        move.wait()
    for copy in range(copies):
        base = copy * units.piece_rows
        out[base : base + unit, :] = own[0]
        out[base + unit : base + 2 * unit, :] = own[1]
        out[base + 2 * unit : base + units.piece_rows, :] = line


def feed_kernel(shape, units, resumed, moves, weights, *refs):
    refs = list(refs)

    def take(count):
        taken = refs[:count]
        del refs[:count]
        return taken

    groups = 1 if resumed is None else 2
    closing = resumed is not False
    normed, cots = take(groups), take(groups)
    if resumed:
        old_grads, old_bias, *near = take(6)
    if resumed:
        out, d_out, both = take(3)
        outs = [out, both.at[shape.rows : 2 * shape.rows, :]]
        d_outs = [d_out, both.at[0 : shape.rows, :]]
        d_near, out_near = take(2)
    else:
        outs, d_outs = take(groups), take(groups)
    grads, bias_grad = take(2)
    first_weight, second_weight, total_grads, total_bias = take(4)
    unit, width = units.unit, shape.width
    bias = None
    for shard in range(units.shards):
        base, here = shard * units.piece_rows, shard * unit
        first_weight[here : here + unit, :] = weights[base : base + unit, :]
        second_weight[here : here + unit, :] = weights[base + unit : base + 2 * unit, :]
        term = weights[base + 2 * unit : base + units.piece_rows, :].astype(f32)
        bias = term if bias is None else bias + term
    bias = bias[0:1]
    if resumed:
        moves.arrive(*near)
        for target, own, arrived in ((d_near, near[0], near[1]), (out_near, near[2], near[3])):
            target[...] = own[...].astype(f32) + arrived[...].astype(f32)
            moves.leave(target)
    for group in range(groups):
        moves.arrive(normed[group], cots[group])
        rows, cot = normed[group], cots[group]
        value, rise = gelu_pair(nt(rows[...], first_weight[...]) + bias)
        hidden = value.astype(bf16)
        outs[group][...] = nn(hidden, second_weight[...]).astype(bf16)
        d_before = (nt(cot[...], second_weight[...]) * rise).astype(bf16)
        d_outs[group][...] = nn(d_before, first_weight[...]).astype(bf16)
        moves.leave(outs[group], d_outs[group])
        first, second = tn(d_before, rows[...]), tn(hidden, cot[...])
        line = fold(d_before.astype(f32))
        if group == 0 and not resumed:
            total_grads[0 : units.total, :] = first
            total_grads[units.total :, :] = second
            total_bias[...] = line
        elif group == 0:
            total_grads[0 : units.total, :] = old_grads[0 : units.total, :] + first
            total_grads[units.total :, :] = old_grads[units.total :, :] + second
            total_bias[...] = old_bias[...] + line
        else:
            total_grads[0 : units.total, :] += first
            total_grads[units.total :, :] += second
            total_bias[...] += line
    if not closing:
        grads[...] = total_grads[...]
        bias_grad[...] = total_bias[...]
        return
    bias_grad[...] = total_bias[...]
    for shard in range(units.shards):
        base, here = shard * units.feed_rows, shard * unit
        more = units.total + here
        grads[base : base + units.feed_rows, :] = jnp.concatenate(
            [total_grads[here : here + unit, :], total_grads[more : more + unit, :]]
        ).astype(bf16)


def heads_kernel(
    shape,
    units,
    moves,
    core,
    small,
    cot,
    middle,
    d_near,
    d_far,
    bias_grads,
    proj_weight,
    query,
    modulator,
    h_weight,
    normed,
    aggregated,
    mixed,
    *refs,
):
    later, refs = refs[:9], refs[9:]
    d_middle, d_query, d_aggregated, own_rest, other_rest, *refs = refs
    fetched, refs = refs[:9], refs[9:]
    heads_body(
        shape,
        units,
        moves,
        core,
        small,
        cot,
        middle,
        d_near,
        d_far,
        bias_grads,
        proj_weight,
        query,
        modulator,
        h_weight,
        normed,
        aggregated,
        mixed,
        list(zip(later, fetched)),
        d_middle,
        d_query,
        d_aggregated,
        own_rest,
        other_rest,
        *refs,
    )


def heads_body(
    shape,
    units,
    moves,
    core,
    small,
    cot,
    middle,
    d_near,
    d_far,
    bias_grads,
    proj_weight,
    query,
    modulator,
    h_weight,
    normed,
    aggregated,
    mixed,
    later,
    d_middle,
    d_query,
    d_aggregated,
    own_rest,
    other_rest,
    d_mixed,
    d_modulator,
    head,
    d_branch,
):
    width = shape.width
    zero = jnp.zeros((8, width), f32)
    moves.arrive(small, cot, middle, d_near)
    for source, target in later:
        moves.copy(source, target)
    gain = small[LN2_GAIN : LN2_GAIN + 1, :]

    def second_norm(rows, carry):
        grads = d_near[rows, :] + d_far[rows, :].astype(f32)
        cots = cot[rows, :].astype(f32)
        d_input, d_gain = norm_back(middle[rows, :], grads, gain)
        d_total = cots + d_input
        d_middle[rows, :] = d_total
        rounded = d_total.astype(bf16)
        d_branch[rows, :] = rounded
        added = (d_gain, grads, rounded.astype(f32), cots)
        return tuple(total + fold(item) for total, item in zip(carry, added))

    d_gain, d_bias, proj_bias, out_bias = blocks(shape, second_norm, (zero,) * 4)
    moves.leave(d_middle)
    moves.arrive(proj_weight)
    d_mixed[...] = nt(d_branch[...], proj_weight[...])
    moves.arrive(query, modulator)

    def split(rows, carry):
        values = d_mixed[rows, :]
        for_query = (values * modulator[rows, :]).astype(bf16)
        for_modulator = (values * query[rows, :]).astype(bf16)
        d_query[rows, :] = for_query
        d_modulator[rows, :] = for_modulator
        return carry[0] + fold(for_query.astype(f32)), carry[1] + fold(for_modulator.astype(f32))

    query_bias, h_bias = blocks(shape, split, (zero, zero))
    moves.leave(d_query)
    moves.arrive(h_weight)
    d_aggregated[...] = nt(d_modulator[...], h_weight[...])
    moves.leave(d_aggregated)
    moves.arrive(normed, aggregated, mixed)
    head[0:width, :] = tn(d_query[...], normed[...])
    head[width : 2 * width, :] = tn(aggregated[...], d_modulator[...])
    head[2 * width : 3 * width, :] = tn(mixed[...], d_branch[...])
    sums = (h_bias, proj_bias, d_gain, d_bias, out_bias, query_bias)
    head[3 * width :, :] = jnp.concatenate(
        [row_sum(item) for item in sums]
        + [jnp.zeros((2, width), f32)]
        + [row_sum(bias_grads[8 * index : 8 * index + 8, :]) for index in range(4)]
        + [jnp.zeros((units.head_total - 3 * width - 12, width), f32)]
    )
    for half, target in enumerate((own_rest, other_rest)):
        absolute = jnp.bitwise_xor(core[0], half)
        for piece in range(units.pieces):
            first = (absolute * units.pieces + piece) * units.head_rows
            target[piece] = head[pl.ds(pl.multiple_of(first, 8), units.head_rows), :].astype(bf16)


def levels_back_kernel(
    shape,
    moves,
    small,
    gates,
    d_aggregated,
    pooled,
    slope_three,
    slope_two,
    slope_one,
    one,
    two,
    three,
    d_one,
    d_two,
    d_three,
    rounded,
    d_gates,
    tap_ref,
    d_levels,
    products,
    d_context,
):
    width = shape.width
    inner = shape.inner
    moves.arrive(small)
    spread_taps(shape, small, tap_ref)
    for ref in (d_one, d_two, d_three):
        clear_edges(shape, ref)
    moves.arrive(gates, d_aggregated, pooled)
    pool_grad = [None] * sublanes
    for image in range(shape.images):
        rows = pl.ds(image * shape.segment, shape.segment)
        for tile in range(shape.tiles):
            slot = tile * shape.images + image
            values = d_aggregated[rows, columns(tile)]
            for level in range(3):
                d_levels[pl.ds(level * inner + slot, shape.patches, stride=sublanes), :] = (
                    values[: shape.patches] * gates[rows, columns(level)][: shape.patches]
                )
            pool_grad[slot] = jnp.sum(values * gates[rows, columns(3)], axis=0, keepdims=True)
    blank = jnp.zeros((1, lanes), f32)
    pool_grad = jnp.concatenate([blank if item is None else item for item in pool_grad])
    pool_grad = pool_grad * pooled[sublanes : 2 * sublanes, :]
    wide_pool = jnp.concatenate([pool_grad] * shape.side)

    def third(line, carry):
        here = pl.multiple_of(line * shape.line, shape.line)
        value = (d_levels[pl.ds(2 * inner + here, shape.line), :] + wide_pool) * slope_three[
            pl.ds(here, shape.line), :
        ]
        d_three[pl.ds(here + shape.centre, shape.line), :] = value
        return carry

    moves.arrive(slope_three)
    lax.fori_loop(0, shape.side, third, 0)
    moves.leave(d_three)
    moves.arrive(slope_two, slope_one)
    for level, source, target, slope in ((2, d_three, d_two, slope_two), (1, d_two, d_one, slope_one)):

        def back(line, carry, level=level, source=source, target=target, slope=slope):
            here = pl.multiple_of(line * shape.line, shape.line)
            value = correlate(shape, source, tap_ref, level, line, True)
            value = (value + d_levels[pl.ds((level - 1) * inner + here, shape.line), :]) * slope[
                pl.ds(here, shape.line), :
            ]
            target[pl.ds(here + shape.centre, shape.line), :] = value
            return carry

        lax.fori_loop(0, shape.side, back, 0)
        moves.leave(target)

    def back_context(line, carry):
        here = pl.multiple_of(line * shape.line, shape.line)
        d_levels[pl.ds(here, shape.line), :] = correlate(shape, d_one, tap_ref, 0, line, True)
        return carry

    lax.fori_loop(0, shape.side, back_context, 0)
    for image, tile, slot in shape.places():
        first = image * shape.segment
        d_context[first : first + shape.patches, columns(tile)] = d_levels[
            pl.ds(slot, shape.patches, stride=sublanes), :
        ]
        if tile == 0 and shape.segment > shape.patches:
            d_context[first + shape.patches : first + shape.segment, :] = jnp.zeros(
                (shape.segment - shape.patches, width), f32
            )
    rounded[...] = d_context[...].astype(bf16)
    moves.leave(rounded)
    moves.arrive(one, two, three)
    for image in range(shape.images):
        rows = pl.ds(image * shape.segment, shape.segment)
        totals = [None] * 4
        for tile in range(shape.tiles):
            slot = tile * shape.images + image
            values = d_aggregated[rows, columns(tile)]
            for level, ref in enumerate((one, two, three)):
                term = values * level_rows(shape, ref, image, slot)
                totals[level] = term if tile == 0 else totals[level] + term
            term = values * pooled[slot : slot + 1, :]
            totals[3] = term if tile == 0 else totals[3] + term
        for gate in range(4):
            products[rows, columns(gate)] = totals[gate]
    chooser = (
        lax.broadcasted_iota(jnp.int32, (4 * lanes, lanes), 0) // lanes
        == lax.broadcasted_iota(jnp.int32, (4 * lanes, lanes), 1)
    ).astype(f32).astype(bf16)
    d_gates[...] = nn(products[...].astype(bf16), chooser).astype(bf16)


def exit_kernel(
    shape,
    units,
    moves,
    core,
    two,
    d_three,
    one,
    d_two,
    context,
    d_one,
    rounded,
    d_gates,
    small,
    normed,
    f_turned,
    d_query,
    tokens,
    d_inputs,
    own_late,
    other_late,
    packed,
    tap_grad,
    inputs,
    d_context,
    gathered,
    gate_rows,
):
    width = shape.width
    moves.arrive(two, d_three)
    tap_grads(shape, two, d_three, 2, tap_grad)
    moves.arrive(one, d_two)
    tap_grads(shape, one, d_two, 1, tap_grad)
    moves.arrive(context, d_one)
    tap_grads(shape, context, d_one, 0, tap_grad)
    moves.arrive(rounded, d_gates, small, normed, f_turned, d_query, tokens)
    gathered[0:width, :] = tn(rounded[...], normed[...])
    gathered[width : width + 8, :] = tn(d_gates[...], normed[...])[0:8]
    for tile in range(shape.tiles):
        total = None
        for image in range(shape.images):
            slot = tile * shape.images + image
            term = tap_grad[pl.ds(slot, taps, stride=sublanes), :]
            total = term if total is None else total + term
        gathered[width + 8 : width + 8 + taps, columns(tile)] = total
    gate_rows[...] = jnp.concatenate(
        [
            f_turned[2 * width : 2 * width + 4, :].astype(f32),
            jnp.zeros((lanes - 4, width), f32),
        ]
    ).astype(bf16)
    d_normed = d_context
    gate_bias = row_sum(fold(d_gates[...].astype(f32)))
    context_bias = row_sum(fold(rounded[...].astype(f32)))
    d_normed[...] = (
        nn(d_query[...], f_turned[0:width, :])
        + nn(rounded[...], f_turned[width : 2 * width, :])
        + nn(d_gates[...], gate_rows[...])
    )
    packed[...] = tokens[...].astype(f32)
    unpack(shape, packed, inputs)
    gain = small[LN1_GAIN : LN1_GAIN + 1, :]
    zero = jnp.zeros((8, width), f32)

    def finish(rows, carry):
        values = d_normed[rows, :]
        d_input, d_gain = norm_back(inputs[rows, :], values, gain)
        d_inputs[rows, :] = d_input
        return carry[0] + fold(d_gain), carry[1] + fold(values)

    d_gain, d_bias = blocks(shape, finish, (zero, zero))
    moves.leave(d_inputs)
    last = width + 8 + taps
    rest = units.late_total - last - 4
    gathered[last:, :] = jnp.concatenate(
        [
            row_sum(d_gain),
            row_sum(d_bias),
            context_bias,
            jnp.concatenate([gate_bias, jnp.zeros((1, width - lanes), f32)], axis=1),
            jnp.zeros((rest, width), f32),
        ]
    )
    for half, target in enumerate((own_late, other_late)):
        absolute = jnp.bitwise_xor(core[0], half)
        for piece in range(units.pieces):
            far = units.shards // 2
            column = jnp.bitwise_xor(core[1], piece // (2 * far)) * 2
            column = column + jnp.bitwise_xor(core[2], piece // far % 2)
            first = absolute * units.pieces + column * far + piece % far
            first = first * units.late_rows
            target[piece] = gathered[
                pl.ds(pl.multiple_of(first, 16), units.late_rows), :
            ].astype(bf16)


def finish_kernel(
    shape,
    moves,
    d_middle,
    d_inputs,
    small,
    middle,
    out_near,
    out_far,
    tokens_grad,
    block_out,
    rows_ref,
):
    moves.arrive(d_middle, d_inputs)

    def add_grads(rows, carry):
        rows_ref[rows, :] = d_middle[rows, :] + d_inputs[rows, :]
        return carry

    blocks(shape, add_grads, 0)
    pack(shape, rows_ref, tokens_grad)
    moves.leave(tokens_grad)
    moves.arrive(small, middle, out_near, out_far)

    def add_outs(rows, carry):
        total = middle[rows, :] + small[FC2_BIAS : FC2_BIAS + 1, :]
        rows_ref[rows, :] = total + out_near[rows, :] + out_far[rows, :].astype(f32)
        return carry

    blocks(shape, add_outs, 0)
    pack(shape, rows_ref, block_out)


def unpack_kernel(
    shape,
    units,
    spots,
    piece,
    piece_x,
    piece_core,
    piece_both,
    own,
    own_b,
    own_x,
    own_both,
    core_own,
    core_b,
    core_x,
    core_both,
    ln1_gain,
    ln1_bias,
    f_grad,
    f_bias,
    small_grad,
    middle_grad,
    large_grad,
    h_grad,
    h_bias,
    proj_grad,
    proj_bias,
    ln2_gain,
    ln2_bias,
    first_grad,
    first_bias,
    second_grad,
    second_bias,
    held,
    head,
    late,
):
    width = shape.width
    unit = units.unit
    size = own.shape[0]
    parts = (own, own_b, own_x, own_both, core_own, core_b, core_x, core_both)
    for index, part in enumerate(parts):
        held[index * size : (index + 1) * size, :] = part[...].astype(f32)
    core, shift = spots[0], spots[2]
    far = units.shards // 2
    for half in range(2):
        for place in range(2):
            for close in range(2):
                slot = jnp.bitwise_xor(core, half) * 4 + jnp.bitwise_xor(spots[3], place) * 2
                base = (slot + jnp.bitwise_xor(spots[4], close)) * size
                to = (half * 2 + place) * 2 + close
                rows = far * units.head_rows
                head[to * rows : (to + 1) * rows, :] = held[
                    pl.ds(pl.multiple_of(base, 8), rows), :
                ]
                first = pl.multiple_of(base + rows, 8)
                rows = far * units.late_rows
                late[to * rows : (to + 1) * rows, :] = held[pl.ds(first, rows), :]
    total = None
    lane = lax.broadcasted_iota(jnp.int32, (8, width), 1)
    for index, source in enumerate((piece, piece_core, piece_x, piece_both)):
        quarter = jnp.bitwise_xor(spots[1], index)
        to = pl.ds(pl.multiple_of(quarter * unit, 8), unit)
        first_grad[to, :] = source[0:unit, :].astype(f32)
        second_grad[to, :] = source[unit : 2 * unit, :].astype(f32)
    for quarter in range(4):
        row = head[3 * width + 8 + quarter : 3 * width + 9 + quarter, :]
        moved = shift + quarter * unit
        moved = jnp.where(moved >= width, moved - width, moved)
        row = pltpu.roll(jnp.broadcast_to(row, (8, width)), moved, 1)
        row = jnp.where((lane >= quarter * unit) & (lane < (quarter + 1) * unit), row, 0.0)
        total = row if total is None else total + row
    first_bias[...] = total[0:1, 0 : first_bias.shape[0]].reshape(first_bias.shape)
    f_grad[0:width, :] = head[0:width, :]
    f_grad[width : 2 * width + 4, :] = late[0 : width + 4, :]
    h_grad[...] = head[width : 2 * width, :]
    proj_grad[...] = head[2 * width : 3 * width, :]
    first = width + 8
    small_grad[...] = late[first : first + 9, :]
    middle_grad[...] = late[first + 9 : first + 34, :]
    large_grad[...] = late[first + 34 : first + taps, :]
    first = first + taps
    for out, source, row in (
        (h_bias, head, 3 * width),
        (proj_bias, head, 3 * width + 1),
        (ln2_gain, head, 3 * width + 2),
        (ln2_bias, head, 3 * width + 3),
        (second_bias, head, 3 * width + 4),
        (ln1_gain, late, first),
        (ln1_bias, late, first + 1),
    ):
        out[...] = source[row : row + 1, :].reshape(width)
    f_bias[0:width] = head[3 * width + 5 : 3 * width + 6, :].reshape(width)
    f_bias[width : 2 * width] = late[first + 2 : first + 3, :].reshape(width)
    f_bias[2 * width : 2 * width + 4] = late[first + 3 : first + 4, 0:4].reshape(4)


def call(kernel, name, outs, scratch, micros, room, *operands):
    spec = pl.BlockSpec(memory_space=pltpu.VMEM)
    outer = pl.BlockSpec(memory_space=pltpu.HBM)
    far_in = [isinstance(item, Far) for item in operands]
    far_out = [isinstance(item, Far) for item in outs]
    anywhere = [isinstance(item, Anywhere) for item in operands]
    raw = [isinstance(item, Raw) for item in operands]
    operands = [item.value if far else item for item, far in zip(operands, far_in)]
    operands = [
        pltpu.with_memory_space_constraint(item, pltpu.HBM) if far and not free else item
        for item, far, free in zip(operands, far_in, anywhere)
    ]
    raw_out = [isinstance(item, Raw) for item in outs]
    outs = [
        pltpu.HBM(item.value.shape, item.value.dtype) if far else item
        for item, far in zip(outs, far_out)
    ]
    specs = []
    for item, far, free in zip(operands, far_in, anywhere):
        if free:
            specs.append(pl.BlockSpec(memory_space=pl.ANY))
        elif item.dtype == jnp.int32:
            specs.append(pl.BlockSpec(memory_space=pltpu.SMEM))
        else:
            specs.append(outer if far else spec)
    out_specs = [outer if far else spec for far in far_out]
    if name not in plain:
        far_in = [far and not own for far, own in zip(far_in, raw)]
        far_out = [far and not own for far, own in zip(far_out, raw_out)]
        pairs = list(zip(operands, far_in)) + list(zip(outs, far_out))
        buffers = [pltpu.VMEM(item.shape, item.dtype) for item, far in pairs if far]
        extra = sum(raw) + sum(raw_out)
        semaphores = pltpu.SemaphoreType.DMA((max(len(buffers) + extra, 1),))
        scratch = list(scratch) + buffers + [semaphores]
        kernel = with_moves(kernel, far_in, far_out, extra)
    moved = sum(item.size * item.dtype.itemsize for item in operands)
    return pl.pallas_call(
        kernel,
        name=name,
        out_shape=outs,
        in_specs=specs,
        out_specs=out_specs,
        scratch_shapes=scratch,
        compiler_params=pltpu.CompilerParams(vmem_limit_bytes=room * 1024 * 1024),
        cost_estimate=pl.CostEstimate(
            flops=int(micros * 1.1e9), bytes_accessed=moved, transcendentals=0
        ),
    )(*operands)


plain = ("piece", "sum", "pair", "share", "add", "unpack")


class Far:
    def __init__(self, value):
        self.value = value


class Anywhere(Far):
    pass


class Raw(Far):
    pass


def far_array(*dims, kind=jnp.float32):
    return Far(array(*dims, kind=kind))


def array(*dims, kind=jnp.float32):
    return jax.ShapeDtypeStruct(dims, kind)


def to_packed(values, shape):
    moved = with_layout_constraint(values.transpose(1, 2, 0, 3), Layout((0, 1, 2, 3)))
    moved = moved.reshape(shape.patches, shape.images, shape.tiles, lanes)
    moved = with_layout_constraint(moved, Layout((0, 2, 1, 3)))
    return moved.transpose(0, 2, 1, 3).reshape(shape.packed, lanes)


def from_packed(values, shape):
    moved = values.reshape(shape.patches, shape.tiles, shape.images, lanes).transpose(0, 2, 1, 3)
    moved = moved.reshape(shape.side, shape.side, shape.images, shape.width)
    return moved.transpose(2, 0, 1, 3)


everyone = ("x", "core", "a", "b")


def gather_plainly(units, first, bias, second):
    first = lax.all_gather(first, ("a", "b"), axis=0, tiled=True)
    second = lax.all_gather(second, ("a", "b"), axis=0, tiled=True)
    bias = lax.all_gather(bias, ("a", "b"), axis=0, tiled=True)
    width = first.shape[1]
    rows = jnp.pad(bias.reshape(4, 1, 1, width), ((0, 0), (0, units.shards - 1), (0, 15), (0, 0)))
    shape = (4, units.shards, units.unit, width)
    both = jnp.concatenate([first.reshape(shape), second.reshape(shape), rows], axis=2)
    both = both.reshape(4, units.shards * units.piece_rows, width)
    return [both[index] for index in range(4)]


def total_of(values, parts):
    rows = values.shape[0] // parts
    kernel = functools.partial(sum_kernel, parts)
    values = values.reshape(parts, rows, values.shape[1])
    return call(kernel, "sum", [array(rows, values.shape[2], kind=bf16)], [], 1, 4, values)[0]


def reduce_plainly(shape, units, feed, rest, late):
    width = shape.width
    unit = units.unit
    both = jnp.stack(feed).reshape(4, units.shards, units.feed_rows, width)
    first = both[:, :, :unit].reshape(4 * units.total, width)
    second = both[:, :, unit:].reshape(4 * units.total, width)

    def shared(values):
        part = lax.psum_scatter(values, ("a", "b"), scatter_dimension=0, tiled=True)
        return lax.psum(part, ("x", "core")).astype(f32)

    late = jnp.concatenate(late).reshape(units.late_total, width)
    late = lax.psum(late, everyone).astype(f32)
    head = jnp.concatenate(rest).reshape(units.head_total, width)
    head = lax.psum(head, everyone).astype(f32)
    bias = head[3 * width + 8 : 3 * width + 12].reshape(-1)
    place = lax.axis_index("a") * 2 + lax.axis_index("b")
    size = bias.shape[0] // (lax.axis_size("a") * 2)
    bias = lax.dynamic_slice_in_dim(bias, place * size, size, 0)
    last = width + 8
    vectors = head[3 * width : 3 * width + 8]
    more = late[last + taps : last + taps + 4]
    return (
        more[0],
        more[1],
        jnp.concatenate([head[:width], late[: width + 4]]),
        jnp.concatenate([vectors[5], more[2], more[3, :4]]),
        late[last : last + 9],
        late[last + 9 : last + 34],
        late[last + 34 : last + taps],
        head[width : 2 * width],
        vectors[0],
        head[2 * width : 3 * width],
        vectors[1],
        vectors[2],
        vectors[3],
        shared(first),
        bias,
        shared(second),
        vectors[4],
    )


def shards(
    sizes,
    tokens,
    ln1_gain,
    ln1_bias,
    f_weight,
    f_bias,
    dw_small,
    dw_middle,
    dw_large,
    h_weight,
    h_bias,
    proj_weight,
    proj_bias,
    ln2_gain,
    ln2_bias,
    fc1_weight,
    fc1_bias,
    fc2_weight,
    fc2_bias,
    out_grad,
):
    images, side, _, width = tokens.shape
    shape = Shape(images, side, width)
    rows, grid, inner = shape.rows, shape.grid, shape.inner
    hidden = fc1_weight.shape[1] * sizes["a"] * sizes["b"]
    quick = sizes["x"] == 2 and sizes["a"] * sizes["b"] == 8
    units = Units(8, hidden // 32)
    f_turned = f_weight.T
    first, second = fc1_weight.T, fc2_weight
    scratch = pltpu.VMEM
    core = jnp.zeros((1,), jnp.int32)
    if quick:
        core = lax.axis_index("core").astype(jnp.int32).reshape(1)
        quarter = lax.axis_index("x") * 2 + core[0]
        shard = lax.axis_index("a") * 2 + lax.axis_index("b")
        turn = lax.rem(shard - quarter + units.shards, units.shards) * units.unit
        spots = jnp.stack([quarter, shard, turn]).astype(jnp.int32)
        (pieces,) = call(
            functools.partial(piece_kernel, units, units.shards),
            "piece",
            [array(units.shards * units.piece_rows, width, kind=bf16)],
            [
                scratch((2, units.unit, width), bf16),
                scratch(fc1_bias.shape, bf16),
                pltpu.SemaphoreType.DMA((3,)),
            ],
            1,
            6,
            spots,
            Far(first),
            Far(second),
            Far(fc1_bias),
        )
        weights = exchange(pieces, ("a", "b"))
    tokens_packed = to_packed(tokens, shape)

    def rows_array(kind=bf16):
        return far_array(rows, width, kind=kind)

    small, cot, inputs, normed, query, gates, context, one, slope_one = call(
        functools.partial(entry_kernel, shape),
        "entry",
        [
            far_array(96, width),
            rows_array(),
            array(rows, width),
            rows_array(),
            array(rows, width),
            array(rows, 4 * lanes),
            far_array(grid, lanes),
            array(grid, lanes),
            array(inner, lanes),
        ],
        [
            scratch((taps * sublanes, lanes), f32),
            scratch((shape.packed, lanes), f32),
            scratch((rows, width), f32),
        ],
        5,
        16,
        tokens_packed,
        f_turned,
        to_packed(out_grad, shape),
        dw_small,
        dw_middle,
        dw_large,
        ln1_gain,
        ln1_bias,
        f_bias,
        h_bias,
        proj_bias,
        ln2_gain,
        ln2_bias,
        fc2_bias,
    )
    if quick:
        cot_far = flip(cot, "x")
        cot_core = flip(cot)
    one, gates, query, slope_one, *results = call(
        functools.partial(modulation_kernel, shape),
        "modulation",
        [
            Raw(array(grid, lanes)),
            Raw(array(rows, 4 * lanes)),
            Raw(array(rows, width)),
            Raw(array(inner, lanes)),
            rows_array(f32),
            rows_array(),
            rows_array(),
            rows_array(f32),
            rows_array(),
            far_array(grid, lanes),
            far_array(grid, lanes),
            far_array(inner, lanes),
            far_array(inner, lanes),
            far_array(2 * sublanes, lanes),
        ],
        [scratch((rows, width), f32), scratch((taps * sublanes, lanes), f32)],
        8,
        20,
        one,
        Far(small),
        gates,
        Far(h_weight),
        query,
        inputs,
        Far(proj_weight),
        slope_one,
    )
    modulator, aggregated, mixed, middle, normed_two, *results = results
    two, three, slope_two, slope_three, pooled = results

    def feed(resumed, outs, *operands):
        return call(
            functools.partial(feed_kernel, shape, units, resumed),
            "feed",
            outs,
            [
                scratch((units.total, width), bf16),
                scratch((units.total, width), bf16),
                scratch((2 * units.total, width), f32),
                scratch((8, width), f32),
            ],
            6,
            24,
            *operands,
        )

    near_rows = array(rows, width, kind=bf16)
    feed_total = array(units.shards * units.feed_rows, width, kind=bf16)
    bias_total = array(8, width)
    if quick:
        cot_both = flip(after(cot_far, middle))
        normed_far = flip(normed_two, "x")
        normed_core = flip(normed_two)
        out_own, out_core, d_own, d_core, *carry = feed(
            False,
            [near_rows] * 4 + [array(2 * units.total, width), bias_total],
            weights,
            Far(normed_two),
            normed_core,
            Far(cot),
            cot_core,
        )
        out_core, d_core = flip(out_core), flip(d_core)
        normed_far = after(normed_far, d_own)
        normed_both = flip(normed_far)
        out_far, d_far, both, d_near, out_near, feed_grads, bias_grad = feed(
            True,
            [near_rows] * 2
            + [array(2 * rows, width, kind=bf16), rows_array(f32), rows_array(f32), feed_total]
            + [bias_total],
            weights,
            normed_far,
            normed_both,
            cot_far,
            cot_both,
            *carry,
            d_own,
            d_core,
            out_own,
            out_core,
        )
        arrived = flip(both)
        d_far, out_far = call(
            functools.partial(rows_kernel, shape),
            "rows",
            [near_rows, rows_array()],
            [],
            1,
            8,
            d_far,
            out_far,
            arrived,
        )
        feed_grads = after(feed_grads, d_far)
        d_far = flip(d_far, "x")
        feed_parts = exchange(feed_grads, ("a", "b"))
        mine = (jnp.arange(4) == quarter).astype(f32)
        bias_grads = (mine[:, None, None] * bias_grad).reshape(32, width)
    else:
        out_far = d_far = jnp.zeros((rows, width), bf16)
        out_near, d_near, feed_grads, bias_grads = jnp.zeros((rows, width), f32), 0.0, [], []
        for weights in gather_plainly(units, first, fc1_bias, second):
            out, d_out, grads, bias_grad = feed(
                None, [near_rows, near_rows, feed_total, bias_total], weights, normed_two, cot
            )
            bias_grads.append(bias_grad)
            out_near, d_near = out_near + out.astype(f32), d_near + d_out.astype(f32)
            feed_grads.append(grads)
        bias_grads = jnp.concatenate(bias_grads)
    rest = array(units.pieces, units.head_rows, width, kind=bf16)
    later = [small, gates, pooled, slope_three, slope_two, slope_one, one, two, three]
    d_middle, d_query, d_aggregated, own_rest, other_rest, *fetched = call(
        functools.partial(heads_kernel, shape, units),
        "heads",
        [rows_array(f32), rows_array(), array(rows, width), rest, rest]
        + [array(*item.shape) for item in later],
        [
            scratch((rows, width), f32),
            scratch((rows, width), bf16),
            scratch((units.head_total, width), f32),
            scratch((rows, width), bf16),
        ],
        5,
        16,
        core,
        Far(small),
        Far(cot),
        Far(middle),
        Far(d_near),
        d_far,
        bias_grads,
        Far(proj_weight),
        Far(query),
        Far(modulator),
        Far(h_weight),
        Far(normed),
        Far(aggregated),
        Far(mixed),
        *[Raw(item) for item in later],
    )
    if quick:
        out_far = flip(after(out_far, d_middle), "x")
        rest_arrived = flip(other_rest)
    d_one, d_two, d_three, rounded, d_gates = call(
        functools.partial(levels_back_kernel, shape),
        "levels_back",
        [
            far_array(grid, lanes),
            far_array(grid, lanes),
            far_array(grid, lanes),
            rows_array(),
            far_array(rows, lanes, kind=bf16),
        ],
        [
            scratch((taps * sublanes, lanes), f32),
            scratch((3 * inner, lanes), f32),
            scratch((rows, 4 * lanes), f32),
            scratch((rows, width), f32),
        ],
        8,
        24,
        fetched[0],
        fetched[1],
        d_aggregated,
        *fetched[2:],
    )
    if quick:
        (rest_half,) = call(pair_kernel, "pair", [rest], [], 1, 4, own_rest, rest_arrived)
        feed_parts = after(feed_parts, d_one)
        piece = total_of(feed_parts, units.shards)
        rest_half = after(rest_half, piece)
        d_one = after(d_one, rest_half, out_far)
        shares = rest_half.shape
        rest_parts = exchange(rest_half.reshape(-1, width), ("x", "b"))
        rest_parts = rest_parts.reshape(4, shares[0] * shares[1] // 4, width)
    late = array(units.pieces, units.late_rows, width, kind=bf16)
    spot_here = jnp.zeros((3,), jnp.int32)
    if quick:
        spot_here = jnp.stack([lax.axis_index(axis) for axis in ("core", "x", "b")])
        spot_here = spot_here.astype(jnp.int32)
    d_inputs, own_late, other_late = call(
        functools.partial(exit_kernel, shape, units),
        "exit",
        [rows_array(f32), late, late],
        [
            scratch((shape.packed, lanes), f32),
            scratch((taps * sublanes, lanes), f32),
            scratch((rows, width), f32),
            scratch((rows, width), f32),
            scratch((units.late_total, width), f32),
            scratch((lanes, width), bf16),
        ],
        9,
        24,
        spot_here,
        Far(two),
        Far(d_three),
        Far(one),
        Far(d_two),
        Far(context),
        Far(d_one),
        Far(rounded),
        Far(d_gates),
        Far(small),
        Far(normed),
        Far(f_turned),
        Far(d_query),
        Far(tokens_packed),
    )
    if quick:
        late_arrived = flip(other_late)
        rest_parts = after(rest_parts, own_late)
        (late_half,) = call(pair_kernel, "pair", [late], [], 1, 4, own_late, late_arrived)
        late_half, rest_parts = lax.optimization_barrier((late_half, rest_parts))
        late_arrived = flip(late_half[units.pieces // 2 :], "x")
        d_inputs = after(d_inputs, late_half)
    tokens_grad, block_out = call(
        functools.partial(finish_kernel, shape),
        "finish",
        [far_array(shape.packed, lanes), far_array(shape.packed, lanes)],
        [scratch((rows, width), f32)],
        3,
        16,
        Far(d_middle),
        Far(d_inputs),
        Far(small),
        Far(middle),
        Far(out_near),
        Anywhere(out_far),
    )
    if quick:
        late_arrived = after(late_arrived, tokens_grad)
        for axis in ("b", None):
            part = array(late_arrived.shape[0], units.late_rows, width, kind=bf16)
            (late_half,) = call(pair_kernel, "pair", [part], [], 1, 4, late_half, late_arrived)
            if axis:
                late_arrived = flip(late_half[late_half.shape[0] // 2 :], axis)
        late_parts = late_half.reshape(1, -1, width)
        share_rows = units.pieces * units.share // 4
        (share,) = call(
            share_kernel,
            "share",
            [array(share_rows, width, kind=bf16)],
            [],
            1,
            8,
            rest_parts,
            late_parts,
        )
        piece = after(piece, share)
        piece_x = flip(piece, "x")
        piece_core, piece_both = flip(piece), flip(piece_x)
        own = share
        for bit in (1, 2):
            arrived = flip(own, "a", sizes["a"], bit)
            if bit == 2:
                arrived = after(arrived, piece_core, piece_both)
            (own,) = call(
                add_kernel, "add", [array(share_rows, width, kind=bf16)], [], 1, 6, own, arrived
            )
        held_b, held_x = flip(own, "b"), flip(own, "x")
        held_both = flip(held_b, "x")
        held = [own, held_b, held_x, held_both]
        held = held + [flip(item) for item in held]
        turn = lax.rem(units.shards - shard, units.shards) * units.unit
        spots = [core[0], quarter, turn] + [lax.axis_index(axis) for axis in ("x", "b")]
        spots = jnp.stack(spots).astype(jnp.int32)
        total = 4 * units.unit
        others = call(
            functools.partial(unpack_kernel, shape, units),
            "unpack",
            [
                array(width),
                array(width),
                array(2 * width + 4, width),
                array(2 * width + 4),
                array(9, width),
                array(25, width),
                array(49, width),
                array(width, width),
                array(width),
                array(width, width),
                array(width),
                array(width),
                array(width),
                array(total, width),
                array(total),
                array(total, width),
                array(width),
            ],
            [
                scratch((2 * units.pieces * units.share, width), f32),
                scratch((units.head_total, width), f32),
                scratch((units.late_total, width), f32),
            ],
            2,
            16,
            spots,
            piece,
            piece_x,
            piece_core,
            piece_both,
            *held,
        )
    else:
        others = reduce_plainly(
            shape, units, feed_grads, (own_rest, other_rest), (own_late, other_late)
        )
    others = list(others)
    others[2] = others[2].T
    others[13] = others[13].T
    return from_packed(block_out, shape), from_packed(tokens_grad, shape), *others


def solution(mesh):
    img, mlp = mesh.shape["img"], mesh.shape["mlp"]
    sizes = {"x": img // 2, "core": 2, "a": mlp // 2, "b": 2}
    finer = Mesh(mesh.devices.reshape(*sizes.values()), everyone)
    images = P(everyone, None, None, None)
    hidden = ("a", "b")
    return jax.shard_map(
        functools.partial(shards, sizes),
        mesh=finer,
        in_specs=(images,)
        + (P(),) * 13
        + (P(None, hidden), P(hidden), P(hidden, None), P(), images),
        out_specs=(images, images)
        + (P(),) * 13
        + (P(None, hidden), P(hidden), P(hidden, None), P()),
        check_vma=False,
    )
```
